512 devices in a mesh: ctx: 64 (over x, z_lo, core), tp: 8 (over z_hi, y).
Axes of the slice: x: 4, y: 4, z: 16 (z_hi: 2, z_lo: 8; z = z_hi * 8 + z_lo), core: 2. Of those that a mesh axis runs over, the one named last changes fastest.
Arguments:
- queries: bfloat16 [8192, 8192], P('ctx', 'tp'), may hold values from -200 to 200
- keys: bfloat16 [8192, 1024], P('ctx', 'tp'), may hold values from -8 to 8
- values: bfloat16 [8192, 1024], P('ctx', 'tp'), may hold values from -6 to 6
- out_weight: bfloat16 [5120, 8192], P('ctx', 'tp'), may hold values from -0.25 to 0.25
- residual: bfloat16 [5120, 256], P('ctx'), may hold values from -200 to 200
- norm_gain: float32 [5120], replicated, may hold values from 0.5 to 1.5
- head_weight: bfloat16 [131072, 5120], P(('ctx', 'tp')), may hold values from -10 to 10
- sampled_ids: int32 [8192], replicated, may hold values from 0 to 131071
- loss_mask: int32 [8192], replicated, may hold values from 0 to 1, as said below
- doc_lengths: int32 [32], replicated, may hold values from 1 to 4224, 8192 in all
Outputs:
- context: bfloat16 [8192, 8192], P('ctx', 'tp')
- logprobs: float32 [8192], P('ctx')
The draws below stay inside these ranges and needn't reach their ends.
Inputs may be any that keep to these rules, and one draw needn't show every extreme that they name: `loss_mask`: each aligned block of 128 positions holds exactly 4 ones. `doc_lengths`: one document has exactly 4224 positions.
All inputs are finite; a program needn't handle non-finite values.
Results may differ from the reference program's by a relative error of at most 0.0045.
Values may be sent and summed in bfloat16 or wider, within the bound.
No kernel may reach another device: no remote copies, remote signals or barrier semaphores. Data moves between devices by JAX's collectives and lax.ppermute only.
A program may use at most 128 MiB of HBM per device.

```python
import math
import jax
import jax.numpy as jnp
import numpy as np
from jax import lax

D = 5120
HEADS = 64
KV_HEADS = 8
HEAD_DIM = 128
VOCAB = 131072
TOK_DEV = 128
SCORED = 4
TOKENS = 8192
SCORED_ALL = 256
DOCS = 32
N_CTX = 64


def shared_keys(key):
    return jax.random.normal(jax.random.fold_in(key, 77), (TOKENS, KV_HEADS * HEAD_DIM), jnp.float32)


def draw_keys(key, part):
    base_keys = shared_keys(key)
    return base_keys.astype(jnp.bfloat16)


def draw_queries(key, part):
    key = jax.random.fold_in(key, 3)
    sampled = jax.random.normal(key, (TOKENS, HEADS * HEAD_DIM), jnp.float32)
    return sampled.astype(jnp.bfloat16)


def draw_residual(key, part):
    key = jax.random.fold_in(key, 1)
    ramp = 0.6 + 1.2 * jnp.arange(D, dtype=jnp.float32) / D
    sampled = jax.random.normal(key, (D, SCORED_ALL), jnp.float32)
    return (0.06 * sampled * ramp[:, None]).astype(jnp.bfloat16)


def draw_head_weight(key, part):
    key = jax.random.fold_in(key, 4)
    return (0.045 * jax.random.normal(key, (VOCAB, D), jnp.float32)).astype(jnp.bfloat16)


def draw_loss_mask(key, part):
    key = jax.random.fold_in(key, 5)
    slab_keys = jax.random.split(key, N_CTX)
    orders = jax.vmap(lambda slab_key: jax.random.permutation(slab_key, TOK_DEV))(slab_keys)
    return (orders < SCORED).astype(jnp.int32).reshape(TOKENS)


def plant(result, key, least, largest):
    spot = [jax.random.randint(jax.random.fold_in(key, axis), (), 0, length) for axis, length in enumerate(result.shape)]
    main_axis = result.shape.index(max(result.shape))
    neighbour = spot[:main_axis] + [(spot[main_axis] + 1) % result.shape[main_axis]] + spot[main_axis + 1:]
    return result.at[tuple(spot)].set(least).at[tuple(neighbour)].set(largest)


def level_of(stream_key, shape, pieces, least, top_value):
    loudness, own = 1.0, jax.random.fold_in(stream_key, 6)
    for position, blocks in pieces:
        draws = jnp.exp(jax.random.uniform(jax.random.fold_in(own, position), (blocks,), jnp.float32, least / len(pieces), top_value / len(pieces)))
        loudness = loudness * jnp.repeat(draws, shape[position] // blocks).reshape([-1 if axis == position else 1 for axis in range(len(shape))])
    return loudness


def wide_ids(stream_key, extent, number_of, lean):
    loads = [min(1 << octave, number_of + 1 - (1 << octave)) * (1 << 20) // math.isqrt((1 << octave) ** lean) + 1 for octave in range((number_of + 1).bit_length()) if 1 << octave <= number_of]
    width = 1 + sum(loads) // (1 << 30)
    grid = np.cumsum(np.array([max(1, weight // width) for weight in loads]))
    ticket = jax.random.randint(jax.random.fold_in(stream_key, 1), extent, 0, int(grid[len(loads) - 1]))
    start = jnp.left_shift(1, jnp.searchsorted(jnp.asarray(grid, jnp.int32), ticket, side="right").astype(jnp.int32))
    rank = start - 1 + jax.random.randint(jax.random.fold_in(stream_key, 4), extent, 0, 1 << 30) % jnp.minimum(start, number_of + 1 - start)
    return jax.random.permutation(jax.random.fold_in(stream_key, 2), number_of)[rank].astype(jnp.int32)


def split_up(count, total, bound, slope):
    loads = [(1 << 20) // math.isqrt(grade ** slope) + 1 for grade in range(2, count + 1)]
    spare, given = total - bound - (count - 1), [1] * (count - 1)
    while spare > 0:
        movable = [i for i in range(count - 1) if given[i] < bound]
        whole, remaining = sum([loads[i] for i in movable]), spare
        for i in movable:
            addition = min(bound - given[i], max(1, remaining * loads[i] // whole), spare)
            given[i] = given[i] + addition
            spare = spare - addition
    return np.array([bound] + given)


def uneven_parts(key, number_of, total, limit, skew):
    if number_of == 2:
        one = jax.random.randint(key, (), max(1, total - limit), min(limit, total - 1) + 1)
        return jnp.stack([one, total - one])
    tallies = jnp.asarray(split_up(number_of, total, limit, skew), jnp.int32)
    twos = (number_of - 1) // 2
    giver, receiver = tallies[1:1 + 2 * twos:2], tallies[2:2 + 2 * twos:2]
    slack = jnp.minimum(giver - 1, limit - receiver)
    moved = jax.random.randint(jax.random.fold_in(key, 1), (twos,), 0, 1 << 20) % (slack + 1)
    tallies = tallies.at[1:1 + 2 * twos:2].set(giver - moved).at[2:2 + 2 * twos:2].set(receiver + moved)
    return tallies[jax.random.permutation(jax.random.fold_in(key, 2), number_of)]


def bell_draw(rng, dims, spread, most, pieces=(), held_as=jnp.bfloat16):
    drawn = jax.random.normal(rng, dims, jnp.float32) * spread
    if len(pieces) > 0:
        drawn = level_of(rng, dims, pieces, -0.22, 0.18) * drawn
    return jnp.clip(drawn, min=-most, max=most).astype(held_as)


def setup_inputs(seed: int = 0) -> dict:
    streams_of = jax.random.split(jax.random.key(seed), 11)
    return {
        "queries": draw_queries(jax.random.fold_in(streams_of[10], 71), 0),
        "keys": draw_keys(jax.random.fold_in(streams_of[10], 71), 0),
        "values": bell_draw(streams_of[2], (TOKENS, KV_HEADS * HEAD_DIM), 1.0, 6.0, ((0, 64), (1, 8))),
        "out_weight": bell_draw(streams_of[3], (D, HEADS * HEAD_DIM), (HEADS * HEAD_DIM // 16) ** -0.5, 0.25, ((0, 64), (1, 8))),
        "residual": draw_residual(jax.random.fold_in(streams_of[10], 71), 0),
        "norm_gain": jnp.clip(1.0 + 0.1 * jax.random.normal(streams_of[5], (D,), jnp.float32), 0.5, 1.5),
        "head_weight": draw_head_weight(jax.random.fold_in(streams_of[10], 71), 0),
        "sampled_ids": plant(wide_ids(streams_of[7], (TOKENS,), VOCAB, 2), jax.random.fold_in(streams_of[7], 3), 0, VOCAB - 1).astype(jnp.int32),
        "loss_mask": draw_loss_mask(jax.random.fold_in(streams_of[10], 71), 0),
        "doc_lengths": uneven_parts(streams_of[9], DOCS, TOKENS, TOKENS // 2 + TOK_DEV, 2).astype(jnp.int32),
    }


neg_fill = -1e+30
norm_eps = 1e-06

def document_index(positions, doc_lengths):
    bounds = jnp.cumsum(doc_lengths).astype(jnp.int32)
    return lax.optimization_barrier(jnp.sum((positions[:, None] >= bounds[None, :]).astype(jnp.int32), axis=1)).astype(jnp.int32)

def scored_positions(loss_mask):
    slabs = loss_mask.reshape(N_CTX, TOK_DEV)
    rank_in = (jnp.cumsum(slabs, axis=1) - 1).astype(jnp.int32)
    chosen = (slabs[:, None, :] == 1) & (rank_in[:, None, :] == jnp.arange(SCORED, dtype=jnp.int32)[None, :, None])
    within = lax.optimization_barrier(jnp.sum(jnp.where(chosen, jnp.arange(TOK_DEV, dtype=jnp.int32)[None, None, :], 0), axis=2)).astype(jnp.int32)
    return (within + jnp.arange(N_CTX, dtype=jnp.int32)[:, None] * TOK_DEV).reshape(SCORED_ALL).astype(jnp.int32)

def reference(queries, keys, values, out_weight, residual, norm_gain, head_weight, sampled_ids, loss_mask, doc_lengths):
    group_size = HEADS // KV_HEADS
    reach_back = TOKENS // 2 + TOK_DEV
    window_len = reach_back + TOK_DEV
    score_scale = 1.0 / math.sqrt(HEAD_DIM)
    doc_of = document_index(jnp.arange(TOKENS, dtype=jnp.int32), doc_lengths)

    def one_slab(slab_index):
        slab_start = (slab_index * TOK_DEV).astype(jnp.int32)
        window_start = jnp.clip(slab_start - reach_back, 0, TOKENS - window_len).astype(jnp.int32)
        query_block = lax.dynamic_slice_in_dim(queries, slab_start, TOK_DEV, 0).astype(jnp.float32).reshape(TOK_DEV, KV_HEADS, group_size, HEAD_DIM)
        key_block = lax.dynamic_slice_in_dim(keys, window_start, window_len, 0).astype(jnp.float32).reshape(window_len, KV_HEADS, HEAD_DIM)
        value_block = lax.dynamic_slice_in_dim(values, window_start, window_len, 0).astype(jnp.float32).reshape(window_len, KV_HEADS, HEAD_DIM)
        query_pos = slab_start + jnp.arange(TOK_DEV, dtype=jnp.int32)
        key_pos = window_start + jnp.arange(window_len, dtype=jnp.int32)
        query_doc = lax.dynamic_slice_in_dim(doc_of, slab_start, TOK_DEV, 0)
        key_doc = lax.dynamic_slice_in_dim(doc_of, window_start, window_len, 0)
        visible = ((key_pos[None, :] <= query_pos[:, None]) & (key_doc[None, :] == query_doc[:, None]))[:, None, None, :]
        scores = jnp.einsum('qkgd,pkd->qkgp', query_block, key_block) * score_scale
        scores = jnp.where(visible, scores, neg_fill)
        row_max = lax.optimization_barrier(jnp.max(scores, axis=3, keepdims=True))
        weights = jnp.where(visible, jnp.exp(scores - row_max), 0.0)
        weight_sum = lax.optimization_barrier(jnp.sum(weights, axis=3))
        rounded = lax.optimization_barrier(weights.astype(jnp.bfloat16)).astype(jnp.float32)
        mixture = jnp.einsum('qkgp,pkd->qkgd', rounded, value_block)
        return (mixture / weight_sum[..., None]).astype(jnp.bfloat16).reshape(TOK_DEV, HEADS * HEAD_DIM)
    context = lax.map(one_slab, jnp.arange(N_CTX, dtype=jnp.int32)).reshape(TOKENS, HEADS * HEAD_DIM)
    picked = scored_positions(loss_mask)
    scored = jnp.take(context, picked, axis=0)
    chosen_ids = jnp.take(sampled_ids, picked, axis=0).astype(jnp.int32)
    projected = jnp.dot(out_weight, scored.T, preferred_element_type=jnp.float32)
    hidden = (residual.astype(jnp.float32) + projected).astype(jnp.bfloat16)
    widened = hidden.astype(jnp.float32)
    mean_square = lax.optimization_barrier(jnp.mean(widened * widened, axis=0))
    normed = (widened * lax.rsqrt(mean_square + norm_eps)[None, :] * norm_gain.astype(jnp.float32)[:, None]).astype(jnp.bfloat16)
    logits = jnp.dot(head_weight, normed, preferred_element_type=jnp.float32)
    column_max = lax.optimization_barrier(jnp.max(logits, axis=0))
    exp_total = lax.optimization_barrier(jnp.sum(jnp.exp(logits - column_max[None, :]), axis=0))
    target = jnp.take_along_axis(logits, chosen_ids[None, :], axis=0)[0]
    logprob = target - column_max - jnp.log(exp_total)
    per_token = jnp.zeros((TOKENS,), jnp.float32).at[picked].set(logprob)
    return (context, per_token)
```

```python
import functools
import math

import jax
import jax.numpy as jnp
import numpy as np
from jax import lax
from jax.experimental import pallas as pl
from jax.experimental.pallas import tpu as pltpu
from jax.sharding import Mesh
from jax.sharding import PartitionSpec as P

HEAD_DIM = 128
SCORED = 4
HEADS_DEV = 8
SLAB = 128
CHIPS = 32
BLOCK = 2 * SLAB + SCORED * HEADS_DEV
FEATS = 80
HALF = 40
D = 5120

masked_fill = -1e30
start_max = -5e29
norm_eps = 1e-06
LOG2E = 1.4426950408889634
SCALE2 = LOG2E / math.sqrt(HEAD_DIM)
NT = (((1,), (1,)), ((), ()))
TN = (((0,), (0,)), ((), ()))
SMEM = pl.BlockSpec(memory_space=pltpu.SMEM)
VMEM = pl.BlockSpec(memory_space=pltpu.VMEM)
PARAMS = pltpu.CompilerParams(vmem_limit_bytes=50 * 2**20)


def iota(shape, axis):
    return lax.broadcasted_iota(jnp.int32, shape, axis)


def pack_kernel(rank_ref, q_ref, k_ref, v_ref, out_ref, rows):
    chosen = (iota((8, SLAB), 0) == rank_ref[...]).astype(jnp.bfloat16)
    picked = jnp.dot(chosen, q_ref[...], preferred_element_type=jnp.float32)
    for h in range(HEADS_DEV):
        rows[pl.ds(h, SCORED, stride=HEADS_DEV), :] = picked[:SCORED, h * 128 : (h + 1) * 128]
    scored = rows[...].astype(jnp.bfloat16)
    for i in range(out_ref.shape[0]):
        out_ref[i, :SLAB, :] = k_ref[...]
        out_ref[i, SLAB : 2 * SLAB, :] = v_ref[...]
        out_ref[i, 2 * SLAB :, :] = scored


def weight_kernel(source_ref, gain_ref, w_ref, out_ref):
    width = 1280
    move = (iota((width, width), 0) == source_ref[...]).astype(jnp.bfloat16)
    for x in range(4):
        part = w_ref[:, x * width : (x + 1) * width].astype(jnp.float32)
        part = (part * gain_ref[:, x * width : (x + 1) * width]).astype(jnp.bfloat16)
        moved = jnp.dot(part, move, preferred_element_type=jnp.float32).astype(jnp.bfloat16)
        for c in range(2):
            out_ref[:, (c * 4 + x) * 640 : (c * 4 + x + 1) * 640] = moved[:, c * 640 : (c + 1) * 640]


def attend(own_ref, other_ref, key0, q, low, high, first, last):
    columns = q.shape[0]

    def step(j, carry):
        top, total, acc = carry
        k = jnp.concatenate((own_ref[j, :SLAB, :], other_ref[j, :SLAB, :]), axis=0)
        v = jnp.concatenate(
            (own_ref[j, SLAB : 2 * SLAB, :], other_ref[j, SLAB : 2 * SLAB, :]), axis=0
        )
        s = lax.dot_general(k, q, NT, preferred_element_type=jnp.float32) * SCALE2
        visible = (key0 >= low - j * 256) & (key0 <= high - j * 256)
        s = jnp.where(visible, s, masked_fill)
        new_top = jnp.maximum(top, jnp.max(s, axis=0, keepdims=True))
        p = jnp.exp2(s - new_top)
        keep = jnp.exp2(top - new_top)
        total = total * keep + jnp.sum(p, axis=0, keepdims=True)
        pv = lax.dot_general(v, p.astype(jnp.bfloat16), TN, preferred_element_type=jnp.float32)
        return new_top, total, acc * keep + pv

    start = (
        jnp.full((1, columns), start_max, jnp.float32),
        jnp.zeros((1, columns), jnp.float32),
        jnp.zeros((HEAD_DIM, columns), jnp.float32),
    )
    _, total, acc = lax.fori_loop(first, last + 1, step, start)
    return acc / total


def key_positions(core, columns):
    row = iota((2 * SLAB, columns), 0)
    return jnp.where(row < SLAB, row + core * SLAB, row - core * SLAB)


def scored_kernel(core_ref, first_ref, low_ref, high_ref, own_ref, other_ref, w_ref, out_ref, rows, scored):
    core = core_ref[0]
    key0 = key_positions(core, 256)
    for t in range(8):
        q = jnp.concatenate(
            (
                own_ref[4 * t : 4 * t + 4, 2 * SLAB :, :].reshape(128, HEAD_DIM),
                other_ref[4 * t : 4 * t + 4, 2 * SLAB :, :].reshape(128, HEAD_DIM),
            ),
            axis=0,
        )
        mixed = attend(
            own_ref, other_ref, key0, q, low_ref[t : t + 1, :], high_ref[t : t + 1, :], first_ref[t], 4 * t + 3
        )
        rows[...] = mixed.T
        for h in range(HEADS_DEV):
            part = rows[pl.ds(h, 32, stride=HEADS_DEV), :].astype(jnp.bfloat16)
            lanes = slice(h * 128, (h + 1) * 128)
            scored[pl.ds(pl.multiple_of(core * 128 + t * 16, 16), 16), lanes] = part[:16]
            scored[pl.ds(pl.multiple_of((1 - core) * 128 + t * 16, 16), 16), lanes] = part[16:]
    partial = lax.dot_general(w_ref[...], scored[...], NT, preferred_element_type=jnp.float32)
    for half in range(2):
        for feats in range(2):
            out_ref[half * 2 + feats] = partial[
                feats * HALF : (feats + 1) * HALF, half * 128 : (half + 1) * 128
            ]


def context_kernel(at_ref, low_ref, high_ref, own_ref, other_ref, q_ref, out_ref):
    key0 = key_positions(at_ref[0], 256)
    for pair in range(HEADS_DEV // 2):
        q = jnp.concatenate(
            [q_ref[:, h * 128 : (h + 1) * 128] for h in (2 * pair, 2 * pair + 1)], axis=0
        )
        mixed = attend(own_ref, other_ref, key0, q, low_ref[...], high_ref[...], at_ref[1], at_ref[2])
        for i in range(2):
            h = 2 * pair + i
            out_ref[:, h * 128 : (h + 1) * 128] = mixed[:, i * 128 : (i + 1) * 128].T.astype(jnp.bfloat16)


def add_kernel(parts_ref, residual_ref, out_ref):
    total = residual_ref[...]
    for i in range(parts_ref.shape[0]):
        total = total + parts_ref[i]
    total = total.astype(jnp.bfloat16)
    for i in range(out_ref.shape[0]):
        out_ref[i] = total


def hidden_kernel(parts_ref, out_ref):
    for z in range(8):
        total = parts_ref[z].astype(jnp.float32) + parts_ref[8 + z].astype(jnp.float32)
        out_ref[z] = total.astype(jnp.bfloat16)


def logits_kernel(at_ref, ids_ref, own_ref, other_ref, w_ref, out_ref):
    core, base = at_ref[0], at_ref[1]
    logits = []
    tops, targets = [], []
    for half in range(2):
        total = jnp.zeros((256, 128), jnp.float32)
        square = jnp.zeros((8, 128), jnp.float32)
        for ref, c in ((own_ref, core), (other_ref, 1 - core)):
            for x in range(4):
                part = ref[x, half]
                lanes = pl.ds(pl.multiple_of((c * 4 + x) * 640, 128), 640)
                total = total + jnp.dot(w_ref[:, lanes], part, preferred_element_type=jnp.float32)
                wide = part.astype(jnp.float32)
                square = square + jnp.sum((wide * wide).reshape(80, 8, 128), axis=0)
        mean = jnp.sum(square, axis=0, keepdims=True) * (1.0 / D)
        total = total * lax.rsqrt(mean + norm_eps)
        top = jnp.max(total, axis=0, keepdims=True)
        tops.append(top + jnp.log(jnp.sum(jnp.exp(total - top), axis=0, keepdims=True)))
        hit = iota((256, 128), 0) + base == ids_ref[half : half + 1, :]
        targets.append(jnp.sum(jnp.where(hit, total, 0.0), axis=0, keepdims=True))
    tile = jnp.concatenate(tops + targets + [jnp.zeros((4, 128), jnp.float32)], axis=0)
    for i in range(out_ref.shape[0]):
        out_ref[i] = tile


def merge(parts_ref):
    parts = parts_ref[...]
    top = jnp.max(parts, axis=0)
    lse = top + jnp.log(jnp.sum(jnp.exp(parts - top[None]), axis=0))
    return jnp.where(iota((8, 128), 0) < 2, lse, jnp.sum(parts, axis=0))


def merge_kernel(parts_ref, out_ref):
    tile = merge(parts_ref)
    for i in range(out_ref.shape[0]):
        out_ref[i] = tile


def final_kernel(at_ref, rank_ref, parts_ref, out_ref):
    core, chip = at_ref[0], at_ref[1]
    tile = merge(parts_ref)
    logprob = jnp.where(core == 0, tile[2:3] - tile[0:1], tile[3:4] - tile[1:2])
    lane = iota((1, 128), 1)
    result = jnp.zeros((1, 128), jnp.float32)
    for k in range(SCORED):
        value = jnp.sum(jnp.where(lane == chip * SCORED + k, logprob, 0.0), axis=1, keepdims=True)
        result = jnp.where(rank_ref[...] == k, value, result)
    out_ref[...] = result


def call(kernel, shape, dtype, specs, scratch=(), flops=0, size=0, name=None):
    return pl.pallas_call(
        kernel,
        out_shape=jax.ShapeDtypeStruct(shape, dtype),
        in_specs=specs,
        out_specs=VMEM,
        scratch_shapes=list(scratch),
        compiler_params=PARAMS,
        cost_estimate=pl.CostEstimate(flops=flops, bytes_accessed=size, transcendentals=0),
        name=name,
    )


def source_columns():
    c, yf, z, k = np.meshgrid(np.arange(2), np.arange(2), np.arange(8), np.arange(40), indexing="ij")
    return (((z * 2 + c) * 2 + yf) * 40 + k).reshape(1, 1280).astype(np.int32)


def body(
    queries,
    keys,
    values,
    out_weight,
    residual,
    norm_gain,
    head_weight,
    sampled_ids,
    loss_mask,
    doc_lengths,
):
    x, z, core = lax.axis_index("x"), lax.axis_index("z"), lax.axis_index("c")
    h, y = lax.axis_index("h"), lax.axis_index("y")
    chip = x * 8 + z
    slab = chip * 2 + core
    slabs = loss_mask.reshape(64, SLAB)
    upto = jnp.tril(jnp.ones((SLAB, SLAB), jnp.float32)).T
    rank = jnp.dot(slabs.astype(jnp.float32), upto, preferred_element_type=jnp.float32).astype(jnp.int32)
    rank = jnp.where(slabs == 1, rank - 1, -1)
    own_rank = lax.dynamic_slice_in_dim(rank, slab, 1, 0)
    packed = call(
        pack_kernel, (8, BLOCK, 128), jnp.bfloat16, [VMEM] * 4, [pltpu.VMEM((32, 128), jnp.float32)], name="pack"
    )(own_rank, queries, keys, values)
    along_z = lax.all_to_all(packed, "z", 0, 0)
    along_x = lax.all_to_all(jnp.broadcast_to(along_z[None], (4, 8, BLOCK, 128)), "x", 0, 0)
    own = along_x.reshape(CHIPS, BLOCK, 128)
    other = lax.ppermute(own, "c", [(0, 1), (1, 0)])

    bounds = jnp.cumsum(doc_lengths)
    position = jnp.arange(64 * SLAB, dtype=jnp.int32)
    begin = jnp.max(jnp.where(bounds[None, :] <= position[:, None], bounds[None, :], 0), axis=1)
    chosen = rank[:, None, :] == jnp.arange(SCORED, dtype=jnp.int32)[None, :, None]

    def pick(values_of):
        return jnp.sum(jnp.where(chosen, values_of.reshape(64, 1, SLAB), 0), axis=2)

    def columns(of_scored):
        pairs = of_scored.reshape(CHIPS, 2, SCORED)
        pairs = jnp.where(core == 0, pairs, pairs[:, ::-1])
        tiles = pairs.reshape(8, 4, 2, SCORED).transpose(0, 2, 1, 3)
        return jnp.repeat(tiles.reshape(8, 32), HEADS_DEV, axis=1)

    high = columns(pick(position))
    low = columns(pick(begin))
    ids = pick(sampled_ids).reshape(CHIPS, 2, SCORED).transpose(1, 0, 2).reshape(2, 128)
    first = jnp.min(low, axis=1) // 256
    core_at = core[None]

    source = jnp.asarray(source_columns())
    weight = call(weight_kernel, (256, D), jnp.bfloat16, [VMEM] * 3, flops=2 * 256 * D * 1280, name="weight")(
        source, norm_gain[None, :], head_weight
    )
    mine = residual.reshape(2, HALF, CHIPS, 2, SCORED).transpose(3, 0, 1, 2, 4).reshape(4, HALF, 128)
    mine = lax.dynamic_index_in_dim(mine, y, 0, keepdims=False).astype(jnp.float32)
    mine = jnp.where(h == 0, mine, 0.0)

    parts = call(
        scored_kernel,
        (4, HALF, 128),
        jnp.float32,
        [SMEM, SMEM] + [VMEM] * 5,
        [pltpu.VMEM((256, 128), jnp.float32), pltpu.VMEM((256, 1024), jnp.bfloat16)],
        name="scored",
    )(core_at, first, low, high, own, other, out_weight)

    own_begin = lax.dynamic_slice_in_dim(begin, slab * SLAB, SLAB, 0)
    own_position = slab * SLAB + jnp.arange(SLAB, dtype=jnp.int32)
    at = jnp.stack((core, own_begin[0] // 256, chip))
    context = call(
        context_kernel,
        (SLAB, 1024),
        jnp.bfloat16,
        [SMEM] + [VMEM] * 5,
        flops=4 * 1024 * 4224 * 128,
        size=6 * 2**20,
        name="context",
    )(at, jnp.tile(own_begin, 2)[None, :], jnp.tile(own_position, 2)[None, :], own, other, queries)

    parts = lax.all_to_all(parts, "y", 0, 0)
    sums = call(add_kernel, (16, HALF, 128), jnp.bfloat16, [VMEM] * 2, name="add")(parts, mine)
    sums = lax.all_to_all(sums, ("h", "z"), 0, 0)
    hidden = call(hidden_kernel, (8, HALF, 128), jnp.bfloat16, [VMEM], name="hidden")(sums)
    hidden = jnp.broadcast_to(hidden.reshape(1, 8 * HALF, 128), (16, 8 * HALF, 128))
    hidden = lax.all_to_all(hidden, ("x", "y"), 0, 0).reshape(4, 2, 640, 128)
    hidden_other = lax.ppermute(hidden, "c", [(0, 1), (1, 0)])
    base = ((slab * 2 + h) * 4 + y) * 256
    tiles = call(logits_kernel, (32, 8, 128), jnp.float32, [SMEM] + [VMEM] * 4, name="logits")(
        jnp.stack((core, base)), ids, hidden, hidden_other, weight
    )
    tiles = lax.all_to_all(tiles, ("x", "y", "c"), 0, 0)
    tiles = call(merge_kernel, (16, 8, 128), jnp.float32, [VMEM], name="merge")(tiles)
    tiles = lax.all_to_all(tiles, ("h", "z"), 0, 0)
    logprob = call(final_kernel, (1, 128), jnp.float32, [SMEM, VMEM, VMEM], name="final")(
        jnp.stack((core, chip)), own_rank, tiles
    )
    return context, logprob.reshape(128)


def solution(mesh):
    fine = Mesh(mesh.devices.reshape(4, 8, 2, 2, 4), ("x", "z", "c", "h", "y"))
    ctx, tp = ("x", "z", "c"), ("h", "y")
    placed = (
        P(ctx, tp),
        P(ctx, tp),
        P(ctx, tp),
        P(ctx, tp),
        P(ctx, None),
        P(),
        P(ctx + tp, None),
        P(),
        P(),
        P(),
    )
    return jax.shard_map(
        body, mesh=fine, in_specs=placed, out_specs=(P(ctx, tp), P(ctx)), check_vma=False
    )
```

```python
import functools
import math

import jax
import jax.numpy as jnp
import numpy as np
from jax import lax
from jax.experimental import pallas as pl
from jax.experimental.pallas import tpu as pltpu
from jax.sharding import Mesh
from jax.sharding import PartitionSpec as P

HEAD_DIM = 128
SCORED = 4
HEADS_DEV = 8
SLAB = 128
CHIPS = 32
BLOCK = 2 * SLAB + SCORED * HEADS_DEV
FEATS = 80
HALF = 40
D = 5120

masked_fill = -1e30
start_max = -5e29
norm_eps = 1e-06
LOG2E = 1.4426950408889634
SCALE2 = LOG2E / math.sqrt(HEAD_DIM)
NT = (((1,), (1,)), ((), ()))
TN = (((0,), (0,)), ((), ()))
SMEM = pl.BlockSpec(memory_space=pltpu.SMEM)
VMEM = pl.BlockSpec(memory_space=pltpu.VMEM)
ANY = pl.BlockSpec(memory_space=pl.ANY)
HBM = pl.BlockSpec(memory_space=pltpu.HBM)


def iota(shape, axis):
    return lax.broadcasted_iota(jnp.int32, shape, axis)


def send_copies(source, out_ref, sems):
    copies = [pltpu.make_async_copy(source, out_ref.at[i], sems.at[i]) for i in range(out_ref.shape[0])]
    for copy in copies:
        copy.start()
    for copy in copies:
        copy.wait()


def pack_kernel(at_ref, mask_ref, q_ref, k_ref, v_ref, out_ref, block, queries, rows, sems):
    copies = [
        pltpu.make_async_copy(k_ref, block.at[pl.ds(0, SLAB)], sems.at[0]),
        pltpu.make_async_copy(v_ref, block.at[pl.ds(SLAB, SLAB)], sems.at[1]),
        pltpu.make_async_copy(q_ref, queries, sems.at[2]),
    ]
    for copy in copies:
        copy.start()
    mask = mask_ref[pl.ds(at_ref[0], 1), :]
    upto = (iota((SLAB, SLAB), 0) <= iota((SLAB, SLAB), 1)).astype(jnp.bfloat16)
    ones = jnp.broadcast_to(mask.astype(jnp.float32), (8, SLAB)).astype(jnp.bfloat16)
    rank = jnp.dot(ones, upto, preferred_element_type=jnp.float32).astype(jnp.int32) - 1
    chosen = jnp.where((iota((8, SLAB), 0) == rank) & (mask == 1), 1.0, 0.0).astype(jnp.bfloat16)
    for copy in copies:
        copy.wait()
    picked = jnp.dot(chosen, queries[...], preferred_element_type=jnp.float32)
    for h in range(HEADS_DEV):
        rows[pl.ds(h, SCORED, stride=HEADS_DEV), :] = picked[:SCORED, h * 128 : (h + 1) * 128]
    block[2 * SLAB :, :] = rows[...].astype(jnp.bfloat16)
    send_copies(block, out_ref, sems)


def spread_kernel(*refs):
    send_copies(refs[0], refs[-2], refs[-1])


def weight_kernel(source_ref, gain_ref, w_ref, out_ref):
    width = 1280
    move = (iota((width, width), 0) == source_ref[...]).astype(jnp.bfloat16)
    for x in range(4):
        part = w_ref[:, x * width : (x + 1) * width].astype(jnp.float32)
        part = (part * gain_ref[:, x * width : (x + 1) * width]).astype(jnp.bfloat16)
        moved = jnp.dot(part, move, preferred_element_type=jnp.float32).astype(jnp.bfloat16)
        for c in range(2):
            out_ref[:, (c * 4 + x) * 640 : (c * 4 + x + 1) * 640] = moved[:, c * 640 : (c + 1) * 640]


def attend(own_ref, other_ref, core, q, low, high, bounds, group):
    columns = q.shape[0]
    half = group * SLAB
    row = iota((2 * half, 1), 0)
    inside = jnp.where(row < half, row, row - half)
    key0 = (inside // SLAB) * (2 * SLAB) + inside % SLAB + jnp.where(row < half, core, 1 - core) * SLAB

    def step(edge, g, carry):
        top, total, acc = carry
        chips = pl.ds(pl.multiple_of(g * group, group), group)

        def rows(at):
            parts = [ref[chips, at : at + SLAB, :].reshape(half, HEAD_DIM) for ref in (own_ref, other_ref)]
            return jnp.concatenate(parts, axis=0)

        s = lax.dot_general(rows(0), q, NT, preferred_element_type=jnp.float32) * SCALE2
        if edge:
            offset = g * (2 * half)
            s = jnp.where((key0 >= low - offset) & (key0 <= high - offset), s, masked_fill)
        new_top = jnp.maximum(top, jnp.max(s, axis=0, keepdims=True))
        p = jnp.exp2(s - new_top)
        keep = jnp.exp2(top - new_top)
        total = total * keep + jnp.sum(p, axis=0, keepdims=True)
        pv = lax.dot_general(rows(SLAB), p.astype(jnp.bfloat16), TN, preferred_element_type=jnp.float32)
        return new_top, total, acc * keep + pv

    carry = (
        jnp.full((1, columns), start_max, jnp.float32),
        jnp.zeros((1, columns), jnp.float32),
        jnp.zeros((HEAD_DIM, columns), jnp.float32),
    )
    for i, edge in enumerate((True, False, True)):
        carry = lax.fori_loop(bounds[i], bounds[i + 1], functools.partial(step, edge), carry)
    _, total, acc = carry
    return acc / total


def group_bounds(first, low, high, last_chip, group):
    size = group * 2 * SLAB
    begin, end = first // size, last_chip // group + 1
    whole = jnp.clip((low + size - 1) // size, begin, end)
    return begin, whole, jnp.clip((high + 1) // size, whole, end), end


def scored_kernel(core_ref, span_ref, low_ref, high_ref, own_ref, other_ref, w_ref, out_ref, rows, scored):
    core = core_ref[0]
    for t in range(8):
        q = jnp.concatenate(
            (
                own_ref[4 * t : 4 * t + 4, 2 * SLAB :, :].reshape(128, HEAD_DIM),
                other_ref[4 * t : 4 * t + 4, 2 * SLAB :, :].reshape(128, HEAD_DIM),
            ),
            axis=0,
        )
        bounds = group_bounds(span_ref[0, t], span_ref[1, t], span_ref[2, t], 4 * t + 3, 4)
        mixed = attend(own_ref, other_ref, core, q, low_ref[t : t + 1, :], high_ref[t : t + 1, :], bounds, 4)
        rows[...] = mixed.T
        for h in range(HEADS_DEV):
            part = rows[pl.ds(h, 32, stride=HEADS_DEV), :].astype(jnp.bfloat16)
            lanes = slice(h * 128, (h + 1) * 128)
            scored[pl.ds(pl.multiple_of(core * 128 + t * 16, 16), 16), lanes] = part[:16]
            scored[pl.ds(pl.multiple_of((1 - core) * 128 + t * 16, 16), 16), lanes] = part[16:]
    partial = lax.dot_general(w_ref[...], scored[...], NT, preferred_element_type=jnp.float32)
    for half in range(2):
        for feats in range(2):
            out_ref[half * 2 + feats] = partial[
                feats * HALF : (feats + 1) * HALF, half * 128 : (half + 1) * 128
            ]


def context_kernel(start_head, at_ref, low_ref, high_ref, own_ref, other_ref, q_ref, *refs):
    out_ref = refs[-1]
    heads = range(start_head, start_head + 4)
    q = jnp.concatenate([q_ref[:, h * 128 : (h + 1) * 128] for h in heads], axis=0)
    low, high = jnp.tile(low_ref[...], (1, 4)), jnp.tile(high_ref[...], (1, 4))
    bounds = group_bounds(at_ref[1], at_ref[2], at_ref[3] * 256, at_ref[3], 4)
    mixed = attend(own_ref, other_ref, at_ref[0], q, low, high, bounds, 4)
    for i in range(4):
        out_ref[:, i * 128 : (i + 1) * 128] = mixed[:, i * 128 : (i + 1) * 128].T.astype(jnp.bfloat16)


def add_kernel(parts_ref, residual_ref, out_ref, block, sems):
    total = residual_ref[...]
    for i in range(parts_ref.shape[0]):
        total = total + parts_ref[i]
    block[...] = total.astype(jnp.bfloat16)
    send_copies(block, out_ref, sems)


def hidden_kernel(parts_ref, dep_ref, out_ref, block, sems):
    total = parts_ref[:8].astype(jnp.float32) + parts_ref[8:].astype(jnp.float32)
    block[...] = total.reshape(8 * HALF, 128).astype(jnp.bfloat16)
    send_copies(block, out_ref, sems)


def add_logits(core, hidden_ref, w_ref, half):
    total = jnp.zeros((256, 128), jnp.float32)
    square = jnp.zeros((8, 128), jnp.float32)
    for x in range(4):
        part = hidden_ref[x, half]
        lanes = pl.ds(pl.multiple_of((core * 4 + x) * 640, 128), 640)
        total = total + jnp.dot(w_ref[:, lanes], part, preferred_element_type=jnp.float32)
        wide = part.astype(jnp.float32)
        square = square + jnp.sum((wide * wide).reshape(80, 8, 128), axis=0)
    return total, square


def own_logits_kernel(at_ref, own_ref, w_ref, out_ref, square_ref):
    for half in range(2):
        out_ref[half], square_ref[half] = add_logits(at_ref[0], own_ref, w_ref, half)


def logits_kernel(at_ref, ids_ref, sum_ref, square_ref, other_ref, w_ref, dep_ref, out_ref):
    core, base = at_ref[0], at_ref[1]
    tops, targets = [], []
    for half in range(2):
        total, square = add_logits(1 - core, other_ref, w_ref, half)
        total, square = total + sum_ref[half], square + square_ref[half]
        mean = jnp.sum(square, axis=0, keepdims=True) * (1.0 / D)
        total = total * lax.rsqrt(mean + norm_eps)
        top = jnp.max(total, axis=0, keepdims=True)
        tops.append(top + jnp.log(jnp.sum(jnp.exp(total - top), axis=0, keepdims=True)))
        hit = iota((256, 128), 0) + base == ids_ref[half : half + 1, :]
        targets.append(jnp.sum(jnp.where(hit, total, 0.0), axis=0, keepdims=True))
    tile = jnp.concatenate(tops + targets + [jnp.zeros((4, 128), jnp.float32)], axis=0)
    for i in range(out_ref.shape[0]):
        out_ref[i] = tile


def merge(parts_ref):
    parts = parts_ref[...]
    top = jnp.max(parts, axis=0)
    lse = top + jnp.log(jnp.sum(jnp.exp(parts - top[None]), axis=0))
    return jnp.where(iota((8, 128), 0) < 2, lse, jnp.sum(parts, axis=0))


def merge_kernel(parts_ref, out_ref):
    tile = merge(parts_ref)
    for i in range(out_ref.shape[0]):
        out_ref[i] = tile


def final_kernel(at_ref, rank_ref, parts_ref, out_ref):
    core, chip = at_ref[0], at_ref[1]
    tile = merge(parts_ref)
    logprob = jnp.where(core == 0, tile[2:3] - tile[0:1], tile[3:4] - tile[1:2])
    lane = iota((1, 128), 1)
    result = jnp.zeros((1, 128), jnp.float32)
    for k in range(SCORED):
        value = jnp.sum(jnp.where(lane == chip * SCORED + k, logprob, 0.0), axis=1, keepdims=True)
        result = jnp.where(rank_ref[...] == k, value, result)
    out_ref[...] = result


def call(kernel, shape, dtype, specs, scratch=(), flops=0, size=0, name=None, out=VMEM, more=None, vmem=16):
    shapes = jax.ShapeDtypeStruct(shape, dtype)
    return pl.pallas_call(
        kernel,
        out_shape=shapes if more is None else (shapes, more),
        in_specs=specs,
        out_specs=out if more is None else (out, out),
        scratch_shapes=list(scratch),
        compiler_params=pltpu.CompilerParams(vmem_limit_bytes=vmem * 2**20),
        cost_estimate=pl.CostEstimate(flops=flops, bytes_accessed=size, transcendentals=0),
        name=name,
    )


def source_columns():
    c, yf, z, k = np.meshgrid(np.arange(2), np.arange(2), np.arange(8), np.arange(40), indexing="ij")
    return (((z * 2 + c) * 2 + yf) * 40 + k).reshape(1, 1280).astype(np.int32)


def body(
    queries,
    keys,
    values,
    out_weight,
    residual,
    norm_gain,
    head_weight,
    sampled_ids,
    loss_mask,
    doc_lengths,
):
    x, z, core = lax.axis_index("x"), lax.axis_index("z"), lax.axis_index("c")
    h, y = lax.axis_index("h"), lax.axis_index("y")
    chip = x * 8 + z
    slab = chip * 2 + core
    slabs = loss_mask.reshape(64, SLAB)
    upto = jnp.tril(jnp.ones((SLAB, SLAB), jnp.float32)).T
    rank = jnp.dot(slabs.astype(jnp.float32), upto, preferred_element_type=jnp.float32).astype(jnp.int32)
    rank = jnp.where(slabs == 1, rank - 1, -1)
    own_rank = lax.dynamic_slice_in_dim(rank, slab, 1, 0)
    packed = call(
        pack_kernel,
        (8, BLOCK, 128),
        jnp.bfloat16,
        [SMEM, VMEM, ANY, ANY, ANY],
        [
            pltpu.VMEM((BLOCK, 128), jnp.bfloat16),
            pltpu.VMEM((SLAB, 1024), jnp.bfloat16),
            pltpu.VMEM((32, 128), jnp.float32),
            pltpu.SemaphoreType.DMA((8,)),
        ],
        name="pack",
        out=HBM,
    )(slab[None], slabs, queries, keys, values)
    along_z = lax.all_to_all(packed, "z", 0, 0)

    bounds = jnp.cumsum(doc_lengths)
    position = jnp.arange(64 * SLAB, dtype=jnp.int32)
    begin = jnp.max(jnp.where(bounds[None, :] <= position[:, None], bounds[None, :], 0), axis=1)
    chosen = rank[:, None, :] == jnp.arange(SCORED, dtype=jnp.int32)[None, :, None]

    def pick(values_of):
        return jnp.sum(jnp.where(chosen, values_of.reshape(64, 1, SLAB), 0), axis=2)

    def columns(of_scored):
        pairs = of_scored.reshape(CHIPS, 2, SCORED)
        pairs = jnp.where(core == 0, pairs, pairs[:, ::-1])
        tiles = pairs.reshape(8, 4, 2, SCORED).transpose(0, 2, 1, 3)
        return jnp.repeat(tiles.reshape(8, 32), HEADS_DEV, axis=1)

    high = columns(pick(position))
    low = columns(pick(begin))
    ids = pick(sampled_ids).reshape(CHIPS, 2, SCORED).transpose(1, 0, 2).reshape(2, 128)
    span = jnp.stack((jnp.min(low, axis=1), jnp.max(low, axis=1), jnp.min(high, axis=1)))
    core_at = core[None]

    source = jnp.asarray(source_columns())
    weight = call(weight_kernel, (256, D), jnp.bfloat16, [VMEM] * 3, flops=2 * 256 * D * 1280, name="weight", vmem=28)(
        source, norm_gain[None, :], head_weight
    )
    mine = residual.reshape(2, HALF, CHIPS, 2, SCORED).transpose(3, 0, 1, 2, 4).reshape(4, HALF, 128)
    mine = lax.dynamic_index_in_dim(mine, y, 0, keepdims=False).astype(jnp.float32)
    mine = jnp.where(h == 0, mine, 0.0)

    own_begin = lax.dynamic_slice_in_dim(begin, slab * SLAB, SLAB, 0)
    own_position = slab * SLAB + jnp.arange(SLAB, dtype=jnp.int32)
    at = jnp.stack((core, own_begin[0], own_begin[SLAB - 1], chip))
    base = ((slab * 2 + h) * 4 + y) * 256

    early = (weight, mine, low, high, span, ids, own_begin)
    spread = call(
        spread_kernel,
        (4, 8, BLOCK, 128),
        jnp.bfloat16,
        [VMEM] + [ANY] * len(early),
        [pltpu.SemaphoreType.DMA((4,))],
        name="spread",
        out=HBM,
    )(along_z, *early)
    own = lax.all_to_all(spread, "x", 0, 0).reshape(CHIPS, BLOCK, 128)
    other = lax.ppermute(own, "c", [(0, 1), (1, 0)])
    parts = call(
        scored_kernel,
        (4, HALF, 128),
        jnp.float32,
        [SMEM, SMEM] + [VMEM] * 5,
        [pltpu.VMEM((256, 128), jnp.float32), pltpu.VMEM((256, 1024), jnp.bfloat16)],
        name="scored",
        vmem=28,
    )(core_at, span, low, high, own, other, out_weight)

    def context_of(start_head, after):
        return call(
            functools.partial(context_kernel, start_head),
            (SLAB, 512),
            jnp.bfloat16,
            [SMEM] + [VMEM] * 5 + [ANY],
            flops=4 * 1024 * 4224 * 128,
            size=6 * 2**20,
            name="context",
            vmem=28,
        )(at, own_begin[None, :], own_position[None, :], own, other, queries, after)

    parts = lax.all_to_all(parts, "y", 0, 0)
    block = pltpu.VMEM((HALF, 128), jnp.bfloat16)
    sums = call(
        add_kernel,
        (16, HALF, 128),
        jnp.bfloat16,
        [VMEM] * 2,
        [block, pltpu.SemaphoreType.DMA((16,))],
        name="add",
        out=HBM,
    )(parts, mine)
    context_a = context_of(0, sums)
    sums = lax.all_to_all(sums, ("h", "z"), 0, 0)
    block = pltpu.VMEM((8 * HALF, 128), jnp.bfloat16)
    hidden = call(
        hidden_kernel,
        (16, 8 * HALF, 128),
        jnp.bfloat16,
        [VMEM, ANY],
        [block, pltpu.SemaphoreType.DMA((16,))],
        name="hidden",
        out=HBM,
    )(sums, context_a)
    context_b = context_of(4, hidden)
    hidden = lax.all_to_all(hidden, ("x", "y"), 0, 0).reshape(4, 2, 640, 128)
    hidden, context_b = lax.optimization_barrier((hidden, context_b))
    hidden_other = lax.ppermute(hidden, "c", [(0, 1), (1, 0)])
    at_logits = jnp.stack((core, base))
    shares, squares = call(
        own_logits_kernel,
        (2, 256, 128),
        jnp.float32,
        [SMEM] + [VMEM] * 2,
        name="own_logits",
        more=jax.ShapeDtypeStruct((2, 8, 128), jnp.float32),
    )(at_logits, hidden, weight)
    tiles = call(logits_kernel, (32, 8, 128), jnp.float32, [SMEM] + [VMEM] * 5 + [ANY], name="logits")(
        at_logits, ids, shares, squares, hidden_other, weight, context_b
    )
    context = jnp.concatenate((context_a, context_b), axis=1)
    tiles = lax.all_to_all(tiles, ("x", "y", "c"), 0, 0)
    tiles = call(merge_kernel, (16, 8, 128), jnp.float32, [VMEM], name="merge")(tiles)
    tiles = lax.all_to_all(tiles, ("h", "z"), 0, 0)
    logprob = call(final_kernel, (1, 128), jnp.float32, [SMEM, VMEM, VMEM], name="final")(
        jnp.stack((core, chip)), own_rank, tiles
    )
    return context, logprob.reshape(128)


def solution(mesh):
    fine = Mesh(mesh.devices.reshape(4, 8, 2, 2, 4), ("x", "z", "c", "h", "y"))
    ctx, tp = ("x", "z", "c"), ("h", "y")
    placed = (
        P(ctx, tp),
        P(ctx, tp),
        P(ctx, tp),
        P(ctx, tp),
        P(ctx, None),
        P(),
        P(ctx + tp, None),
        P(),
        P(),
        P(),
    )
    return jax.shard_map(
        body, mesh=fine, in_specs=placed, out_specs=(P(ctx, tp), P(ctx)), check_vma=False
    )
```

```python
import functools
import math

import jax
import jax.numpy as jnp
import numpy as np
from jax import lax
from jax.experimental import pallas as pl
from jax.experimental.pallas import tpu as pltpu
from jax.sharding import Mesh
from jax.sharding import PartitionSpec as P

HEAD_DIM = 128
SCORED = 4
HEADS_DEV = 8
SLAB = 128
GROUP = 2
CHIPS = 32
BLOCK = 2 * SLAB + SCORED * HEADS_DEV
FEATS = 80
HALF = 40
D = 5120

masked_fill = -1e30
start_max = -5e29
norm_eps = 1e-06
LOG2E = 1.4426950408889634
SCALE2 = LOG2E / math.sqrt(HEAD_DIM)
NT = (((1,), (1,)), ((), ()))
TN = (((0,), (0,)), ((), ()))
SMEM = pl.BlockSpec(memory_space=pltpu.SMEM)
VMEM = pl.BlockSpec(memory_space=pltpu.VMEM)
ANY = pl.BlockSpec(memory_space=pl.ANY)
HBM = pl.BlockSpec(memory_space=pltpu.HBM)


def iota(shape, axis):
    return lax.broadcasted_iota(jnp.int32, shape, axis)


def send_copies(source, out_ref, sems):
    copies = [pltpu.make_async_copy(source, out_ref.at[i], sems.at[i]) for i in range(out_ref.shape[0])]
    for copy in copies:
        copy.start()
    for copy in copies:
        copy.wait()


def pack_kernel(at_ref, mask_ref, q_ref, k_ref, v_ref, block_ref, out_ref, block, queries, rows, sems):
    copies = [
        pltpu.make_async_copy(k_ref, block.at[pl.ds(0, SLAB)], sems.at[0]),
        pltpu.make_async_copy(v_ref, block.at[pl.ds(SLAB, SLAB)], sems.at[1]),
        pltpu.make_async_copy(q_ref, queries, sems.at[2]),
    ]
    for copy in copies:
        copy.start()
    mask = mask_ref[pl.ds(at_ref[0], 1), :]
    upto = (iota((SLAB, SLAB), 0) <= iota((SLAB, SLAB), 1)).astype(jnp.bfloat16)
    ones = jnp.broadcast_to(mask.astype(jnp.float32), (8, SLAB)).astype(jnp.bfloat16)
    rank = jnp.dot(ones, upto, preferred_element_type=jnp.float32).astype(jnp.int32) - 1
    chosen = jnp.where((iota((8, SLAB), 0) == rank) & (mask == 1), 1.0, 0.0).astype(jnp.bfloat16)
    for copy in copies:
        copy.wait()
    picked = jnp.dot(chosen, queries[...], preferred_element_type=jnp.float32)
    for h in range(HEADS_DEV):
        rows[pl.ds(h, SCORED, stride=HEADS_DEV), :] = picked[:SCORED, h * 128 : (h + 1) * 128]
    block[2 * SLAB :, :] = rows[...].astype(jnp.bfloat16)
    single = pltpu.make_async_copy(block, block_ref, sems.at[4])
    single.start()
    send_copies(block, out_ref, sems)
    single.wait()


def spread_kernel(at_ref, near_ref, far_ref, out_ref, sems):
    copies = []
    for i in range(4):
        for j, (ref, half) in enumerate(((near_ref, at_ref[0]), (far_ref, 1 - at_ref[0]))):
            target = out_ref.at[i, pl.ds(half * 4, 4)]
            copies.append(pltpu.make_async_copy(ref, target, sems.at[2 * i + j]))
    for copy in copies:
        copy.start()
    for copy in copies:
        copy.wait()


def weight_kernel(source_ref, gain_ref, w_ref, out_ref):
    width = 1280
    move = (iota((width, width), 0) == source_ref[...]).astype(jnp.bfloat16)
    for x in range(4):
        part = w_ref[:, x * width : (x + 1) * width].astype(jnp.float32)
        part = (part * gain_ref[:, x * width : (x + 1) * width]).astype(jnp.bfloat16)
        moved = jnp.dot(part, move, preferred_element_type=jnp.float32).astype(jnp.bfloat16)
        for c in range(2):
            out_ref[:, (c * 4 + x) * 640 : (c * 4 + x + 1) * 640] = moved[:, c * 640 : (c + 1) * 640]


def attend(own_ref, other_ref, core, q, low, high, first, last, bufs):
    columns = q.shape[0]
    half = GROUP * SLAB
    row = iota((2 * half, 1), 0)
    inside = jnp.where(row < half, row, row - half)
    key0 = (inside // SLAB) * (2 * SLAB) + inside % SLAB + jnp.where(row < half, core, 1 - core) * SLAB
    turned = q.T

    def rows(g, at):
        chips = pl.ds(pl.multiple_of(jnp.minimum(g * GROUP, CHIPS - GROUP), GROUP), GROUP)
        parts = [ref[chips, at : at + SLAB, :].reshape(half, HEAD_DIM) for ref in (own_ref, other_ref)]
        return jnp.concatenate(parts, axis=0)

    def scores(g):
        return jnp.dot(rows(g, 0), turned, preferred_element_type=jnp.float32)

    def soften(g, buf, carry):
        top, total, acc = carry
        offset = g * (2 * half)
        s = jnp.where((key0 >= low - offset) & (key0 <= high - offset), buf[...] * SCALE2, masked_fill)
        new_top = jnp.maximum(top, jnp.max(s, axis=0, keepdims=True))
        p = jnp.exp2(s - new_top)
        keep = jnp.exp2(top - new_top)
        total = total * keep + jnp.sum(p, axis=0, keepdims=True)
        pv = lax.dot_general(rows(g, SLAB), p.astype(jnp.bfloat16), TN, preferred_element_type=jnp.float32)
        return new_top, total, acc * keep + pv

    begin = first // GROUP
    steps = (last // GROUP + 2 - begin) // 2

    def step(i, carry):
        g = begin + 2 * i
        bufs[1][...] = scores(g + 1)
        carry = soften(g, bufs[0], carry)
        bufs[0][...] = scores(g + 2)
        return soften(g + 1, bufs[1], carry)

    bufs[0][...] = scores(begin)
    start = (
        jnp.full((1, columns), start_max, jnp.float32),
        jnp.zeros((1, columns), jnp.float32),
        jnp.zeros((HEAD_DIM, columns), jnp.float32),
    )
    _, total, acc = lax.fori_loop(0, steps, step, start)
    return acc / total


def scored_kernel(core_ref, first_ref, low_ref, high_ref, own_ref, other_ref, w_ref, *refs):
    out_ref, rows, scored = refs[-5:-2]
    core = core_ref[0]
    for t in range(8):
        q = jnp.concatenate(
            (
                own_ref[4 * t : 4 * t + 4, 2 * SLAB :, :].reshape(128, HEAD_DIM),
                other_ref[4 * t : 4 * t + 4, 2 * SLAB :, :].reshape(128, HEAD_DIM),
            ),
            axis=0,
        )
        mixed = attend(
            own_ref,
            other_ref,
            core,
            q,
            low_ref[t : t + 1, :],
            high_ref[t : t + 1, :],
            first_ref[t],
            4 * t + 3,
            refs[-2:],
        )
        rows[...] = mixed.T
        for h in range(HEADS_DEV):
            part = rows[pl.ds(h, 32, stride=HEADS_DEV), :].astype(jnp.bfloat16)
            lanes = slice(h * 128, (h + 1) * 128)
            scored[pl.ds(pl.multiple_of(core * 128 + t * 16, 16), 16), lanes] = part[:16]
            scored[pl.ds(pl.multiple_of((1 - core) * 128 + t * 16, 16), 16), lanes] = part[16:]
    partial = lax.dot_general(w_ref[...], scored[...], NT, preferred_element_type=jnp.float32)
    for half in range(2):
        for feats in range(2):
            out_ref[half * 2 + feats] = partial[
                feats * HALF : (feats + 1) * HALF, half * 128 : (half + 1) * 128
            ]


def context_kernel(start_head, at_ref, low_ref, high_ref, own_ref, other_ref, q_ref, *refs):
    out_ref = refs[-3]
    heads = range(start_head, start_head + 4)
    q = jnp.concatenate([q_ref[:, h * 128 : (h + 1) * 128] for h in heads], axis=0)
    low, high = jnp.tile(low_ref[...], (1, 4)), jnp.tile(high_ref[...], (1, 4))
    mixed = attend(own_ref, other_ref, at_ref[0], q, low, high, at_ref[1], at_ref[2], refs[-2:])
    for i in range(4):
        out_ref[:, i * 128 : (i + 1) * 128] = mixed[:, i * 128 : (i + 1) * 128].T.astype(jnp.bfloat16)


def add_kernel(parts_ref, residual_ref, out_ref, block, sems):
    total = residual_ref[...]
    for i in range(parts_ref.shape[0]):
        total = total + parts_ref[i]
    block[...] = total.astype(jnp.bfloat16)
    send_copies(block, out_ref, sems)


def hidden_kernel(parts_ref, dep_ref, out_ref):
    total = parts_ref[:8].astype(jnp.float32) + parts_ref[8:].astype(jnp.float32)
    total = total.reshape(8 * HALF, 128).astype(jnp.bfloat16)
    for i in range(out_ref.shape[0]):
        out_ref[i] = total


def add_logits(core, hidden_ref, w_ref, half):
    total = jnp.zeros((256, 128), jnp.float32)
    square = jnp.zeros((8, 128), jnp.float32)
    for x in range(4):
        part = hidden_ref[x, half]
        lanes = pl.ds(pl.multiple_of((core * 4 + x) * 640, 128), 640)
        total = total + jnp.dot(w_ref[:, lanes], part, preferred_element_type=jnp.float32)
        wide = part.astype(jnp.float32)
        square = square + jnp.sum((wide * wide).reshape(80, 8, 128), axis=0)
    return total, square


def own_logits_kernel(at_ref, own_ref, w_ref, out_ref, square_ref):
    for half in range(2):
        out_ref[half], square_ref[half] = add_logits(at_ref[0], own_ref, w_ref, half)


def logits_kernel(at_ref, ids_ref, sum_ref, square_ref, other_ref, w_ref, dep_ref, out_ref):
    core, base = at_ref[0], at_ref[1]
    tops, targets = [], []
    for half in range(2):
        total, square = add_logits(1 - core, other_ref, w_ref, half)
        total, square = total + sum_ref[half], square + square_ref[half]
        mean = jnp.sum(square, axis=0, keepdims=True) * (1.0 / D)
        total = total * lax.rsqrt(mean + norm_eps)
        top = jnp.max(total, axis=0, keepdims=True)
        tops.append(top + jnp.log(jnp.sum(jnp.exp(total - top), axis=0, keepdims=True)))
        hit = iota((256, 128), 0) + base == ids_ref[half : half + 1, :]
        targets.append(jnp.sum(jnp.where(hit, total, 0.0), axis=0, keepdims=True))
    tile = jnp.concatenate(tops + targets + [jnp.zeros((4, 128), jnp.float32)], axis=0)
    for i in range(out_ref.shape[0]):
        out_ref[i] = tile


def merge(parts_ref):
    parts = parts_ref[...]
    top = jnp.max(parts, axis=0)
    lse = top + jnp.log(jnp.sum(jnp.exp(parts - top[None]), axis=0))
    return jnp.where(iota((8, 128), 0) < 2, lse, jnp.sum(parts, axis=0))


def merge_kernel(parts_ref, out_ref):
    tile = merge(parts_ref)
    for i in range(out_ref.shape[0]):
        out_ref[i] = tile


def final_kernel(at_ref, rank_ref, parts_ref, out_ref):
    core, chip = at_ref[0], at_ref[1]
    tile = merge(parts_ref)
    logprob = jnp.where(core == 0, tile[2:3] - tile[0:1], tile[3:4] - tile[1:2])
    lane = iota((1, 128), 1)
    result = jnp.zeros((1, 128), jnp.float32)
    for k in range(SCORED):
        value = jnp.sum(jnp.where(lane == chip * SCORED + k, logprob, 0.0), axis=1, keepdims=True)
        result = jnp.where(rank_ref[...] == k, value, result)
    out_ref[...] = result


def call(kernel, shape, dtype, specs, scratch=(), flops=0, size=0, name=None, out=VMEM, more=None, vmem=16):
    shapes = jax.ShapeDtypeStruct(shape, dtype)
    return pl.pallas_call(
        kernel,
        out_shape=shapes if more is None else (shapes, more),
        in_specs=specs,
        out_specs=out if more is None else (out, out),
        scratch_shapes=list(scratch),
        compiler_params=pltpu.CompilerParams(vmem_limit_bytes=vmem * 2**20),
        cost_estimate=pl.CostEstimate(flops=flops, bytes_accessed=size, transcendentals=0),
        name=name,
    )


def source_columns():
    c, yf, z, k = np.meshgrid(np.arange(2), np.arange(2), np.arange(8), np.arange(40), indexing="ij")
    return (((z * 2 + c) * 2 + yf) * 40 + k).reshape(1, 1280).astype(np.int32)


def body(
    queries,
    keys,
    values,
    out_weight,
    residual,
    norm_gain,
    head_weight,
    sampled_ids,
    loss_mask,
    doc_lengths,
):
    x, z, core = lax.axis_index("x"), lax.axis_index(("zh", "zl")), lax.axis_index("c")
    h, y = lax.axis_index("h"), lax.axis_index("y")
    chip = x * 8 + z
    slab = chip * 2 + core
    slabs = loss_mask.reshape(64, SLAB)
    upto = jnp.tril(jnp.ones((SLAB, SLAB), jnp.float32)).T
    rank = jnp.dot(slabs.astype(jnp.float32), upto, preferred_element_type=jnp.float32).astype(jnp.int32)
    rank = jnp.where(slabs == 1, rank - 1, -1)
    own_rank = lax.dynamic_slice_in_dim(rank, slab, 1, 0)
    block, packed = call(
        pack_kernel,
        (BLOCK, 128),
        jnp.bfloat16,
        [SMEM, VMEM, HBM, HBM, HBM],
        [
            pltpu.VMEM((BLOCK, 128), jnp.bfloat16),
            pltpu.VMEM((SLAB, 1024), jnp.bfloat16),
            pltpu.VMEM((32, 128), jnp.float32),
            pltpu.SemaphoreType.DMA((5,)),
        ],
        name="pack",
        out=ANY,
        more=jax.ShapeDtypeStruct((4, BLOCK, 128), jnp.bfloat16),
    )(slab[None], slabs, queries, keys, values)
    block = lax.ppermute(block, ("zh", "zl"), [(i, i ^ 4) for i in range(8)])
    near = lax.all_to_all(packed, "zl", 0, 0)
    near, block = lax.optimization_barrier((near, block))
    far = lax.all_to_all(jnp.broadcast_to(block[None], (4, BLOCK, 128)), "zl", 0, 0)

    bounds = jnp.cumsum(doc_lengths)
    position = jnp.arange(64 * SLAB, dtype=jnp.int32)
    begin = jnp.max(jnp.where(bounds[None, :] <= position[:, None], bounds[None, :], 0), axis=1)
    chosen = rank[:, None, :] == jnp.arange(SCORED, dtype=jnp.int32)[None, :, None]

    def pick(values_of):
        return jnp.sum(jnp.where(chosen, values_of.reshape(64, 1, SLAB), 0), axis=2)

    def columns(of_scored):
        pairs = of_scored.reshape(CHIPS, 2, SCORED)
        pairs = jnp.where(core == 0, pairs, pairs[:, ::-1])
        tiles = pairs.reshape(8, 4, 2, SCORED).transpose(0, 2, 1, 3)
        return jnp.repeat(tiles.reshape(8, 32), HEADS_DEV, axis=1)

    high = columns(pick(position))
    low = columns(pick(begin))
    ids = pick(sampled_ids).reshape(CHIPS, 2, SCORED).transpose(1, 0, 2).reshape(2, 128)
    first = jnp.min(low, axis=1) // 256
    core_at = core[None]

    source = jnp.asarray(source_columns())
    weight = call(weight_kernel, (256, D), jnp.bfloat16, [VMEM] * 3, flops=2 * 256 * D * 1280, name="weight", vmem=28)(
        source, norm_gain[None, :], head_weight
    )
    mine = residual.reshape(2, HALF, CHIPS, 2, SCORED).transpose(3, 0, 1, 2, 4).reshape(4, HALF, 128)
    mine = lax.dynamic_index_in_dim(mine, y, 0, keepdims=False).astype(jnp.float32)
    mine = jnp.where(h == 0, mine, 0.0)

    own_begin = lax.dynamic_slice_in_dim(begin, slab * SLAB, SLAB, 0)
    own_position = slab * SLAB + jnp.arange(SLAB, dtype=jnp.int32)
    at = jnp.stack((core, own_begin[0] // 256, chip))
    base = ((slab * 2 + h) * 4 + y) * 256

    spread = call(
        spread_kernel,
        (4, 8, BLOCK, 128),
        jnp.bfloat16,
        [SMEM, VMEM, VMEM],
        [pltpu.SemaphoreType.DMA((8,))],
        name="spread",
        out=ANY,
    )(lax.axis_index("zh")[None], near, far)
    own = lax.all_to_all(spread, "x", 0, 0).reshape(CHIPS, BLOCK, 128)
    own, weight, mine, low, high, first, ids, own_begin = lax.optimization_barrier(
        (own, weight, mine, low, high, first, ids, own_begin)
    )
    other = lax.ppermute(own, "c", [(0, 1), (1, 0)])
    scores = pltpu.VMEM((2 * GROUP * SLAB, 256), jnp.float32)
    parts = call(
        scored_kernel,
        (4, HALF, 128),
        jnp.float32,
        [SMEM, SMEM] + [VMEM] * 5,
        [pltpu.VMEM((256, 128), jnp.float32), pltpu.VMEM((256, 1024), jnp.bfloat16), scores, scores],
        name="scored",
        vmem=28,
    )(core_at, first, low, high, own, other, out_weight)

    def context_of(start_head, after):
        return call(
            functools.partial(context_kernel, start_head),
            (SLAB, 512),
            jnp.bfloat16,
            [SMEM] + [VMEM] * 5 + [ANY],
            [pltpu.VMEM((2 * GROUP * SLAB, 512), jnp.float32)] * 2,
            flops=4 * 1024 * 4224 * 128,
            size=6 * 2**20,
            name="context",
            vmem=28,
        )(at, own_begin[None, :], own_position[None, :], own, other, queries, after)

    parts = lax.all_to_all(parts, "y", 0, 0)
    block = pltpu.VMEM((HALF, 128), jnp.bfloat16)
    sums = call(
        add_kernel,
        (16, HALF, 128),
        jnp.bfloat16,
        [VMEM] * 2,
        [block, pltpu.SemaphoreType.DMA((16,))],
        name="add",
        out=HBM,
    )(parts, mine)
    context_a = context_of(0, sums)
    sums = lax.all_to_all(sums, ("h", "zh", "zl"), 0, 0)
    hidden = call(hidden_kernel, (16, 8 * HALF, 128), jnp.bfloat16, [VMEM, ANY], name="hidden")(sums, context_a)
    context_b = context_of(4, hidden)
    hidden = lax.all_to_all(hidden, ("x", "y"), 0, 0).reshape(4, 2, 640, 128)
    hidden, context_b = lax.optimization_barrier((hidden, context_b))
    hidden_other = lax.ppermute(hidden, "c", [(0, 1), (1, 0)])
    at_logits = jnp.stack((core, base))
    shares, squares = call(
        own_logits_kernel,
        (2, 256, 128),
        jnp.float32,
        [SMEM] + [VMEM] * 2,
        name="own_logits",
        more=jax.ShapeDtypeStruct((2, 8, 128), jnp.float32),
    )(at_logits, hidden, weight)
    tiles = call(logits_kernel, (32, 8, 128), jnp.float32, [SMEM] + [VMEM] * 5 + [ANY], name="logits")(
        at_logits, ids, shares, squares, hidden_other, weight, context_b
    )
    context = jnp.concatenate((context_a, context_b), axis=1)
    tiles = lax.all_to_all(tiles, ("x", "y", "c"), 0, 0)
    tiles = call(merge_kernel, (16, 8, 128), jnp.float32, [VMEM], name="merge")(tiles)
    tiles = lax.all_to_all(tiles, ("h", "zh", "zl"), 0, 0)
    logprob = call(final_kernel, (1, 128), jnp.float32, [SMEM, VMEM, VMEM], name="final")(
        jnp.stack((core, chip)), own_rank, tiles
    )
    return context, logprob.reshape(128)


def solution(mesh):
    fine = Mesh(mesh.devices.reshape(4, 2, 4, 2, 2, 4), ("x", "zh", "zl", "c", "h", "y"))
    ctx, tp = ("x", "zh", "zl", "c"), ("h", "y")
    placed = (
        P(ctx, tp),
        P(ctx, tp),
        P(ctx, tp),
        P(ctx, tp),
        P(ctx, None),
        P(),
        P(ctx + tp, None),
        P(),
        P(),
        P(),
    )
    return jax.shard_map(
        body, mesh=fine, in_specs=placed, out_specs=(P(ctx, tp), P(ctx)), check_vma=False
    )
```

```python
import functools
import math

import jax
import jax.numpy as jnp
import numpy as np
from jax import lax
from jax.experimental import pallas as pl
from jax.experimental.pallas import tpu as pltpu
from jax.sharding import Mesh
from jax.sharding import PartitionSpec as P

HEAD_DIM = 128
SCORED = 4
HEADS_DEV = 8
SLAB = 128
GROUP = 2
CHIPS = 32
BLOCK = 2 * SLAB + SCORED * HEADS_DEV
FEATS = 80
HALF = 40
D = 5120

masked_fill = -1e30
start_max = -5e29
norm_eps = 1e-06
LOG2E = 1.4426950408889634
SCALE2 = LOG2E / math.sqrt(HEAD_DIM)
NT = (((1,), (1,)), ((), ()))
TN = (((0,), (0,)), ((), ()))
SMEM = pl.BlockSpec(memory_space=pltpu.SMEM)
VMEM = pl.BlockSpec(memory_space=pltpu.VMEM)
ANY = pl.BlockSpec(memory_space=pl.ANY)
HBM = pl.BlockSpec(memory_space=pltpu.HBM)


def iota(shape, axis):
    return lax.broadcasted_iota(jnp.int32, shape, axis)


def send_copies(source, out_ref, sems):
    copies = [pltpu.make_async_copy(source, out_ref.at[i], sems.at[i]) for i in range(out_ref.shape[0])]
    for copy in copies:
        copy.start()
    for copy in copies:
        copy.wait()


def pack_kernel(at_ref, mask_ref, q_ref, k_ref, v_ref, block_ref, out_ref, block, queries, rows, sems):
    copies = [
        pltpu.make_async_copy(k_ref, block.at[pl.ds(0, SLAB)], sems.at[0]),
        pltpu.make_async_copy(v_ref, block.at[pl.ds(SLAB, SLAB)], sems.at[1]),
        pltpu.make_async_copy(q_ref, queries, sems.at[2]),
    ]
    for copy in copies:
        copy.start()
    mask = mask_ref[pl.ds(at_ref[0], 1), :]
    upto = (iota((SLAB, SLAB), 0) <= iota((SLAB, SLAB), 1)).astype(jnp.bfloat16)
    ones = jnp.broadcast_to(mask.astype(jnp.float32), (8, SLAB)).astype(jnp.bfloat16)
    rank = jnp.dot(ones, upto, preferred_element_type=jnp.float32).astype(jnp.int32) - 1
    chosen = jnp.where((iota((8, SLAB), 0) == rank) & (mask == 1), 1.0, 0.0).astype(jnp.bfloat16)
    for copy in copies:
        copy.wait()
    picked = jnp.dot(chosen, queries[...], preferred_element_type=jnp.float32)
    for h in range(HEADS_DEV):
        rows[pl.ds(h, SCORED, stride=HEADS_DEV), :] = picked[:SCORED, h * 128 : (h + 1) * 128]
    block[2 * SLAB :, :] = rows[...].astype(jnp.bfloat16)
    single = pltpu.make_async_copy(block, block_ref, sems.at[4])
    single.start()
    send_copies(block, out_ref, sems)
    single.wait()


def spread_kernel(near_ref, out_ref, sems):
    send_copies(near_ref, out_ref, sems)


def spread_far_kernel(at_ref, *refs):
    out_ref, sems = refs[-2:]
    copies = []
    for i in range(4):
        for k in range(4):
            copies.append(
                pltpu.make_async_copy(refs[k], out_ref.at[i, jnp.bitwise_xor(at_ref[0], k)], sems.at[i * 4 + k])
            )
    for copy in copies:
        copy.start()
    for copy in copies:
        copy.wait()


def collect(half, near_far, held, sems):
    copies = []
    for i, (near_ref, far_ref) in enumerate(near_far):
        for x in range(4):
            for j, ref in enumerate((near_ref, far_ref)):
                at = x * 8 + (half * 4 if j == 0 else (1 - half) * 4)
                target = held.at[i, pl.ds(pl.multiple_of(at, 4), 4)]
                copies.append(pltpu.make_async_copy(ref.at[x], target, sems.at[i * 8 + x * 2 + j]))
    for copy in copies:
        copy.start()
    for copy in copies:
        copy.wait()


def weight_kernel(source_ref, gain_ref, w_ref, out_ref):
    width = 1280
    move = (iota((width, width), 0) == source_ref[...]).astype(jnp.bfloat16)
    for x in range(4):
        part = w_ref[:, x * width : (x + 1) * width].astype(jnp.float32)
        part = (part * gain_ref[:, x * width : (x + 1) * width]).astype(jnp.bfloat16)
        moved = jnp.dot(part, move, preferred_element_type=jnp.float32).astype(jnp.bfloat16)
        for c in range(2):
            out_ref[:, (c * 4 + x) * 640 : (c * 4 + x + 1) * 640] = moved[:, c * 640 : (c + 1) * 640]


def attend(own_ref, other_ref, core, q, low, high, first, last, bufs):
    columns = q.shape[0]
    half = GROUP * SLAB
    row = iota((2 * half, 1), 0)
    inside = jnp.where(row < half, row, row - half)
    key0 = (inside // SLAB) * (2 * SLAB) + inside % SLAB + jnp.where(row < half, core, 1 - core) * SLAB
    turned = q.T

    def rows(g, at):
        chips = pl.ds(pl.multiple_of(jnp.minimum(g * GROUP, CHIPS - GROUP), GROUP), GROUP)
        parts = [ref[chips, at : at + SLAB, :].reshape(half, HEAD_DIM) for ref in (own_ref, other_ref)]
        return jnp.concatenate(parts, axis=0)

    def scores(g):
        return jnp.dot(rows(g, 0), turned, preferred_element_type=jnp.float32)

    def soften(g, buf, carry):
        top, total, acc = carry
        offset = g * (2 * half)
        s = jnp.where((key0 >= low - offset) & (key0 <= high - offset), buf[...] * SCALE2, masked_fill)
        new_top = jnp.maximum(top, jnp.max(s, axis=0, keepdims=True))
        p = jnp.exp2(s - new_top)
        keep = jnp.exp2(top - new_top)
        total = total * keep + jnp.sum(p, axis=0, keepdims=True)
        pv = lax.dot_general(rows(g, SLAB), p.astype(jnp.bfloat16), TN, preferred_element_type=jnp.float32)
        return new_top, total, acc * keep + pv

    begin = first // GROUP
    steps = (last // GROUP + 2 - begin) // 2

    def step(i, carry):
        g = begin + 2 * i
        bufs[1][...] = scores(g + 1)
        carry = soften(g, bufs[0], carry)
        bufs[0][...] = scores(g + 2)
        return soften(g + 1, bufs[1], carry)

    bufs[0][...] = scores(begin)
    start = (
        jnp.full((1, columns), start_max, jnp.float32),
        jnp.zeros((1, columns), jnp.float32),
        jnp.zeros((HEAD_DIM, columns), jnp.float32),
    )
    _, total, acc = lax.fori_loop(0, steps, step, start)
    return acc / total


def scored_kernel(core_ref, first_ref, low_ref, high_ref, near, far, near_other, far_other, w_ref, *refs):
    out_ref, rows, scored, held, sems = refs[-7:-2]
    core = core_ref[0]
    collect(core_ref[1], ((near, far), (near_other, far_other)), held, sems)
    own_ref, other_ref = held.at[0], held.at[1]
    for t in range(8):
        q = jnp.concatenate(
            (
                own_ref[4 * t : 4 * t + 4, 2 * SLAB :, :].reshape(128, HEAD_DIM),
                other_ref[4 * t : 4 * t + 4, 2 * SLAB :, :].reshape(128, HEAD_DIM),
            ),
            axis=0,
        )
        mixed = attend(
            own_ref,
            other_ref,
            core,
            q,
            low_ref[t : t + 1, :],
            high_ref[t : t + 1, :],
            first_ref[t],
            4 * t + 3,
            refs[-2:],
        )
        rows[...] = mixed.T
        for h in range(HEADS_DEV):
            part = rows[pl.ds(h, 32, stride=HEADS_DEV), :].astype(jnp.bfloat16)
            lanes = slice(h * 128, (h + 1) * 128)
            scored[pl.ds(pl.multiple_of(core * 128 + t * 16, 16), 16), lanes] = part[:16]
            scored[pl.ds(pl.multiple_of((1 - core) * 128 + t * 16, 16), 16), lanes] = part[16:]
    partial = lax.dot_general(w_ref[...], scored[...], NT, preferred_element_type=jnp.float32)
    for half in range(2):
        for feats in range(2):
            out_ref[half * 2 + feats] = partial[
                feats * HALF : (feats + 1) * HALF, half * 128 : (half + 1) * 128
            ]


def context_kernel(start_head, at_ref, low_ref, high_ref, near, far, near_other, far_other, q_ref, *refs):
    out_ref, held, sems = refs[-5:-2]
    collect(at_ref[3], ((near, far), (near_other, far_other)), held, sems)
    own_ref, other_ref = held.at[0], held.at[1]
    heads = range(start_head, start_head + 4)
    q = jnp.concatenate([q_ref[:, h * 128 : (h + 1) * 128] for h in heads], axis=0)
    low, high = jnp.tile(low_ref[...], (1, 4)), jnp.tile(high_ref[...], (1, 4))
    mixed = attend(own_ref, other_ref, at_ref[0], q, low, high, at_ref[1], at_ref[2], refs[-2:])
    for i in range(4):
        out_ref[:, i * 128 : (i + 1) * 128] = mixed[:, i * 128 : (i + 1) * 128].T.astype(jnp.bfloat16)


def add_kernel(parts_ref, residual_ref, out_ref, block, sems):
    total = residual_ref[...]
    for i in range(parts_ref.shape[0]):
        total = total + parts_ref[i]
    block[...] = total.astype(jnp.bfloat16)
    send_copies(block, out_ref, sems)


def hidden_kernel(parts_ref, dep_ref, out_ref):
    total = parts_ref[:8].astype(jnp.float32) + parts_ref[8:].astype(jnp.float32)
    total = total.reshape(8 * HALF, 128).astype(jnp.bfloat16)
    for i in range(out_ref.shape[0]):
        out_ref[i] = total


def add_logits(core, hidden_ref, w_ref, half):
    total = jnp.zeros((256, 128), jnp.float32)
    square = jnp.zeros((8, 128), jnp.float32)
    for x in range(4):
        part = hidden_ref[x, half]
        lanes = pl.ds(pl.multiple_of((core * 4 + x) * 640, 128), 640)
        total = total + jnp.dot(w_ref[:, lanes], part, preferred_element_type=jnp.float32)
        wide = part.astype(jnp.float32)
        square = square + jnp.sum((wide * wide).reshape(80, 8, 128), axis=0)
    return total, square


def own_logits_kernel(at_ref, own_ref, w_ref, out_ref, square_ref):
    for half in range(2):
        out_ref[half], square_ref[half] = add_logits(at_ref[0], own_ref, w_ref, half)


def logits_kernel(at_ref, ids_ref, sum_ref, square_ref, other_ref, w_ref, dep_ref, out_ref):
    core, base = at_ref[0], at_ref[1]
    tops, targets = [], []
    for half in range(2):
        total, square = add_logits(1 - core, other_ref, w_ref, half)
        total, square = total + sum_ref[half], square + square_ref[half]
        mean = jnp.sum(square, axis=0, keepdims=True) * (1.0 / D)
        total = total * lax.rsqrt(mean + norm_eps)
        top = jnp.max(total, axis=0, keepdims=True)
        tops.append(top + jnp.log(jnp.sum(jnp.exp(total - top), axis=0, keepdims=True)))
        hit = iota((256, 128), 0) + base == ids_ref[half : half + 1, :]
        targets.append(jnp.sum(jnp.where(hit, total, 0.0), axis=0, keepdims=True))
    tile = jnp.concatenate(tops + targets + [jnp.zeros((4, 128), jnp.float32)], axis=0)
    for i in range(out_ref.shape[0]):
        out_ref[i] = tile


def merge(parts_ref):
    parts = parts_ref[...]
    top = jnp.max(parts, axis=0)
    lse = top + jnp.log(jnp.sum(jnp.exp(parts - top[None]), axis=0))
    return jnp.where(iota((8, 128), 0) < 2, lse, jnp.sum(parts, axis=0))


def merge_kernel(parts_ref, out_ref):
    tile = merge(parts_ref)
    for i in range(out_ref.shape[0]):
        out_ref[i] = tile


def final_kernel(at_ref, rank_ref, parts_ref, out_ref):
    core, chip = at_ref[0], at_ref[1]
    tile = merge(parts_ref)
    logprob = jnp.where(core == 0, tile[2:3] - tile[0:1], tile[3:4] - tile[1:2])
    lane = iota((1, 128), 1)
    result = jnp.zeros((1, 128), jnp.float32)
    for k in range(SCORED):
        value = jnp.sum(jnp.where(lane == chip * SCORED + k, logprob, 0.0), axis=1, keepdims=True)
        result = jnp.where(rank_ref[...] == k, value, result)
    out_ref[...] = result


def call(kernel, shape, dtype, specs, scratch=(), flops=0, size=0, name=None, out=VMEM, more=None, vmem=16):
    shapes = jax.ShapeDtypeStruct(shape, dtype)
    return pl.pallas_call(
        kernel,
        out_shape=shapes if more is None else (shapes, more),
        in_specs=specs,
        out_specs=out if more is None else (out, out),
        scratch_shapes=list(scratch),
        compiler_params=pltpu.CompilerParams(vmem_limit_bytes=int(vmem * 2**20)),
        cost_estimate=pl.CostEstimate(flops=flops, bytes_accessed=size, transcendentals=0),
        name=name,
    )


def source_columns():
    c, yf, z, k = np.meshgrid(np.arange(2), np.arange(2), np.arange(8), np.arange(40), indexing="ij")
    return (((z * 2 + c) * 2 + yf) * 40 + k).reshape(1, 1280).astype(np.int32)


def body(
    queries,
    keys,
    values,
    out_weight,
    residual,
    norm_gain,
    head_weight,
    sampled_ids,
    loss_mask,
    doc_lengths,
):
    x, z, core = lax.axis_index("x"), lax.axis_index(("zh", "zl")), lax.axis_index("c")
    h, y = lax.axis_index("h"), lax.axis_index("y")
    chip = x * 8 + z
    slab = chip * 2 + core
    slabs = loss_mask.reshape(64, SLAB)
    upto = jnp.tril(jnp.ones((SLAB, SLAB), jnp.float32)).T
    rank = jnp.dot(slabs.astype(jnp.float32), upto, preferred_element_type=jnp.float32).astype(jnp.int32)
    rank = jnp.where(slabs == 1, rank - 1, -1)
    own_rank = lax.dynamic_slice_in_dim(rank, slab, 1, 0)
    block, packed = call(
        pack_kernel,
        (BLOCK, 128),
        jnp.bfloat16,
        [SMEM, VMEM, HBM, HBM, HBM],
        [
            pltpu.VMEM((BLOCK, 128), jnp.bfloat16),
            pltpu.VMEM((SLAB, 1024), jnp.bfloat16),
            pltpu.VMEM((32, 128), jnp.float32),
            pltpu.SemaphoreType.DMA((5,)),
        ],
        name="pack",
        out=ANY,
        vmem=63.9,
        more=jax.ShapeDtypeStruct((4, BLOCK, 128), jnp.bfloat16),
    )(slab[None], slabs, queries, keys, values)
    block = lax.ppermute(block, ("zh", "zl"), [(i, i ^ 4) for i in range(8)])
    near = lax.all_to_all(packed, "zl", 0, 0)
    spread = call(
        spread_kernel, (4, 4, BLOCK, 128), jnp.bfloat16, [VMEM], [pltpu.SemaphoreType.DMA((4,))], name="spread", out=ANY
    )(near)
    spread, block = lax.optimization_barrier((spread, block))
    near = lax.all_to_all(spread, "x", 0, 0)
    blocks = [block] + [lax.ppermute(block, "zl", [(i, i ^ k) for i in range(4)]) for k in (1, 2, 3)]
    spread = call(
        spread_far_kernel,
        (4, 4, BLOCK, 128),
        jnp.bfloat16,
        [SMEM] + [VMEM] * 4,
        [pltpu.SemaphoreType.DMA((16,))],
        name="spread_far",
        out=ANY,
    )(lax.axis_index("zl")[None], *blocks)
    near, spread = lax.optimization_barrier((near, spread))
    far = lax.all_to_all(spread, "x", 0, 0)
    near_other = lax.ppermute(near, "c", [(0, 1), (1, 0)])

    bounds = jnp.cumsum(doc_lengths)
    position = jnp.arange(64 * SLAB, dtype=jnp.int32)
    begin = jnp.max(jnp.where(bounds[None, :] <= position[:, None], bounds[None, :], 0), axis=1)
    chosen = rank[:, None, :] == jnp.arange(SCORED, dtype=jnp.int32)[None, :, None]

    def pick(values_of):
        return jnp.sum(jnp.where(chosen, values_of.reshape(64, 1, SLAB), 0), axis=2)

    def columns(of_scored):
        pairs = of_scored.reshape(CHIPS, 2, SCORED)
        pairs = jnp.where(core == 0, pairs, pairs[:, ::-1])
        tiles = pairs.reshape(8, 4, 2, SCORED).transpose(0, 2, 1, 3)
        return jnp.repeat(tiles.reshape(8, 32), HEADS_DEV, axis=1)

    high = columns(pick(position))
    low = columns(pick(begin))
    ids = pick(sampled_ids).reshape(CHIPS, 2, SCORED).transpose(1, 0, 2).reshape(2, 128)
    first = jnp.min(low, axis=1) // 256
    half = lax.axis_index("zh")
    core_at = jnp.stack((core, half))

    source = jnp.asarray(source_columns())
    weight = call(weight_kernel, (256, D), jnp.bfloat16, [VMEM] * 3, flops=2 * 256 * D * 1280, name="weight", vmem=28)(
        source, norm_gain[None, :], head_weight
    )
    mine = residual.reshape(2, HALF, CHIPS, 2, SCORED).transpose(3, 0, 1, 2, 4).reshape(4, HALF, 128)
    mine = lax.dynamic_index_in_dim(mine, y, 0, keepdims=False).astype(jnp.float32)
    mine = jnp.where(h == 0, mine, 0.0)

    own_begin = lax.dynamic_slice_in_dim(begin, slab * SLAB, SLAB, 0)
    own_position = slab * SLAB + jnp.arange(SLAB, dtype=jnp.int32)
    at = jnp.stack((core, own_begin[0] // 256, chip, half))
    base = ((slab * 2 + h) * 4 + y) * 256

    far, near_other, weight, mine, low, high, first, ids, own_begin = lax.optimization_barrier(
        (far, near_other, weight, mine, low, high, first, ids, own_begin)
    )
    far_other = lax.ppermute(far, "c", [(0, 1), (1, 0)])
    blocks = (near, far, near_other, far_other)
    held = [pltpu.VMEM((2, CHIPS, BLOCK, 128), jnp.bfloat16), pltpu.SemaphoreType.DMA((16,))]
    scores = pltpu.VMEM((2 * GROUP * SLAB, 256), jnp.float32)
    parts = call(
        scored_kernel,
        (4, HALF, 128),
        jnp.float32,
        [SMEM, SMEM, VMEM, VMEM] + [ANY] * 4 + [VMEM],
        [pltpu.VMEM((256, 128), jnp.float32), pltpu.VMEM((256, 1024), jnp.bfloat16)] + held + [scores, scores],
        name="scored",
        vmem=28,
    )(core_at, first, low, high, *blocks, out_weight)

    def context_of(start_head, after):
        return call(
            functools.partial(context_kernel, start_head),
            (SLAB, 512),
            jnp.bfloat16,
            [SMEM, VMEM, VMEM] + [ANY] * 4 + [VMEM, ANY],
            held + [pltpu.VMEM((2 * GROUP * SLAB, 512), jnp.float32)] * 2,
            flops=4 * 1024 * 4224 * 128,
            size=6 * 2**20,
            name="context",
            vmem=28,
        )(at, own_begin[None, :], own_position[None, :], *blocks, queries, after)

    parts = lax.all_to_all(parts, "y", 0, 0)
    block = pltpu.VMEM((HALF, 128), jnp.bfloat16)
    sums = call(
        add_kernel,
        (16, HALF, 128),
        jnp.bfloat16,
        [VMEM] * 2,
        [block, pltpu.SemaphoreType.DMA((16,))],
        name="add",
        out=HBM,
    )(parts, mine)
    context_a = context_of(0, sums)
    sums = lax.all_to_all(sums, ("h", "zh", "zl"), 0, 0)
    hidden = call(hidden_kernel, (16, 8 * HALF, 128), jnp.bfloat16, [VMEM, ANY], name="hidden")(sums, context_a)
    context_b = context_of(4, hidden)
    hidden = lax.all_to_all(hidden, ("x", "y"), 0, 0).reshape(4, 2, 640, 128)
    hidden, context_b = lax.optimization_barrier((hidden, context_b))
    hidden_other = lax.ppermute(hidden, "c", [(0, 1), (1, 0)])
    at_logits = jnp.stack((core, base))
    shares, squares = call(
        own_logits_kernel,
        (2, 256, 128),
        jnp.float32,
        [SMEM] + [VMEM] * 2,
        name="own_logits",
        more=jax.ShapeDtypeStruct((2, 8, 128), jnp.float32),
    )(at_logits, hidden, weight)
    tiles = call(logits_kernel, (32, 8, 128), jnp.float32, [SMEM] + [VMEM] * 5 + [ANY], name="logits")(
        at_logits, ids, shares, squares, hidden_other, weight, context_b
    )
    context = jnp.concatenate((context_a, context_b), axis=1)
    tiles = lax.all_to_all(tiles, ("x", "y", "c"), 0, 0)
    tiles = call(merge_kernel, (16, 8, 128), jnp.float32, [VMEM], name="merge")(tiles)
    tiles = lax.all_to_all(tiles, ("h", "zh", "zl"), 0, 0)
    logprob = call(final_kernel, (1, 128), jnp.float32, [SMEM, VMEM, VMEM], name="final")(
        jnp.stack((core, chip)), own_rank, tiles
    )
    return context, logprob.reshape(128)


def solution(mesh):
    fine = Mesh(mesh.devices.reshape(4, 2, 4, 2, 2, 4), ("x", "zh", "zl", "c", "h", "y"))
    ctx, tp = ("x", "zh", "zl", "c"), ("h", "y")
    placed = (
        P(ctx, tp),
        P(ctx, tp),
        P(ctx, tp),
        P(ctx, tp),
        P(ctx, None),
        P(),
        P(ctx + tp, None),
        P(),
        P(),
        P(),
    )
    return jax.shard_map(
        body, mesh=fine, in_specs=placed, out_specs=(P(ctx, tp), P(ctx)), check_vma=False
    )
```

```python
import functools
import math

import jax
import jax.numpy as jnp
import numpy as np
from jax import lax
from jax.experimental import pallas as pl
from jax.experimental.pallas import tpu as pltpu
from jax.sharding import Mesh
from jax.sharding import PartitionSpec as P

HEAD_DIM = 128
SCORED = 4
HEADS_DEV = 8
SLAB = 128
GROUP = 2
CHIPS = 32
BLOCK = 2 * SLAB + SCORED * HEADS_DEV
FEATS = 80
HALF = 40
D = 5120

masked_fill = -1e30
start_max = -5e29
norm_eps = 1e-06
LOG2E = 1.4426950408889634
SCALE2 = LOG2E / math.sqrt(HEAD_DIM)
NT = (((1,), (1,)), ((), ()))
TN = (((0,), (0,)), ((), ()))
SMEM = pl.BlockSpec(memory_space=pltpu.SMEM)
VMEM = pl.BlockSpec(memory_space=pltpu.VMEM)
ANY = pl.BlockSpec(memory_space=pl.ANY)
HBM = pl.BlockSpec(memory_space=pltpu.HBM)


def iota(shape, axis):
    return lax.broadcasted_iota(jnp.int32, shape, axis)


def send_copies(source, out_ref, sems):
    copies = [pltpu.make_async_copy(source, out_ref.at[i], sems.at[i]) for i in range(out_ref.shape[0])]
    for copy in copies:
        copy.start()
    for copy in copies:
        copy.wait()


def pack_kernel(at_ref, mask_ref, q_ref, k_ref, v_ref, block_ref, out_ref, block, queries, rows, sems):
    copies = [
        pltpu.make_async_copy(k_ref, block.at[pl.ds(0, SLAB)], sems.at[0]),
        pltpu.make_async_copy(v_ref, block.at[pl.ds(SLAB, SLAB)], sems.at[1]),
        pltpu.make_async_copy(q_ref, queries, sems.at[2]),
    ]
    for copy in copies:
        copy.start()
    mask = mask_ref[pl.ds(at_ref[0], 1), :]
    upto = (iota((SLAB, SLAB), 0) <= iota((SLAB, SLAB), 1)).astype(jnp.bfloat16)
    ones = jnp.broadcast_to(mask.astype(jnp.float32), (8, SLAB)).astype(jnp.bfloat16)
    rank = jnp.dot(ones, upto, preferred_element_type=jnp.float32).astype(jnp.int32) - 1
    chosen = jnp.where((iota((8, SLAB), 0) == rank) & (mask == 1), 1.0, 0.0).astype(jnp.bfloat16)
    for copy in copies:
        copy.wait()
    picked = jnp.dot(chosen, queries[...], preferred_element_type=jnp.float32)
    for h in range(HEADS_DEV):
        rows[pl.ds(h, SCORED, stride=HEADS_DEV), :] = picked[:SCORED, h * 128 : (h + 1) * 128]
    block[2 * SLAB :, :] = rows[...].astype(jnp.bfloat16)
    single = pltpu.make_async_copy(block, block_ref, sems.at[4])
    single.start()
    send_copies(block, out_ref, sems)
    single.wait()


def spread_kernel(*refs):
    out_ref, sems = refs[-2:]
    copies = []
    for i in range(4):
        at = 0
        for ref in refs[:-2]:
            count = ref.shape[0] if len(ref.shape) == 3 else 1
            target = out_ref.at[i, pl.ds(at, count)] if len(ref.shape) == 3 else out_ref.at[i, at]
            copies.append(pltpu.make_async_copy(ref, target, sems.at[len(copies)]))
            at += count
    for copy in copies:
        copy.start()
    for copy in copies:
        copy.wait()


def collect(half, place, near_far, held, sems):
    copies = []

    def add(source, i, at, count=None):
        target = held.at[i, at] if count is None else held.at[i, pl.ds(pl.multiple_of(at, 4), count)]
        copies.append(pltpu.make_async_copy(source, target, sems.at[len(copies)]))

    for i, (near_ref, far_ref) in enumerate(near_far):
        for x in range(4):
            beyond = x * 8 + (1 - half) * 4
            add(near_ref.at[x, pl.ds(0, 4)], i, x * 8 + half * 4, 4)
            add(near_ref.at[x, 4], i, beyond + place)
            for k in range(1, 4):
                add(far_ref.at[x, k - 1], i, beyond + jnp.bitwise_xor(place, k))
    for copy in copies:
        copy.start()
    for copy in copies:
        copy.wait()


def weight_kernel(source_ref, gain_ref, w_ref, out_ref):
    width = 1280
    move = (iota((width, width), 0) == source_ref[...]).astype(jnp.bfloat16)
    for x in range(4):
        part = w_ref[:, x * width : (x + 1) * width].astype(jnp.float32)
        part = (part * gain_ref[:, x * width : (x + 1) * width]).astype(jnp.bfloat16)
        moved = jnp.dot(part, move, preferred_element_type=jnp.float32).astype(jnp.bfloat16)
        for c in range(2):
            out_ref[:, (c * 4 + x) * 640 : (c * 4 + x + 1) * 640] = moved[:, c * 640 : (c + 1) * 640]


def attend(own_ref, other_ref, core, q, low, high, first, last, bufs):
    columns = q.shape[0]
    half = GROUP * SLAB
    row = iota((2 * half, 1), 0)
    inside = jnp.where(row < half, row, row - half)
    key0 = (inside // SLAB) * (2 * SLAB) + inside % SLAB + jnp.where(row < half, core, 1 - core) * SLAB
    turned = q.T

    def rows(g, at):
        chips = pl.ds(pl.multiple_of(jnp.minimum(g * GROUP, CHIPS - GROUP), GROUP), GROUP)
        parts = [ref[chips, at : at + SLAB, :].reshape(half, HEAD_DIM) for ref in (own_ref, other_ref)]
        return jnp.concatenate(parts, axis=0)

    def scores(g):
        return jnp.dot(rows(g, 0), turned, preferred_element_type=jnp.float32)

    def soften(g, buf, carry):
        top, total, acc = carry
        offset = g * (2 * half)
        s = jnp.where((key0 >= low - offset) & (key0 <= high - offset), buf[...] * SCALE2, masked_fill)
        new_top = jnp.maximum(top, jnp.max(s, axis=0, keepdims=True))
        p = jnp.exp2(s - new_top)
        keep = jnp.exp2(top - new_top)
        total = total * keep + jnp.sum(p, axis=0, keepdims=True)
        pv = lax.dot_general(rows(g, SLAB), p.astype(jnp.bfloat16), TN, preferred_element_type=jnp.float32)
        return new_top, total, acc * keep + pv

    begin = first // GROUP
    steps = (last // GROUP + 2 - begin) // 2

    def step(i, carry):
        g = begin + 2 * i
        bufs[1][...] = scores(g + 1)
        carry = soften(g, bufs[0], carry)
        bufs[0][...] = scores(g + 2)
        return soften(g + 1, bufs[1], carry)

    bufs[0][...] = scores(begin)
    start = (
        jnp.full((1, columns), start_max, jnp.float32),
        jnp.zeros((1, columns), jnp.float32),
        jnp.zeros((HEAD_DIM, columns), jnp.float32),
    )
    _, total, acc = lax.fori_loop(0, steps, step, start)
    return acc / total


def scored_kernel(core_ref, first_ref, low_ref, high_ref, near, far, near_other, far_other, w_ref, *refs):
    out_ref, rows, scored, held, sems = refs[-7:-2]
    core = core_ref[0]
    collect(core_ref[1], core_ref[2], ((near, far), (near_other, far_other)), held, sems)
    own_ref, other_ref = held.at[0], held.at[1]
    for t in range(8):
        q = jnp.concatenate(
            (
                own_ref[4 * t : 4 * t + 4, 2 * SLAB :, :].reshape(128, HEAD_DIM),
                other_ref[4 * t : 4 * t + 4, 2 * SLAB :, :].reshape(128, HEAD_DIM),
            ),
            axis=0,
        )
        mixed = attend(
            own_ref,
            other_ref,
            core,
            q,
            low_ref[t : t + 1, :],
            high_ref[t : t + 1, :],
            first_ref[t],
            4 * t + 3,
            refs[-2:],
        )
        rows[...] = mixed.T
        for h in range(HEADS_DEV):
            part = rows[pl.ds(h, 32, stride=HEADS_DEV), :].astype(jnp.bfloat16)
            lanes = slice(h * 128, (h + 1) * 128)
            scored[pl.ds(pl.multiple_of(core * 128 + t * 16, 16), 16), lanes] = part[:16]
            scored[pl.ds(pl.multiple_of((1 - core) * 128 + t * 16, 16), 16), lanes] = part[16:]
    partial = lax.dot_general(w_ref[...], scored[...], NT, preferred_element_type=jnp.float32)
    for half in range(2):
        for feats in range(2):
            out_ref[half * 2 + feats] = partial[
                feats * HALF : (feats + 1) * HALF, half * 128 : (half + 1) * 128
            ]


def context_kernel(start_head, at_ref, low_ref, high_ref, near, far, near_other, far_other, q_ref, *refs):
    out_ref, held, sems = refs[-5:-2]
    collect(at_ref[3], at_ref[4], ((near, far), (near_other, far_other)), held, sems)
    own_ref, other_ref = held.at[0], held.at[1]
    heads = range(start_head, start_head + 4)
    q = jnp.concatenate([q_ref[:, h * 128 : (h + 1) * 128] for h in heads], axis=0)
    low, high = jnp.tile(low_ref[...], (1, 4)), jnp.tile(high_ref[...], (1, 4))
    mixed = attend(own_ref, other_ref, at_ref[0], q, low, high, at_ref[1], at_ref[2], refs[-2:])
    for i in range(4):
        out_ref[:, i * 128 : (i + 1) * 128] = mixed[:, i * 128 : (i + 1) * 128].T.astype(jnp.bfloat16)


def add_kernel(parts_ref, residual_ref, out_ref, block, sems):
    total = residual_ref[...]
    for i in range(parts_ref.shape[0]):
        total = total + parts_ref[i]
    block[...] = total.astype(jnp.bfloat16)
    send_copies(block, out_ref, sems)


def hidden_kernel(parts_ref, dep_ref, out_ref):
    total = parts_ref[:8].astype(jnp.float32) + parts_ref[8:].astype(jnp.float32)
    total = total.reshape(8 * HALF, 128).astype(jnp.bfloat16)
    for i in range(out_ref.shape[0]):
        out_ref[i] = total


def add_logits(core, hidden_ref, w_ref, half):
    total = jnp.zeros((256, 128), jnp.float32)
    square = jnp.zeros((8, 128), jnp.float32)
    for x in range(4):
        part = hidden_ref[x, half]
        lanes = pl.ds(pl.multiple_of((core * 4 + x) * 640, 128), 640)
        total = total + jnp.dot(w_ref[:, lanes], part, preferred_element_type=jnp.float32)
        wide = part.astype(jnp.float32)
        square = square + jnp.sum((wide * wide).reshape(80, 8, 128), axis=0)
    return total, square


def own_logits_kernel(at_ref, own_ref, w_ref, out_ref, square_ref):
    for half in range(2):
        out_ref[half], square_ref[half] = add_logits(at_ref[0], own_ref, w_ref, half)


def logits_kernel(at_ref, ids_ref, sum_ref, square_ref, other_ref, w_ref, dep_ref, out_ref):
    core, base = at_ref[0], at_ref[1]
    tops, targets = [], []
    for half in range(2):
        total, square = add_logits(1 - core, other_ref, w_ref, half)
        total, square = total + sum_ref[half], square + square_ref[half]
        mean = jnp.sum(square, axis=0, keepdims=True) * (1.0 / D)
        total = total * lax.rsqrt(mean + norm_eps)
        top = jnp.max(total, axis=0, keepdims=True)
        tops.append(top + jnp.log(jnp.sum(jnp.exp(total - top), axis=0, keepdims=True)))
        hit = iota((256, 128), 0) + base == ids_ref[half : half + 1, :]
        targets.append(jnp.sum(jnp.where(hit, total, 0.0), axis=0, keepdims=True))
    tile = jnp.concatenate(tops + targets + [jnp.zeros((4, 128), jnp.float32)], axis=0)
    for i in range(out_ref.shape[0]):
        out_ref[i] = tile


def merge(parts_ref):
    parts = parts_ref[...]
    top = jnp.max(parts, axis=0)
    lse = top + jnp.log(jnp.sum(jnp.exp(parts - top[None]), axis=0))
    return jnp.where(iota((8, 128), 0) < 2, lse, jnp.sum(parts, axis=0))


def merge_kernel(parts_ref, out_ref):
    tile = merge(parts_ref)
    for i in range(out_ref.shape[0]):
        out_ref[i] = tile


def final_kernel(at_ref, rank_ref, parts_ref, out_ref):
    core, chip = at_ref[0], at_ref[1]
    tile = merge(parts_ref)
    logprob = jnp.where(core == 0, tile[2:3] - tile[0:1], tile[3:4] - tile[1:2])
    lane = iota((1, 128), 1)
    result = jnp.zeros((1, 128), jnp.float32)
    for k in range(SCORED):
        value = jnp.sum(jnp.where(lane == chip * SCORED + k, logprob, 0.0), axis=1, keepdims=True)
        result = jnp.where(rank_ref[...] == k, value, result)
    out_ref[...] = result


def call(kernel, shape, dtype, specs, scratch=(), flops=0, size=0, name=None, out=VMEM, more=None, vmem=16):
    shapes = jax.ShapeDtypeStruct(shape, dtype)
    return pl.pallas_call(
        kernel,
        out_shape=shapes if more is None else (shapes, more),
        in_specs=specs,
        out_specs=out if more is None else (out, out),
        scratch_shapes=list(scratch),
        compiler_params=pltpu.CompilerParams(vmem_limit_bytes=int(vmem * 2**20)),
        cost_estimate=pl.CostEstimate(flops=flops, bytes_accessed=size, transcendentals=0),
        name=name,
    )


def source_columns():
    c, yf, z, k = np.meshgrid(np.arange(2), np.arange(2), np.arange(8), np.arange(40), indexing="ij")
    return (((z * 2 + c) * 2 + yf) * 40 + k).reshape(1, 1280).astype(np.int32)


def body(
    queries,
    keys,
    values,
    out_weight,
    residual,
    norm_gain,
    head_weight,
    sampled_ids,
    loss_mask,
    doc_lengths,
):
    x, z, core = lax.axis_index("x"), lax.axis_index(("zh", "zl")), lax.axis_index("c")
    h, y = lax.axis_index("h"), lax.axis_index("y")
    chip = x * 8 + z
    slab = chip * 2 + core
    slabs = loss_mask.reshape(64, SLAB)
    upto = jnp.tril(jnp.ones((SLAB, SLAB), jnp.float32)).T
    rank = jnp.dot(slabs.astype(jnp.float32), upto, preferred_element_type=jnp.float32).astype(jnp.int32)
    rank = jnp.where(slabs == 1, rank - 1, -1)
    own_rank = lax.dynamic_slice_in_dim(rank, slab, 1, 0)
    block, packed = call(
        pack_kernel,
        (BLOCK, 128),
        jnp.bfloat16,
        [SMEM, VMEM, HBM, HBM, HBM],
        [
            pltpu.VMEM((BLOCK, 128), jnp.bfloat16),
            pltpu.VMEM((SLAB, 1024), jnp.bfloat16),
            pltpu.VMEM((32, 128), jnp.float32),
            pltpu.SemaphoreType.DMA((5,)),
        ],
        name="pack",
        out=ANY,
        vmem=63.9,
        more=jax.ShapeDtypeStruct((4, BLOCK, 128), jnp.bfloat16),
    )(slab[None], slabs, queries, keys, values)
    block = lax.ppermute(block, ("zh", "zl"), [(i, i ^ 4) for i in range(8)])
    near = lax.all_to_all(packed, "zl", 0, 0)

    def spread(name, *parts):
        count = sum(part.shape[0] if part.ndim == 3 else 1 for part in parts)
        return call(
            spread_kernel,
            (4, count, BLOCK, 128),
            jnp.bfloat16,
            [VMEM] * len(parts),
            [pltpu.SemaphoreType.DMA((4 * len(parts),))],
            name=name,
            out=ANY,
        )(*parts)

    bounds = jnp.cumsum(doc_lengths)
    position = jnp.arange(64 * SLAB, dtype=jnp.int32)
    begin = jnp.max(jnp.where(bounds[None, :] <= position[:, None], bounds[None, :], 0), axis=1)
    chosen = rank[:, None, :] == jnp.arange(SCORED, dtype=jnp.int32)[None, :, None]

    def pick(values_of):
        return jnp.sum(jnp.where(chosen, values_of.reshape(64, 1, SLAB), 0), axis=2)

    def columns(of_scored):
        pairs = of_scored.reshape(CHIPS, 2, SCORED)
        pairs = jnp.where(core == 0, pairs, pairs[:, ::-1])
        tiles = pairs.reshape(8, 4, 2, SCORED).transpose(0, 2, 1, 3)
        return jnp.repeat(tiles.reshape(8, 32), HEADS_DEV, axis=1)

    high = columns(pick(position))
    low = columns(pick(begin))
    ids = pick(sampled_ids).reshape(CHIPS, 2, SCORED).transpose(1, 0, 2).reshape(2, 128)
    first = jnp.min(low, axis=1) // 256
    half = lax.axis_index("zh")
    place = lax.axis_index("zl")
    core_at = jnp.stack((core, half, place))

    mine = residual.reshape(2, HALF, CHIPS, 2, SCORED).transpose(3, 0, 1, 2, 4).reshape(4, HALF, 128)
    mine = lax.dynamic_index_in_dim(mine, y, 0, keepdims=False).astype(jnp.float32)
    mine = jnp.where(h == 0, mine, 0.0)

    own_begin = lax.dynamic_slice_in_dim(begin, slab * SLAB, SLAB, 0)
    own_position = slab * SLAB + jnp.arange(SLAB, dtype=jnp.int32)
    at = jnp.stack((core, own_begin[0] // 256, chip, half, place))
    base = ((slab * 2 + h) * 4 + y) * 256

    near, low, high, first, ids, own_begin = lax.optimization_barrier((near, low, high, first, ids, own_begin))
    near = lax.all_to_all(spread("spread_near", near, block), "x", 0, 0)
    blocks = [lax.ppermute(block, "zl", [(i, i ^ k) for i in range(4)]) for k in (1, 2, 3)]
    near, far = lax.optimization_barrier((near, spread("spread_far", *blocks)))
    far = lax.all_to_all(far, "x", 0, 0)
    source = jnp.asarray(source_columns())
    weight = call(
        weight_kernel, (256, D), jnp.bfloat16, [VMEM] * 3, flops=2 * 256 * D * 1280, name="weight", vmem=28
    )(source, norm_gain[None, :], head_weight)
    near_other = lax.ppermute(near, "c", [(0, 1), (1, 0)])

    far, weight, mine = lax.optimization_barrier((far, weight, mine))
    far_other = lax.ppermute(far, "c", [(0, 1), (1, 0)])
    blocks = (near, far, near_other, far_other)
    held = [pltpu.VMEM((2, CHIPS, BLOCK, 128), jnp.bfloat16), pltpu.SemaphoreType.DMA((40,))]
    scores = pltpu.VMEM((2 * GROUP * SLAB, 256), jnp.float32)
    parts = call(
        scored_kernel,
        (4, HALF, 128),
        jnp.float32,
        [SMEM, SMEM, VMEM, VMEM] + [ANY] * 4 + [VMEM],
        [pltpu.VMEM((256, 128), jnp.float32), pltpu.VMEM((256, 1024), jnp.bfloat16)] + held + [scores, scores],
        name="scored",
        vmem=28,
    )(core_at, first, low, high, *blocks, out_weight)

    def context_of(start_head, after):
        return call(
            functools.partial(context_kernel, start_head),
            (SLAB, 512),
            jnp.bfloat16,
            [SMEM, VMEM, VMEM] + [ANY] * 4 + [VMEM, ANY],
            held + [pltpu.VMEM((2 * GROUP * SLAB, 512), jnp.float32)] * 2,
            flops=4 * 1024 * 4224 * 128,
            size=6 * 2**20,
            name="context",
            vmem=28,
        )(at, own_begin[None, :], own_position[None, :], *blocks, queries, after)

    parts = lax.all_to_all(parts, "y", 0, 0)
    block = pltpu.VMEM((HALF, 128), jnp.bfloat16)
    sums = call(
        add_kernel,
        (16, HALF, 128),
        jnp.bfloat16,
        [VMEM] * 2,
        [block, pltpu.SemaphoreType.DMA((16,))],
        name="add",
        out=HBM,
    )(parts, mine)
    context_a = context_of(0, sums)
    sums = lax.all_to_all(sums, ("h", "zh", "zl"), 0, 0)
    hidden = call(hidden_kernel, (16, 8 * HALF, 128), jnp.bfloat16, [VMEM, ANY], name="hidden")(sums, context_a)
    context_b = context_of(4, hidden)
    hidden = lax.all_to_all(hidden, ("x", "y"), 0, 0).reshape(4, 2, 640, 128)
    hidden, context_b = lax.optimization_barrier((hidden, context_b))
    hidden_other = lax.ppermute(hidden, "c", [(0, 1), (1, 0)])
    at_logits = jnp.stack((core, base))
    shares, squares = call(
        own_logits_kernel,
        (2, 256, 128),
        jnp.float32,
        [SMEM] + [VMEM] * 2,
        name="own_logits",
        more=jax.ShapeDtypeStruct((2, 8, 128), jnp.float32),
    )(at_logits, hidden, weight)
    tiles = call(logits_kernel, (32, 8, 128), jnp.float32, [SMEM] + [VMEM] * 5 + [ANY], name="logits")(
        at_logits, ids, shares, squares, hidden_other, weight, context_b
    )
    context = jnp.concatenate((context_a, context_b), axis=1)
    tiles = lax.all_to_all(tiles, ("x", "y", "c"), 0, 0)
    tiles = call(merge_kernel, (16, 8, 128), jnp.float32, [VMEM], name="merge")(tiles)
    tiles = lax.all_to_all(tiles, ("h", "zh", "zl"), 0, 0)
    logprob = call(final_kernel, (1, 128), jnp.float32, [SMEM, VMEM, VMEM], name="final")(
        jnp.stack((core, chip)), own_rank, tiles
    )
    return context, logprob.reshape(128)


def solution(mesh):
    fine = Mesh(mesh.devices.reshape(4, 2, 4, 2, 2, 4), ("x", "zh", "zl", "c", "h", "y"))
    ctx, tp = ("x", "zh", "zl", "c"), ("h", "y")
    placed = (
        P(ctx, tp),
        P(ctx, tp),
        P(ctx, tp),
        P(ctx, tp),
        P(ctx, None),
        P(),
        P(ctx + tp, None),
        P(),
        P(),
        P(),
    )
    return jax.shard_map(
        body, mesh=fine, in_specs=placed, out_specs=(P(ctx, tp), P(ctx)), check_vma=False
    )
```

```python
import functools
import math

import jax
import jax.numpy as jnp
import numpy as np
from jax import lax
from jax.experimental import pallas as pl
from jax.experimental.pallas import tpu as pltpu
from jax.sharding import Mesh
from jax.sharding import PartitionSpec as P

HEAD_DIM = 128
SCORED = 4
HEADS_DEV = 8
SLAB = 128
GROUP = 2
CHIPS = 32
BLOCK = 2 * SLAB + SCORED * HEADS_DEV
FEATS = 80
HALF = 40
D = 5120

masked_fill = -1e30
start_max = -5e29
norm_eps = 1e-06
LOG2E = 1.4426950408889634
SCALE2 = LOG2E / math.sqrt(HEAD_DIM)
NT = (((1,), (1,)), ((), ()))
TN = (((0,), (0,)), ((), ()))
SMEM = pl.BlockSpec(memory_space=pltpu.SMEM)
VMEM = pl.BlockSpec(memory_space=pltpu.VMEM)
ANY = pl.BlockSpec(memory_space=pl.ANY)
HBM = pl.BlockSpec(memory_space=pltpu.HBM)


def iota(shape, axis):
    return lax.broadcasted_iota(jnp.int32, shape, axis)


def send_copies(source, out_ref, sems):
    copies = [pltpu.make_async_copy(source, out_ref.at[i], sems.at[i]) for i in range(out_ref.shape[0])]
    for copy in copies:
        copy.start()
    for copy in copies:
        copy.wait()


def pack_kernel(at_ref, mask_ref, q_ref, k_ref, v_ref, block_ref, out_ref, block, queries, rows, sems):
    copies = [
        pltpu.make_async_copy(k_ref, block.at[pl.ds(0, SLAB)], sems.at[0]),
        pltpu.make_async_copy(v_ref, block.at[pl.ds(SLAB, SLAB)], sems.at[1]),
        pltpu.make_async_copy(q_ref, queries, sems.at[2]),
    ]
    for copy in copies:
        copy.start()
    mask = mask_ref[pl.ds(at_ref[0], 1), :]
    upto = (iota((SLAB, SLAB), 0) <= iota((SLAB, SLAB), 1)).astype(jnp.bfloat16)
    ones = jnp.broadcast_to(mask.astype(jnp.float32), (8, SLAB)).astype(jnp.bfloat16)
    rank = jnp.dot(ones, upto, preferred_element_type=jnp.float32).astype(jnp.int32) - 1
    chosen = jnp.where((iota((8, SLAB), 0) == rank) & (mask == 1), 1.0, 0.0).astype(jnp.bfloat16)
    for copy in copies:
        copy.wait()
    picked = jnp.dot(chosen, queries[...], preferred_element_type=jnp.float32)
    for h in range(HEADS_DEV):
        rows[pl.ds(h, SCORED, stride=HEADS_DEV), :] = picked[:SCORED, h * 128 : (h + 1) * 128]
    block[2 * SLAB :, :] = rows[...].astype(jnp.bfloat16)
    single = pltpu.make_async_copy(block, block_ref, sems.at[4])
    single.start()
    send_copies(block, out_ref, sems)
    single.wait()


def spread_kernel(*refs):
    out_ref, sems = refs[-2:]
    copies = []
    for i in range(4):
        at = 0
        for ref in refs[:-2]:
            count = ref.shape[0] if len(ref.shape) == 3 else 1
            target = out_ref.at[i, pl.ds(at, count)] if len(ref.shape) == 3 else out_ref.at[i, at]
            copies.append(pltpu.make_async_copy(ref, target, sems.at[len(copies)]))
            at += count
    for copy in copies:
        copy.start()
    for copy in copies:
        copy.wait()


def collect(near_far, held, sems):
    copies = []
    for i, (near_ref, far_ref) in enumerate(near_far):
        for x in range(4):
            for ref, at, count in ((near_ref, 8 * x, 5), (far_ref, 8 * x + 5, 3)):
                target = held.at[i, pl.ds(at, count)]
                copies.append(pltpu.make_async_copy(ref.at[x], target, sems.at[len(copies)]))
    for copy in copies:
        copy.start()
    for copy in copies:
        copy.wait()


def held_at(half, place, t, j):
    far = jnp.bitwise_xor(place, j) + 4
    return t // 2 * 8 + jnp.where(half == t % 2, j, far)


def weight_kernel(source_ref, gain_ref, w_ref, out_ref):
    width = 1280
    move = (iota((width, width), 0) == source_ref[...]).astype(jnp.bfloat16)
    for x in range(4):
        part = w_ref[:, x * width : (x + 1) * width].astype(jnp.float32)
        part = (part * gain_ref[:, x * width : (x + 1) * width]).astype(jnp.bfloat16)
        moved = jnp.dot(part, move, preferred_element_type=jnp.float32).astype(jnp.bfloat16)
        for c in range(2):
            out_ref[:, (c * 4 + x) * 640 : (c * 4 + x + 1) * 640] = moved[:, c * 640 : (c + 1) * 640]


def attend(held, core, half, place, q, low, high, first, last, bufs):
    columns = q.shape[0]
    count = GROUP * SLAB
    row = iota((2 * count, 1), 0)
    inside = jnp.where(row < count, row, row - count)
    key0 = (inside // SLAB) * (2 * SLAB) + inside % SLAB + jnp.where(row < count, core, 1 - core) * SLAB

    turned = q.T

    def far(g):
        return (g // 2) % 2 != half

    def rows(g, at):
        g = jnp.minimum(g, CHIPS // GROUP - 1)
        pair = jnp.where(far(g), 2 + jnp.bitwise_xor(g % 2, place // 2), g % 2)
        chips = pl.ds(pl.multiple_of((g // 4 * 4 + pair) * GROUP, GROUP), GROUP)
        parts = [held[i, chips, at : at + SLAB, :].reshape(count, HEAD_DIM) for i in range(2)]
        return jnp.concatenate(parts, axis=0)

    def scores(g):
        return jnp.dot(rows(g, 0), turned, preferred_element_type=jnp.float32)

    def soften(g, buf, carry):
        top, total, acc = carry
        offset = g * (2 * count)
        turn = jnp.where(far(g) & (place % 2 == 1), 2 * SLAB, 0)
        key = jnp.bitwise_xor(key0, turn)
        s = jnp.where((key >= low - offset) & (key <= high - offset), buf[...] * SCALE2, masked_fill)
        new_top = jnp.maximum(top, jnp.max(s, axis=0, keepdims=True))
        p = jnp.exp2(s - new_top)
        keep = jnp.exp2(top - new_top)
        total = total * keep + jnp.sum(p, axis=0, keepdims=True)
        pv = lax.dot_general(rows(g, SLAB), p.astype(jnp.bfloat16), TN, preferred_element_type=jnp.float32)
        return new_top, total, acc * keep + pv

    begin = first // GROUP
    steps = (last // GROUP + 2 - begin) // 2

    def step(i, carry):
        g = begin + 2 * i
        bufs[1][...] = scores(g + 1)
        carry = soften(g, bufs[0], carry)
        bufs[0][...] = scores(g + 2)
        return soften(g + 1, bufs[1], carry)

    bufs[0][...] = scores(begin)
    start = (
        jnp.full((1, columns), start_max, jnp.float32),
        jnp.zeros((1, columns), jnp.float32),
        jnp.zeros((HEAD_DIM, columns), jnp.float32),
    )
    _, total, acc = lax.fori_loop(0, steps, step, start)
    return acc / total


def scored_kernel(core_ref, first_ref, low_ref, high_ref, near, far, near_other, far_other, w_ref, *refs):
    out_ref, rows, scored, held, sems = refs[-7:-2]
    core = core_ref[0]
    half, place = core_ref[1], core_ref[2]
    collect(((near, far), (near_other, far_other)), held, sems)
    for t in range(8):
        q = jnp.concatenate(
            [held[i, held_at(half, place, t, j), 2 * SLAB :, :] for i in range(2) for j in range(4)], axis=0
        )
        mixed = attend(
            held,
            core,
            half,
            place,
            q,
            low_ref[t : t + 1, :],
            high_ref[t : t + 1, :],
            first_ref[t],
            4 * t + 3,
            refs[-2:],
        )
        rows[...] = mixed.T
        for h in range(HEADS_DEV):
            part = rows[pl.ds(h, 32, stride=HEADS_DEV), :].astype(jnp.bfloat16)
            lanes = slice(h * 128, (h + 1) * 128)
            scored[pl.ds(pl.multiple_of(core * 128 + t * 16, 16), 16), lanes] = part[:16]
            scored[pl.ds(pl.multiple_of((1 - core) * 128 + t * 16, 16), 16), lanes] = part[16:]
    partial = lax.dot_general(w_ref[...], scored[...], NT, preferred_element_type=jnp.float32)
    for half in range(2):
        for feats in range(2):
            out_ref[half * 2 + feats] = partial[
                feats * HALF : (feats + 1) * HALF, half * 128 : (half + 1) * 128
            ]


def context_kernel(start_head, at_ref, low_ref, high_ref, near, far, near_other, far_other, q_ref, *refs):
    out_ref, token_ref, held, sems = refs[-6:-2]
    token_ref[...] = jnp.zeros_like(token_ref)
    collect(((near, far), (near_other, far_other)), held, sems)
    heads = range(start_head, start_head + 4)
    q = jnp.concatenate([q_ref[:, h * 128 : (h + 1) * 128] for h in heads], axis=0)
    low, high = jnp.tile(low_ref[...], (1, 4)), jnp.tile(high_ref[...], (1, 4))
    mixed = attend(held, at_ref[0], at_ref[3], at_ref[4], q, low, high, at_ref[1], at_ref[2], refs[-2:])
    for i in range(4):
        out_ref[:, i * 128 : (i + 1) * 128] = mixed[:, i * 128 : (i + 1) * 128].T.astype(jnp.bfloat16)


def add_kernel(parts_ref, residual_ref, out_ref, token_ref, block, sems):
    token_ref[...] = jnp.zeros_like(token_ref)
    total = residual_ref[...]
    for i in range(parts_ref.shape[0]):
        total = total + parts_ref[i]
    block[...] = total.astype(jnp.bfloat16)
    send_copies(block, out_ref, sems)


def hidden_kernel(parts_ref, dep_ref, out_ref, token_ref):
    token_ref[...] = jnp.zeros_like(token_ref)
    total = parts_ref[:8].astype(jnp.float32) + parts_ref[8:].astype(jnp.float32)
    total = total.reshape(8 * HALF, 128).astype(jnp.bfloat16)
    for i in range(out_ref.shape[0]):
        out_ref[i] = total


def add_logits(core, hidden_ref, w_ref, half):
    total = jnp.zeros((256, 128), jnp.float32)
    square = jnp.zeros((8, 128), jnp.float32)
    for x in range(4):
        part = hidden_ref[x, half]
        lanes = pl.ds(pl.multiple_of((core * 4 + x) * 640, 128), 640)
        total = total + jnp.dot(w_ref[:, lanes], part, preferred_element_type=jnp.float32)
        wide = part.astype(jnp.float32)
        square = square + jnp.sum((wide * wide).reshape(80, 8, 128), axis=0)
    return total, square


def own_logits_kernel(at_ref, own_ref, w_ref, out_ref, square_ref):
    for half in range(2):
        out_ref[half], square_ref[half] = add_logits(at_ref[0], own_ref, w_ref, half)


def logits_kernel(at_ref, ids_ref, sum_ref, square_ref, other_ref, w_ref, dep_ref, out_ref):
    core, base = at_ref[0], at_ref[1]
    tops, targets = [], []
    for half in range(2):
        total, square = add_logits(1 - core, other_ref, w_ref, half)
        total, square = total + sum_ref[half], square + square_ref[half]
        mean = jnp.sum(square, axis=0, keepdims=True) * (1.0 / D)
        total = total * lax.rsqrt(mean + norm_eps)
        top = jnp.max(total, axis=0, keepdims=True)
        tops.append(top + jnp.log(jnp.sum(jnp.exp(total - top), axis=0, keepdims=True)))
        hit = iota((256, 128), 0) + base == ids_ref[half : half + 1, :]
        targets.append(jnp.sum(jnp.where(hit, total, 0.0), axis=0, keepdims=True))
    tile = jnp.concatenate(tops + targets + [jnp.zeros((4, 128), jnp.float32)], axis=0)
    for i in range(out_ref.shape[0]):
        out_ref[i] = tile


def merge(parts_ref):
    parts = parts_ref[...]
    top = jnp.max(parts, axis=0)
    lse = top + jnp.log(jnp.sum(jnp.exp(parts - top[None]), axis=0))
    return jnp.where(iota((8, 128), 0) < 2, lse, jnp.sum(parts, axis=0))


def merge_kernel(parts_ref, out_ref):
    tile = merge(parts_ref)
    for i in range(out_ref.shape[0]):
        out_ref[i] = tile


def final_kernel(at_ref, rank_ref, parts_ref, out_ref):
    core, chip = at_ref[0], at_ref[1]
    tile = merge(parts_ref)
    logprob = jnp.where(core == 0, tile[2:3] - tile[0:1], tile[3:4] - tile[1:2])
    lane = iota((1, 128), 1)
    result = jnp.zeros((1, 128), jnp.float32)
    for k in range(SCORED):
        value = jnp.sum(jnp.where(lane == chip * SCORED + k, logprob, 0.0), axis=1, keepdims=True)
        result = jnp.where(rank_ref[...] == k, value, result)
    out_ref[...] = result


def call(kernel, shape, dtype, specs, scratch=(), flops=0, size=0, name=None, out=VMEM, more=None, more_out=VMEM, vmem=16):
    shapes = jax.ShapeDtypeStruct(shape, dtype)
    return pl.pallas_call(
        kernel,
        out_shape=shapes if more is None else (shapes, more),
        in_specs=specs,
        out_specs=out if more is None else (out, more_out),
        scratch_shapes=list(scratch),
        compiler_params=pltpu.CompilerParams(vmem_limit_bytes=int(vmem * 2**20)),
        cost_estimate=pl.CostEstimate(flops=flops, bytes_accessed=size, transcendentals=0),
        name=name,
    )


def source_columns():
    c, yf, z, k = np.meshgrid(np.arange(2), np.arange(2), np.arange(8), np.arange(40), indexing="ij")
    return (((z * 2 + c) * 2 + yf) * 40 + k).reshape(1, 1280).astype(np.int32)


def body(
    queries,
    keys,
    values,
    out_weight,
    residual,
    norm_gain,
    head_weight,
    sampled_ids,
    loss_mask,
    doc_lengths,
):
    x, z, core = lax.axis_index("x"), lax.axis_index(("zh", "zl")), lax.axis_index("c")
    h, y = lax.axis_index("h"), lax.axis_index("y")
    chip = x * 8 + z
    slab = chip * 2 + core
    slabs = loss_mask.reshape(64, SLAB)
    upto = jnp.tril(jnp.ones((SLAB, SLAB), jnp.float32)).T
    rank = jnp.dot(slabs.astype(jnp.float32), upto, preferred_element_type=jnp.float32).astype(jnp.int32)
    rank = jnp.where(slabs == 1, rank - 1, -1)
    own_rank = lax.dynamic_slice_in_dim(rank, slab, 1, 0)
    block, packed = call(
        pack_kernel,
        (BLOCK, 128),
        jnp.bfloat16,
        [SMEM, VMEM, HBM, HBM, HBM],
        [
            pltpu.VMEM((BLOCK, 128), jnp.bfloat16),
            pltpu.VMEM((SLAB, 1024), jnp.bfloat16),
            pltpu.VMEM((32, 128), jnp.float32),
            pltpu.SemaphoreType.DMA((5,)),
        ],
        name="pack",
        out=ANY,
        more_out=ANY,
        vmem=63.9,
        more=jax.ShapeDtypeStruct((4, BLOCK, 128), jnp.bfloat16),
    )(slab[None], slabs, queries, keys, values)
    block = lax.ppermute(block, ("zh", "zl"), [(i, i ^ 4) for i in range(8)])
    near = lax.all_to_all(packed, "zl", 0, 0)

    def spread(name, *parts):
        count = sum(part.shape[0] if part.ndim == 3 else 1 for part in parts)
        return call(
            spread_kernel,
            (4, count, BLOCK, 128),
            jnp.bfloat16,
            [VMEM] * len(parts),
            [pltpu.SemaphoreType.DMA((4 * len(parts),))],
            name=name,
            out=ANY,
        )(*parts)

    bounds = jnp.cumsum(doc_lengths)
    position = jnp.arange(64 * SLAB, dtype=jnp.int32)
    begin = jnp.max(jnp.where(bounds[None, :] <= position[:, None], bounds[None, :], 0), axis=1)
    chosen = rank[:, None, :] == jnp.arange(SCORED, dtype=jnp.int32)[None, :, None]

    def pick(values_of):
        return jnp.sum(jnp.where(chosen, values_of.reshape(64, 1, SLAB), 0), axis=2)

    def columns(of_scored):
        pairs = of_scored.reshape(CHIPS, 2, SCORED)
        pairs = jnp.where(core == 0, pairs, pairs[:, ::-1])
        tiles = pairs.reshape(8, 4, 2, SCORED).transpose(0, 2, 1, 3)
        return jnp.repeat(tiles.reshape(8, 32), HEADS_DEV, axis=1)

    high = columns(pick(position))
    low = columns(pick(begin))
    ids = pick(sampled_ids).reshape(CHIPS, 2, SCORED).transpose(1, 0, 2).reshape(2, 128)
    first = jnp.min(low, axis=1) // 256
    half = lax.axis_index("zh")
    place = lax.axis_index("zl")
    core_at = jnp.stack((core, half, place))

    mine = residual.reshape(2, HALF, CHIPS, 2, SCORED).transpose(3, 0, 1, 2, 4).reshape(4, HALF, 128)
    mine = lax.dynamic_index_in_dim(mine, y, 0, keepdims=False).astype(jnp.float32)
    mine = jnp.where(h == 0, mine, 0.0)

    own_begin = lax.dynamic_slice_in_dim(begin, slab * SLAB, SLAB, 0)
    own_position = slab * SLAB + jnp.arange(SLAB, dtype=jnp.int32)
    at = jnp.stack((core, own_begin[0] // 256, chip, half, place))
    base = ((slab * 2 + h) * 4 + y) * 256

    near, low, high, first, ids, own_begin = lax.optimization_barrier((near, low, high, first, ids, own_begin))
    near = lax.all_to_all(spread("spread_near", near, block), "x", 0, 0)
    blocks = [lax.ppermute(block, "zl", [(i, i ^ k) for i in range(4)]) for k in (1, 2, 3)]
    near, far = lax.optimization_barrier((near, spread("spread_far", *blocks)))
    far = lax.all_to_all(far, "x", 0, 0)
    source = jnp.asarray(source_columns())
    weight = call(
        weight_kernel, (256, D), jnp.bfloat16, [VMEM] * 3, flops=2 * 256 * D * 1280, name="weight", vmem=28
    )(source, norm_gain[None, :], head_weight)
    near_other = lax.ppermute(near, "c", [(0, 1), (1, 0)])

    far, weight, mine = lax.optimization_barrier((far, weight, mine))
    far_other = lax.ppermute(far, "c", [(0, 1), (1, 0)])
    blocks = (near, far, near_other, far_other)
    held = [pltpu.VMEM((2, CHIPS, BLOCK, 128), jnp.bfloat16), pltpu.SemaphoreType.DMA((16,))]
    scores = pltpu.VMEM((2 * GROUP * SLAB, 256), jnp.float32)
    parts = call(
        scored_kernel,
        (4, HALF, 128),
        jnp.float32,
        [SMEM, SMEM, VMEM, VMEM] + [ANY] * 4 + [VMEM],
        [pltpu.VMEM((256, 128), jnp.float32), pltpu.VMEM((256, 1024), jnp.bfloat16)] + held + [scores, scores],
        name="scored",
        vmem=28,
    )(core_at, first, low, high, *blocks, out_weight)

    token = jax.ShapeDtypeStruct((8, 128), jnp.float32)

    def context_of(start_head, after):
        return call(
            functools.partial(context_kernel, start_head),
            (SLAB, 512),
            jnp.bfloat16,
            [SMEM, VMEM, VMEM] + [ANY] * 4 + [VMEM, ANY],
            held + [pltpu.VMEM((2 * GROUP * SLAB, 512), jnp.float32)] * 2,
            flops=4 * 1024 * 4224 * 128,
            size=6 * 2**20,
            name="context",
            vmem=28,
            more=token,
        )(at, own_begin[None, :], own_position[None, :], *blocks, queries, after)

    parts = lax.all_to_all(parts, "y", 0, 0)
    block = pltpu.VMEM((HALF, 128), jnp.bfloat16)
    sums, after = call(
        add_kernel,
        (16, HALF, 128),
        jnp.bfloat16,
        [VMEM] * 2,
        [block, pltpu.SemaphoreType.DMA((16,))],
        name="add",
        out=HBM,
        more=token,
    )(parts, mine)
    context_a, done_a = context_of(0, after)
    sums = lax.all_to_all(sums, ("h", "zh", "zl"), 0, 0)
    hidden, after = call(hidden_kernel, (16, 8 * HALF, 128), jnp.bfloat16, [VMEM, ANY], name="hidden", more=token)(
        sums, done_a
    )
    context_b, done_b = context_of(4, after)
    hidden = lax.all_to_all(hidden, ("x", "y"), 0, 0).reshape(4, 2, 640, 128)
    hidden, done_b = lax.optimization_barrier((hidden, done_b))
    hidden_other = lax.ppermute(hidden, "c", [(0, 1), (1, 0)])
    at_logits = jnp.stack((core, base))
    shares, squares = call(
        own_logits_kernel,
        (2, 256, 128),
        jnp.float32,
        [SMEM] + [VMEM] * 2,
        name="own_logits",
        more=jax.ShapeDtypeStruct((2, 8, 128), jnp.float32),
    )(at_logits, hidden, weight)
    tiles = call(logits_kernel, (32, 8, 128), jnp.float32, [SMEM] + [VMEM] * 5 + [ANY], name="logits")(
        at_logits, ids, shares, squares, hidden_other, weight, done_b
    )
    context = jnp.concatenate((context_a, context_b), axis=1)
    tiles = lax.all_to_all(tiles, ("x", "y", "c"), 0, 0)
    tiles = call(merge_kernel, (16, 8, 128), jnp.float32, [VMEM], name="merge")(tiles)
    tiles = lax.all_to_all(tiles, ("h", "zh", "zl"), 0, 0)
    logprob = call(final_kernel, (1, 128), jnp.float32, [SMEM, VMEM, VMEM], name="final")(
        jnp.stack((core, chip)), own_rank, tiles
    )
    return context, logprob.reshape(128)


def solution(mesh):
    fine = Mesh(mesh.devices.reshape(4, 2, 4, 2, 2, 4), ("x", "zh", "zl", "c", "h", "y"))
    ctx, tp = ("x", "zh", "zl", "c"), ("h", "y")
    placed = (
        P(ctx, tp),
        P(ctx, tp),
        P(ctx, tp),
        P(ctx, tp),
        P(ctx, None),
        P(),
        P(ctx + tp, None),
        P(),
        P(),
        P(),
    )
    return jax.shard_map(
        body, mesh=fine, in_specs=placed, out_specs=(P(ctx, tp), P(ctx)), check_vma=False
    )
```

```python
import functools
import math

import jax
import jax.numpy as jnp
import numpy as np
from jax import lax
from jax.experimental import pallas as pl
from jax.experimental.pallas import tpu as pltpu
from jax.sharding import Mesh
from jax.sharding import PartitionSpec as P

HEAD_DIM = 128
SCORED = 4
HEADS_DEV = 8
SLAB = 128
GROUP = 2
CHIPS = 32
BLOCK = 2 * SLAB + SCORED * HEADS_DEV
FEATS = 80
HALF = 40
D = 5120

masked_fill = -1e30
start_max = -5e29
norm_eps = 1e-06
LOG2E = 1.4426950408889634
SCALE2 = LOG2E / math.sqrt(HEAD_DIM)
NT = (((1,), (1,)), ((), ()))
TN = (((0,), (0,)), ((), ()))
SMEM = pl.BlockSpec(memory_space=pltpu.SMEM)
VMEM = pl.BlockSpec(memory_space=pltpu.VMEM)
ANY = pl.BlockSpec(memory_space=pl.ANY)
HBM = pl.BlockSpec(memory_space=pltpu.HBM)


def iota(shape, axis):
    return lax.broadcasted_iota(jnp.int32, shape, axis)


def send_copies(source, out_ref, sems):
    copies = [pltpu.make_async_copy(source, out_ref.at[i], sems.at[i]) for i in range(out_ref.shape[0])]
    for copy in copies:
        copy.start()
    for copy in copies:
        copy.wait()


def pack_kernel(at_ref, mask_ref, q_ref, k_ref, v_ref, block_ref, out_ref, block, queries, rows, sems):
    copies = [
        pltpu.make_async_copy(k_ref, block.at[pl.ds(0, SLAB)], sems.at[0]),
        pltpu.make_async_copy(v_ref, block.at[pl.ds(SLAB, SLAB)], sems.at[1]),
        pltpu.make_async_copy(q_ref, queries, sems.at[2]),
    ]
    for copy in copies:
        copy.start()
    mask = mask_ref[pl.ds(at_ref[0], 1), :]
    upto = (iota((SLAB, SLAB), 0) <= iota((SLAB, SLAB), 1)).astype(jnp.bfloat16)
    ones = jnp.broadcast_to(mask.astype(jnp.float32), (8, SLAB)).astype(jnp.bfloat16)
    rank = jnp.dot(ones, upto, preferred_element_type=jnp.float32).astype(jnp.int32) - 1
    chosen = jnp.where((iota((8, SLAB), 0) == rank) & (mask == 1), 1.0, 0.0).astype(jnp.bfloat16)
    for copy in copies:
        copy.wait()
    picked = jnp.dot(chosen, queries[...], preferred_element_type=jnp.float32)
    for h in range(HEADS_DEV):
        rows[pl.ds(h, SCORED, stride=HEADS_DEV), :] = picked[:SCORED, h * 128 : (h + 1) * 128]
    block[2 * SLAB :, :] = rows[...].astype(jnp.bfloat16)
    single = pltpu.make_async_copy(block, block_ref, sems.at[4])
    single.start()
    send_copies(block, out_ref, sems)
    single.wait()


def spread_kernel(near_ref, out_ref, sems):
    send_copies(near_ref, out_ref, sems)


def spread_far_kernel(at_ref, *refs):
    out_ref, sems = refs[-2:]
    copies = []
    for i in range(4):
        for k in range(4):
            copies.append(
                pltpu.make_async_copy(refs[k], out_ref.at[i, jnp.bitwise_xor(at_ref[0], k)], sems.at[i * 4 + k])
            )
    for copy in copies:
        copy.start()
    for copy in copies:
        copy.wait()


def collect(half, near_far, held, sems):
    copies = []
    for i, (near_ref, far_ref) in enumerate(near_far):
        for x in range(4):
            for j, ref in enumerate((near_ref, far_ref)):
                at = x * 8 + (half * 4 if j == 0 else (1 - half) * 4)
                target = held.at[i, pl.ds(pl.multiple_of(at, 4), 4)]
                copies.append(pltpu.make_async_copy(ref.at[x], target, sems.at[i * 8 + x * 2 + j]))
    for copy in copies:
        copy.start()
    for copy in copies:
        copy.wait()


def weight_kernel(source_ref, gain_ref, w_ref, out_ref):
    width = 1280
    move = (iota((width, width), 0) == source_ref[...]).astype(jnp.bfloat16)
    for x in range(4):
        part = w_ref[:, x * width : (x + 1) * width].astype(jnp.float32)
        part = (part * gain_ref[:, x * width : (x + 1) * width]).astype(jnp.bfloat16)
        moved = jnp.dot(part, move, preferred_element_type=jnp.float32).astype(jnp.bfloat16)
        for c in range(2):
            out_ref[:, (c * 4 + x) * 640 : (c * 4 + x + 1) * 640] = moved[:, c * 640 : (c + 1) * 640]


def attend(own_ref, other_ref, core, q, low, high, first, last, bufs):
    columns = q.shape[0]
    half = GROUP * SLAB
    row = iota((2 * half, 1), 0)
    inside = jnp.where(row < half, row, row - half)
    key0 = (inside // SLAB) * (2 * SLAB) + inside % SLAB + jnp.where(row < half, core, 1 - core) * SLAB
    turned = q.T

    def rows(g, at):
        chips = pl.ds(pl.multiple_of(jnp.minimum(g * GROUP, CHIPS - GROUP), GROUP), GROUP)
        parts = [ref[chips, at : at + SLAB, :].reshape(half, HEAD_DIM) for ref in (own_ref, other_ref)]
        return jnp.concatenate(parts, axis=0)

    def scores(g):
        return jnp.dot(rows(g, 0), turned, preferred_element_type=jnp.float32)

    def soften(g, buf, carry):
        top, total, acc = carry
        offset = g * (2 * half)
        s = jnp.where((key0 >= low - offset) & (key0 <= high - offset), buf[...] * SCALE2, masked_fill)
        new_top = jnp.maximum(top, jnp.max(s, axis=0, keepdims=True))
        p = jnp.exp2(s - new_top)
        keep = jnp.exp2(top - new_top)
        total = total * keep + jnp.sum(p, axis=0, keepdims=True)
        pv = lax.dot_general(rows(g, SLAB), p.astype(jnp.bfloat16), TN, preferred_element_type=jnp.float32)
        return new_top, total, acc * keep + pv

    begin = first // GROUP
    steps = (last // GROUP + 2 - begin) // 2

    def step(i, carry):
        g = begin + 2 * i
        bufs[1][...] = scores(g + 1)
        carry = soften(g, bufs[0], carry)
        bufs[0][...] = scores(g + 2)
        return soften(g + 1, bufs[1], carry)

    bufs[0][...] = scores(begin)
    start = (
        jnp.full((1, columns), start_max, jnp.float32),
        jnp.zeros((1, columns), jnp.float32),
        jnp.zeros((HEAD_DIM, columns), jnp.float32),
    )
    _, total, acc = lax.fori_loop(0, steps, step, start)
    return acc / total


def scored_kernel(core_ref, first_ref, low_ref, high_ref, near, far, near_other, far_other, w_ref, *refs):
    out_ref, rows, scored, held, sems = refs[-7:-2]
    core = core_ref[0]
    collect(core_ref[1], ((near, far), (near_other, far_other)), held, sems)
    own_ref, other_ref = held.at[0], held.at[1]
    for t in range(8):
        q = jnp.concatenate(
            (
                own_ref[4 * t : 4 * t + 4, 2 * SLAB :, :].reshape(128, HEAD_DIM),
                other_ref[4 * t : 4 * t + 4, 2 * SLAB :, :].reshape(128, HEAD_DIM),
            ),
            axis=0,
        )
        mixed = attend(
            own_ref,
            other_ref,
            core,
            q,
            low_ref[t : t + 1, :],
            high_ref[t : t + 1, :],
            first_ref[t],
            4 * t + 3,
            refs[-2:],
        )
        rows[...] = mixed.T
        for h in range(HEADS_DEV):
            part = rows[pl.ds(h, 32, stride=HEADS_DEV), :].astype(jnp.bfloat16)
            lanes = slice(h * 128, (h + 1) * 128)
            scored[pl.ds(pl.multiple_of(core * 128 + t * 16, 16), 16), lanes] = part[:16]
            scored[pl.ds(pl.multiple_of((1 - core) * 128 + t * 16, 16), 16), lanes] = part[16:]
    partial = lax.dot_general(w_ref[...], scored[...], NT, preferred_element_type=jnp.float32)
    for half in range(2):
        for feats in range(2):
            out_ref[half * 2 + feats] = partial[
                feats * HALF : (feats + 1) * HALF, half * 128 : (half + 1) * 128
            ]


def context_kernel(start_head, at_ref, low_ref, high_ref, near, far, near_other, far_other, q_ref, *refs):
    out_ref, token_ref, held, sems = refs[-6:-2]
    token_ref[...] = jnp.zeros_like(token_ref)
    collect(at_ref[3], ((near, far), (near_other, far_other)), held, sems)
    own_ref, other_ref = held.at[0], held.at[1]
    heads = range(start_head, start_head + 4)
    q = jnp.concatenate([q_ref[:, h * 128 : (h + 1) * 128] for h in heads], axis=0)
    low, high = jnp.tile(low_ref[...], (1, 4)), jnp.tile(high_ref[...], (1, 4))
    mixed = attend(own_ref, other_ref, at_ref[0], q, low, high, at_ref[1], at_ref[2], refs[-2:])
    for i in range(4):
        out_ref[:, i * 128 : (i + 1) * 128] = mixed[:, i * 128 : (i + 1) * 128].T.astype(jnp.bfloat16)


def add_kernel(parts_ref, residual_ref, out_ref, token_ref, block, sems):
    token_ref[...] = jnp.zeros_like(token_ref)
    total = residual_ref[...]
    for i in range(parts_ref.shape[0]):
        total = total + parts_ref[i]
    block[...] = total.astype(jnp.bfloat16)
    send_copies(block, out_ref, sems)


def hidden_kernel(parts_ref, dep_ref, out_ref, token_ref):
    token_ref[...] = jnp.zeros_like(token_ref)
    total = parts_ref[:8].astype(jnp.float32) + parts_ref[8:].astype(jnp.float32)
    total = total.reshape(8 * HALF, 128).astype(jnp.bfloat16)
    for i in range(out_ref.shape[0]):
        out_ref[i] = total


def add_logits(core, hidden_ref, w_ref, half):
    total = jnp.zeros((256, 128), jnp.float32)
    square = jnp.zeros((8, 128), jnp.float32)
    for x in range(4):
        part = hidden_ref[x, half]
        lanes = pl.ds(pl.multiple_of((core * 4 + x) * 640, 128), 640)
        total = total + jnp.dot(w_ref[:, lanes], part, preferred_element_type=jnp.float32)
        wide = part.astype(jnp.float32)
        square = square + jnp.sum((wide * wide).reshape(80, 8, 128), axis=0)
    return total, square


def own_logits_kernel(at_ref, own_ref, w_ref, out_ref, square_ref):
    for half in range(2):
        out_ref[half], square_ref[half] = add_logits(at_ref[0], own_ref, w_ref, half)


def logits_kernel(at_ref, ids_ref, sum_ref, square_ref, other_ref, w_ref, dep_ref, out_ref):
    core, base = at_ref[0], at_ref[1]
    tops, targets = [], []
    for half in range(2):
        total, square = add_logits(1 - core, other_ref, w_ref, half)
        total, square = total + sum_ref[half], square + square_ref[half]
        mean = jnp.sum(square, axis=0, keepdims=True) * (1.0 / D)
        total = total * lax.rsqrt(mean + norm_eps)
        top = jnp.max(total, axis=0, keepdims=True)
        tops.append(top + jnp.log(jnp.sum(jnp.exp(total - top), axis=0, keepdims=True)))
        hit = iota((256, 128), 0) + base == ids_ref[half : half + 1, :]
        targets.append(jnp.sum(jnp.where(hit, total, 0.0), axis=0, keepdims=True))
    tile = jnp.concatenate(tops + targets + [jnp.zeros((4, 128), jnp.float32)], axis=0)
    for i in range(out_ref.shape[0]):
        out_ref[i] = tile


def merge(parts_ref):
    parts = parts_ref[...]
    top = jnp.max(parts, axis=0)
    lse = top + jnp.log(jnp.sum(jnp.exp(parts - top[None]), axis=0))
    return jnp.where(iota((8, 128), 0) < 2, lse, jnp.sum(parts, axis=0))


def merge_kernel(parts_ref, out_ref):
    tile = merge(parts_ref)
    for i in range(out_ref.shape[0]):
        out_ref[i] = tile


def final_kernel(at_ref, rank_ref, parts_ref, out_ref):
    core, chip = at_ref[0], at_ref[1]
    tile = merge(parts_ref)
    logprob = jnp.where(core == 0, tile[2:3] - tile[0:1], tile[3:4] - tile[1:2])
    lane = iota((1, 128), 1)
    result = jnp.zeros((1, 128), jnp.float32)
    for k in range(SCORED):
        value = jnp.sum(jnp.where(lane == chip * SCORED + k, logprob, 0.0), axis=1, keepdims=True)
        result = jnp.where(rank_ref[...] == k, value, result)
    out_ref[...] = result


def call(kernel, shape, dtype, specs, scratch=(), flops=0, size=0, name=None, out=VMEM, more=None, more_out=VMEM, vmem=16):
    shapes = jax.ShapeDtypeStruct(shape, dtype)
    return pl.pallas_call(
        kernel,
        out_shape=shapes if more is None else (shapes, more),
        in_specs=specs,
        out_specs=out if more is None else (out, more_out),
        scratch_shapes=list(scratch),
        compiler_params=pltpu.CompilerParams(vmem_limit_bytes=int(vmem * 2**20)),
        cost_estimate=pl.CostEstimate(flops=flops, bytes_accessed=size, transcendentals=0),
        name=name,
    )


def source_columns():
    c, yf, z, k = np.meshgrid(np.arange(2), np.arange(2), np.arange(8), np.arange(40), indexing="ij")
    return (((z * 2 + c) * 2 + yf) * 40 + k).reshape(1, 1280).astype(np.int32)


def body(
    queries,
    keys,
    values,
    out_weight,
    residual,
    norm_gain,
    head_weight,
    sampled_ids,
    loss_mask,
    doc_lengths,
):
    x, z, core = lax.axis_index("x"), lax.axis_index(("zh", "zl")), lax.axis_index("c")
    h, y = lax.axis_index("h"), lax.axis_index("y")
    chip = x * 8 + z
    slab = chip * 2 + core
    slabs = loss_mask.reshape(64, SLAB)
    upto = jnp.tril(jnp.ones((SLAB, SLAB), jnp.float32)).T
    rank = jnp.dot(slabs.astype(jnp.float32), upto, preferred_element_type=jnp.float32).astype(jnp.int32)
    rank = jnp.where(slabs == 1, rank - 1, -1)
    own_rank = lax.dynamic_slice_in_dim(rank, slab, 1, 0)
    block, packed = call(
        pack_kernel,
        (BLOCK, 128),
        jnp.bfloat16,
        [SMEM, VMEM, HBM, HBM, HBM],
        [
            pltpu.VMEM((BLOCK, 128), jnp.bfloat16),
            pltpu.VMEM((SLAB, 1024), jnp.bfloat16),
            pltpu.VMEM((32, 128), jnp.float32),
            pltpu.SemaphoreType.DMA((5,)),
        ],
        name="pack",
        out=ANY,
        more_out=ANY,
        vmem=63.9,
        more=jax.ShapeDtypeStruct((4, BLOCK, 128), jnp.bfloat16),
    )(slab[None], slabs, queries, keys, values)
    block = lax.ppermute(block, ("zh", "zl"), [(i, i ^ 4) for i in range(8)])
    near = lax.all_to_all(packed, "zl", 0, 0)
    bounds = jnp.cumsum(doc_lengths)
    position = jnp.arange(64 * SLAB, dtype=jnp.int32)
    begin = jnp.max(jnp.where(bounds[None, :] <= position[:, None], bounds[None, :], 0), axis=1)
    chosen = rank[:, None, :] == jnp.arange(SCORED, dtype=jnp.int32)[None, :, None]

    def pick(values_of):
        return jnp.sum(jnp.where(chosen, values_of.reshape(64, 1, SLAB), 0), axis=2)

    def columns(of_scored):
        pairs = of_scored.reshape(CHIPS, 2, SCORED)
        pairs = jnp.where(core == 0, pairs, pairs[:, ::-1])
        tiles = pairs.reshape(8, 4, 2, SCORED).transpose(0, 2, 1, 3)
        return jnp.repeat(tiles.reshape(8, 32), HEADS_DEV, axis=1)

    high = columns(pick(position))
    low = columns(pick(begin))
    ids = pick(sampled_ids).reshape(CHIPS, 2, SCORED).transpose(1, 0, 2).reshape(2, 128)
    first = jnp.min(low, axis=1) // 256
    half = lax.axis_index("zh")
    core_at = jnp.stack((core, half))

    mine = residual.reshape(2, HALF, CHIPS, 2, SCORED).transpose(3, 0, 1, 2, 4).reshape(4, HALF, 128)
    mine = lax.dynamic_index_in_dim(mine, y, 0, keepdims=False).astype(jnp.float32)
    mine = jnp.where(h == 0, mine, 0.0)

    own_begin = lax.dynamic_slice_in_dim(begin, slab * SLAB, SLAB, 0)
    own_position = slab * SLAB + jnp.arange(SLAB, dtype=jnp.int32)
    at = jnp.stack((core, own_begin[0] // 256, chip, half))
    base = ((slab * 2 + h) * 4 + y) * 256

    near, low, high, first, ids, own_begin = lax.optimization_barrier((near, low, high, first, ids, own_begin))
    near = call(
        spread_kernel, (4, 4, BLOCK, 128), jnp.bfloat16, [VMEM], [pltpu.SemaphoreType.DMA((4,))], name="spread", out=ANY
    )(near)
    near, block = lax.optimization_barrier((near, block))
    near = lax.all_to_all(near, "x", 0, 0)
    blocks = [block] + [lax.ppermute(block, "zl", [(i, i ^ k) for i in range(4)]) for k in (1, 2, 3)]
    far = call(
        spread_far_kernel,
        (4, 4, BLOCK, 128),
        jnp.bfloat16,
        [SMEM] + [VMEM] * 4,
        [pltpu.SemaphoreType.DMA((16,))],
        name="spread_far",
        out=ANY,
    )(lax.axis_index("zl")[None], *blocks)
    near, far = lax.optimization_barrier((near, far))
    far = lax.all_to_all(far, "x", 0, 0)
    source = jnp.asarray(source_columns())
    weight = call(
        weight_kernel, (256, D), jnp.bfloat16, [VMEM] * 3, flops=2 * 256 * D * 1280, name="weight", vmem=28
    )(source, norm_gain[None, :], head_weight)
    near_other = lax.ppermute(near, "c", [(0, 1), (1, 0)])

    far, weight, mine = lax.optimization_barrier((far, weight, mine))
    far_other = lax.ppermute(far, "c", [(0, 1), (1, 0)])
    blocks = (near, far, near_other, far_other)
    held = [pltpu.VMEM((2, CHIPS, BLOCK, 128), jnp.bfloat16), pltpu.SemaphoreType.DMA((16,))]
    scores = pltpu.VMEM((2 * GROUP * SLAB, 256), jnp.float32)
    parts = call(
        scored_kernel,
        (4, HALF, 128),
        jnp.float32,
        [SMEM, SMEM, VMEM, VMEM] + [ANY] * 4 + [VMEM],
        [pltpu.VMEM((256, 128), jnp.float32), pltpu.VMEM((256, 1024), jnp.bfloat16)] + held + [scores, scores],
        name="scored",
        vmem=28,
    )(core_at, first, low, high, *blocks, out_weight)

    token = jax.ShapeDtypeStruct((8, 128), jnp.float32)

    def context_of(start_head, after):
        return call(
            functools.partial(context_kernel, start_head),
            (SLAB, 512),
            jnp.bfloat16,
            [SMEM, VMEM, VMEM] + [ANY] * 4 + [VMEM, ANY],
            held + [pltpu.VMEM((2 * GROUP * SLAB, 512), jnp.float32)] * 2,
            flops=4 * 1024 * 4224 * 128,
            size=6 * 2**20,
            name="context",
            vmem=28,
            more=token,
        )(at, own_begin[None, :], own_position[None, :], *blocks, queries, after)

    parts = lax.all_to_all(parts, "y", 0, 0)
    block = pltpu.VMEM((HALF, 128), jnp.bfloat16)
    sums, after = call(
        add_kernel,
        (16, HALF, 128),
        jnp.bfloat16,
        [VMEM] * 2,
        [block, pltpu.SemaphoreType.DMA((16,))],
        name="add",
        out=HBM,
        more=token,
    )(parts, mine)
    context_a, done_a = context_of(0, after)
    sums = lax.all_to_all(sums, ("h", "zh", "zl"), 0, 0)
    hidden, after = call(hidden_kernel, (16, 8 * HALF, 128), jnp.bfloat16, [VMEM, ANY], name="hidden", more=token)(
        sums, done_a
    )
    context_b, done_b = context_of(4, after)
    hidden = lax.all_to_all(hidden, ("x", "y"), 0, 0).reshape(4, 2, 640, 128)
    hidden, done_b = lax.optimization_barrier((hidden, done_b))
    hidden_other = lax.ppermute(hidden, "c", [(0, 1), (1, 0)])
    at_logits = jnp.stack((core, base))
    shares, squares = call(
        own_logits_kernel,
        (2, 256, 128),
        jnp.float32,
        [SMEM] + [VMEM] * 2,
        name="own_logits",
        more=jax.ShapeDtypeStruct((2, 8, 128), jnp.float32),
    )(at_logits, hidden, weight)
    tiles = call(logits_kernel, (32, 8, 128), jnp.float32, [SMEM] + [VMEM] * 5 + [ANY], name="logits")(
        at_logits, ids, shares, squares, hidden_other, weight, done_b
    )
    context = jnp.concatenate((context_a, context_b), axis=1)
    tiles = lax.all_to_all(tiles, ("x", "y", "c"), 0, 0)
    tiles = call(merge_kernel, (16, 8, 128), jnp.float32, [VMEM], name="merge")(tiles)
    tiles = lax.all_to_all(tiles, ("h", "zh", "zl"), 0, 0)
    logprob = call(final_kernel, (1, 128), jnp.float32, [SMEM, VMEM, VMEM], name="final")(
        jnp.stack((core, chip)), own_rank, tiles
    )
    return context, logprob.reshape(128)


def solution(mesh):
    fine = Mesh(mesh.devices.reshape(4, 2, 4, 2, 2, 4), ("x", "zh", "zl", "c", "h", "y"))
    ctx, tp = ("x", "zh", "zl", "c"), ("h", "y")
    placed = (
        P(ctx, tp),
        P(ctx, tp),
        P(ctx, tp),
        P(ctx, tp),
        P(ctx, None),
        P(),
        P(ctx + tp, None),
        P(),
        P(),
        P(),
    )
    return jax.shard_map(
        body, mesh=fine, in_specs=placed, out_specs=(P(ctx, tp), P(ctx)), check_vma=False
    )
```

```python
import functools
import math

import jax
import jax.numpy as jnp
import numpy as np
from jax import lax
from jax.experimental import pallas as pl
from jax.experimental.pallas import tpu as pltpu
from jax.sharding import Mesh
from jax.sharding import PartitionSpec as P

HEAD_DIM = 128
SCORED = 4
HEADS_DEV = 8
SLAB = 128
GROUP = 2
CHIPS = 32
BLOCK = 2 * SLAB + SCORED * HEADS_DEV
FEATS = 80
HALF = 40
D = 5120

masked_fill = -1e30
start_max = -5e29
norm_eps = 1e-06
LOG2E = 1.4426950408889634
SCALE2 = LOG2E / math.sqrt(HEAD_DIM)
NT = (((1,), (1,)), ((), ()))
TN = (((0,), (0,)), ((), ()))
SMEM = pl.BlockSpec(memory_space=pltpu.SMEM)
VMEM = pl.BlockSpec(memory_space=pltpu.VMEM)
ANY = pl.BlockSpec(memory_space=pl.ANY)
HBM = pl.BlockSpec(memory_space=pltpu.HBM)


def iota(shape, axis):
    return lax.broadcasted_iota(jnp.int32, shape, axis)


def send_copies(source, out_ref, sems):
    copies = [pltpu.make_async_copy(source, out_ref.at[i], sems.at[i]) for i in range(out_ref.shape[0])]
    for copy in copies:
        copy.start()
    for copy in copies:
        copy.wait()


def pack_kernel(at_ref, mask_ref, q_ref, k_ref, v_ref, block_ref, out_ref, block, queries, rows, sems):
    copies = [
        pltpu.make_async_copy(k_ref, block.at[pl.ds(0, SLAB)], sems.at[0]),
        pltpu.make_async_copy(v_ref, block.at[pl.ds(SLAB, SLAB)], sems.at[1]),
        pltpu.make_async_copy(q_ref, queries, sems.at[2]),
    ]
    for copy in copies:
        copy.start()
    mask = mask_ref[pl.ds(at_ref[0], 1), :]
    upto = (iota((SLAB, SLAB), 0) <= iota((SLAB, SLAB), 1)).astype(jnp.bfloat16)
    ones = jnp.broadcast_to(mask.astype(jnp.float32), (8, SLAB)).astype(jnp.bfloat16)
    rank = jnp.dot(ones, upto, preferred_element_type=jnp.float32).astype(jnp.int32) - 1
    chosen = jnp.where((iota((8, SLAB), 0) == rank) & (mask == 1), 1.0, 0.0).astype(jnp.bfloat16)
    for copy in copies:
        copy.wait()
    picked = jnp.dot(chosen, queries[...], preferred_element_type=jnp.float32)
    for h in range(HEADS_DEV):
        rows[pl.ds(h, SCORED, stride=HEADS_DEV), :] = picked[:SCORED, h * 128 : (h + 1) * 128]
    block[2 * SLAB :, :] = rows[...].astype(jnp.bfloat16)
    single = pltpu.make_async_copy(block, block_ref, sems.at[4])
    single.start()
    send_copies(block, out_ref, sems)
    single.wait()


def spread_kernel(near_ref, out_ref, sems):
    send_copies(near_ref, out_ref, sems)


def spread_far_kernel(at_ref, *refs):
    out_ref, sems = refs[-2:]
    copies = []
    for i in range(4):
        for k in range(4):
            copies.append(
                pltpu.make_async_copy(refs[k], out_ref.at[i, jnp.bitwise_xor(at_ref[0], k)], sems.at[i * 4 + k])
            )
    for copy in copies:
        copy.start()
    for copy in copies:
        copy.wait()


def collect(half, near_far, held, sems):
    copies = []
    for i, (near_ref, far_ref) in enumerate(near_far):
        for x in range(4):
            for j, ref in enumerate((near_ref, far_ref)):
                at = x * 8 + (half * 4 if j == 0 else (1 - half) * 4)
                target = held.at[i, pl.ds(pl.multiple_of(at, 4), 4)]
                copies.append(pltpu.make_async_copy(ref.at[x], target, sems.at[i * 8 + x * 2 + j]))
    for copy in copies:
        copy.start()
    for copy in copies:
        copy.wait()


def weight_kernel(source_ref, gain_ref, w_ref, out_ref):
    width = 1280
    move = (iota((width, width), 0) == source_ref[...]).astype(jnp.bfloat16)
    for x in range(4):
        part = w_ref[:, x * width : (x + 1) * width].astype(jnp.float32)
        part = (part * gain_ref[:, x * width : (x + 1) * width]).astype(jnp.bfloat16)
        moved = jnp.dot(part, move, preferred_element_type=jnp.float32).astype(jnp.bfloat16)
        for c in range(2):
            out_ref[:, (c * 4 + x) * 640 : (c * 4 + x + 1) * 640] = moved[:, c * 640 : (c + 1) * 640]


def attend(own_ref, other_ref, core, q, low, high, first, last, bufs):
    columns = q.shape[0]
    half = GROUP * SLAB
    row = iota((2 * half, 1), 0)
    inside = jnp.where(row < half, row, row - half)
    key0 = (inside // SLAB) * (2 * SLAB) + inside % SLAB + jnp.where(row < half, core, 1 - core) * SLAB
    turned = q.T

    def rows(g, at):
        chips = pl.ds(pl.multiple_of(jnp.minimum(g * GROUP, CHIPS - GROUP), GROUP), GROUP)
        parts = [ref[chips, at : at + SLAB, :].reshape(half, HEAD_DIM) for ref in (own_ref, other_ref)]
        return jnp.concatenate(parts, axis=0)

    def scores(g):
        return jnp.dot(rows(g, 0), turned, preferred_element_type=jnp.float32)

    def soften(g, buf, carry):
        top, total, acc = carry
        offset = g * (2 * half)
        s = jnp.where((key0 >= low - offset) & (key0 <= high - offset), buf[...] * SCALE2, masked_fill)
        new_top = jnp.maximum(top, jnp.max(s, axis=0, keepdims=True))
        p = jnp.exp2(s - new_top)
        keep = jnp.exp2(top - new_top)
        total = total * keep + jnp.sum(p, axis=0, keepdims=True)
        pv = lax.dot_general(rows(g, SLAB), p.astype(jnp.bfloat16), TN, preferred_element_type=jnp.float32)
        return new_top, total, acc * keep + pv

    begin = first // GROUP
    steps = (last // GROUP + 2 - begin) // 2

    def step(i, carry):
        g = begin + 2 * i
        bufs[1][...] = scores(g + 1)
        carry = soften(g, bufs[0], carry)
        bufs[0][...] = scores(g + 2)
        return soften(g + 1, bufs[1], carry)

    bufs[0][...] = scores(begin)
    start = (
        jnp.full((1, columns), start_max, jnp.float32),
        jnp.zeros((1, columns), jnp.float32),
        jnp.zeros((HEAD_DIM, columns), jnp.float32),
    )
    _, total, acc = lax.fori_loop(0, steps, step, start)
    return acc / total


def scored_kernel(core_ref, first_ref, low_ref, high_ref, near, far, near_other, far_other, w_ref, *refs):
    out_ref, rows, scored, held, sems = refs[-7:-2]
    core = core_ref[0]
    collect(core_ref[1], ((near, far), (near_other, far_other)), held, sems)
    own_ref, other_ref = held.at[0], held.at[1]
    for t in range(8):
        q = jnp.concatenate(
            (
                own_ref[4 * t : 4 * t + 4, 2 * SLAB :, :].reshape(128, HEAD_DIM),
                other_ref[4 * t : 4 * t + 4, 2 * SLAB :, :].reshape(128, HEAD_DIM),
            ),
            axis=0,
        )
        mixed = attend(
            own_ref,
            other_ref,
            core,
            q,
            low_ref[t : t + 1, :],
            high_ref[t : t + 1, :],
            first_ref[t],
            4 * t + 3,
            refs[-2:],
        )
        rows[...] = mixed.T
        for h in range(HEADS_DEV):
            part = rows[pl.ds(h, 32, stride=HEADS_DEV), :].astype(jnp.bfloat16)
            lanes = slice(h * 128, (h + 1) * 128)
            scored[pl.ds(pl.multiple_of(core * 128 + t * 16, 16), 16), lanes] = part[:16]
            scored[pl.ds(pl.multiple_of((1 - core) * 128 + t * 16, 16), 16), lanes] = part[16:]
    partial = lax.dot_general(w_ref[...], scored[...], NT, preferred_element_type=jnp.float32)
    for half in range(2):
        for feats in range(2):
            out_ref[half * 2 + feats] = partial[
                feats * HALF : (feats + 1) * HALF, half * 128 : (half + 1) * 128
            ]


def context_kernel(start_head, at_ref, low_ref, high_ref, near, far, near_other, far_other, q_ref, *refs):
    out_ref, token_ref, held, sems = refs[-6:-2]
    token_ref[...] = jnp.zeros_like(token_ref)
    collect(at_ref[3], ((near, far), (near_other, far_other)), held, sems)
    own_ref, other_ref = held.at[0], held.at[1]
    heads = range(start_head, start_head + 4)
    q = jnp.concatenate([q_ref[:, h * 128 : (h + 1) * 128] for h in heads], axis=0)
    low, high = jnp.tile(low_ref[...], (1, 4)), jnp.tile(high_ref[...], (1, 4))
    mixed = attend(own_ref, other_ref, at_ref[0], q, low, high, at_ref[1], at_ref[2], refs[-2:])
    for i in range(4):
        out_ref[:, i * 128 : (i + 1) * 128] = mixed[:, i * 128 : (i + 1) * 128].T.astype(jnp.bfloat16)


def add_kernel(parts_ref, residual_ref, out_ref, token_ref, block, sems):
    token_ref[...] = jnp.zeros_like(token_ref)
    total = residual_ref[...]
    for i in range(parts_ref.shape[0]):
        total = total + parts_ref[i]
    block[...] = total.astype(jnp.bfloat16)
    send_copies(block, out_ref, sems)


def hidden_kernel(parts_ref, dep_ref, out_ref, token_ref):
    token_ref[...] = jnp.zeros_like(token_ref)
    total = parts_ref[:8].astype(jnp.float32) + parts_ref[8:].astype(jnp.float32)
    total = total.reshape(8 * HALF, 128).astype(jnp.bfloat16)
    for i in range(out_ref.shape[0]):
        out_ref[i] = total


def add_logits(core, hidden_ref, w_ref, half):
    total = jnp.zeros((256, 128), jnp.float32)
    square = jnp.zeros((8, 128), jnp.float32)
    for x in range(4):
        part = hidden_ref[x, half]
        lanes = pl.ds(pl.multiple_of((core * 4 + x) * 640, 128), 640)
        total = total + jnp.dot(w_ref[:, lanes], part, preferred_element_type=jnp.float32)
        wide = part.astype(jnp.float32)
        square = square + jnp.sum((wide * wide).reshape(80, 8, 128), axis=0)
    return total, square


def own_logits_kernel(at_ref, own_ref, w_ref, out_ref, square_ref):
    for half in range(2):
        out_ref[half], square_ref[half] = add_logits(at_ref[0], own_ref, w_ref, half)


def logits_kernel(at_ref, ids_ref, sum_ref, square_ref, other_ref, w_ref, dep_ref, out_ref):
    core, base = at_ref[0], at_ref[1]
    tops, targets = [], []
    for half in range(2):
        total, square = add_logits(1 - core, other_ref, w_ref, half)
        total, square = total + sum_ref[half], square + square_ref[half]
        mean = jnp.sum(square, axis=0, keepdims=True) * (1.0 / D)
        total = total * lax.rsqrt(mean + norm_eps)
        top = jnp.max(total, axis=0, keepdims=True)
        tops.append(top + jnp.log(jnp.sum(jnp.exp(total - top), axis=0, keepdims=True)))
        hit = iota((256, 128), 0) + base == ids_ref[half : half + 1, :]
        targets.append(jnp.sum(jnp.where(hit, total, 0.0), axis=0, keepdims=True))
    tile = jnp.concatenate(tops + targets + [jnp.zeros((4, 128), jnp.float32)], axis=0)
    for i in range(out_ref.shape[0]):
        out_ref[i] = tile


def merge(parts_ref):
    parts = parts_ref[...]
    top = jnp.max(parts, axis=0)
    lse = top + jnp.log(jnp.sum(jnp.exp(parts - top[None]), axis=0))
    return jnp.where(iota((8, 128), 0) < 2, lse, jnp.sum(parts, axis=0))


def merge_kernel(parts_ref, out_ref):
    tile = merge(parts_ref)
    for i in range(out_ref.shape[0]):
        out_ref[i] = tile


def final_kernel(at_ref, rank_ref, parts_ref, out_ref):
    core, chip = at_ref[0], at_ref[1]
    tile = merge(parts_ref)
    logprob = jnp.where(core == 0, tile[2:3] - tile[0:1], tile[3:4] - tile[1:2])
    lane = iota((1, 128), 1)
    result = jnp.zeros((1, 128), jnp.float32)
    for k in range(SCORED):
        value = jnp.sum(jnp.where(lane == chip * SCORED + k, logprob, 0.0), axis=1, keepdims=True)
        result = jnp.where(rank_ref[...] == k, value, result)
    out_ref[...] = result


def call(kernel, shape, dtype, specs, scratch=(), flops=0, size=0, name=None, out=VMEM, more=None, more_out=VMEM, vmem=16):
    shapes = jax.ShapeDtypeStruct(shape, dtype)
    return pl.pallas_call(
        kernel,
        out_shape=shapes if more is None else (shapes, more),
        in_specs=specs,
        out_specs=out if more is None else (out, more_out),
        scratch_shapes=list(scratch),
        compiler_params=pltpu.CompilerParams(vmem_limit_bytes=int(vmem * 2**20)),
        cost_estimate=pl.CostEstimate(flops=flops, bytes_accessed=size, transcendentals=0),
        name=name,
    )


def source_columns():
    c, yf, z, k = np.meshgrid(np.arange(2), np.arange(2), np.arange(8), np.arange(40), indexing="ij")
    return (((z * 2 + c) * 2 + yf) * 40 + k).reshape(1, 1280).astype(np.int32)


def body(
    queries,
    keys,
    values,
    out_weight,
    residual,
    norm_gain,
    head_weight,
    sampled_ids,
    loss_mask,
    doc_lengths,
):
    x, z, core = lax.axis_index("x"), lax.axis_index(("zh", "zl")), lax.axis_index("c")
    h, y = lax.axis_index("h"), lax.axis_index("y")
    chip = x * 8 + z
    slab = chip * 2 + core
    slabs = loss_mask.reshape(64, SLAB)
    block, packed = call(
        pack_kernel,
        (BLOCK, 128),
        jnp.bfloat16,
        [SMEM, VMEM, HBM, HBM, HBM],
        [
            pltpu.VMEM((BLOCK, 128), jnp.bfloat16),
            pltpu.VMEM((SLAB, 1024), jnp.bfloat16),
            pltpu.VMEM((32, 128), jnp.float32),
            pltpu.SemaphoreType.DMA((5,)),
        ],
        name="pack",
        out=ANY,
        more_out=ANY,
        vmem=63.9,
        more=jax.ShapeDtypeStruct((4, BLOCK, 128), jnp.bfloat16),
    )(slab[None], slabs, queries, keys, values)
    block = lax.ppermute(block, ("zh", "zl"), [(i, i ^ 4) for i in range(8)])
    near = lax.all_to_all(packed, "zl", 0, 0)
    near = call(
        spread_kernel, (4, 4, BLOCK, 128), jnp.bfloat16, [VMEM], [pltpu.SemaphoreType.DMA((4,))], name="spread", out=ANY
    )(near)
    near, block = lax.optimization_barrier((near, block))
    near = lax.all_to_all(near, "x", 0, 0)
    blocks = [block] + [lax.ppermute(block, "zl", [(i, i ^ k) for i in range(4)]) for k in (1, 2, 3)]
    far = call(
        spread_far_kernel,
        (4, 4, BLOCK, 128),
        jnp.bfloat16,
        [SMEM] + [VMEM] * 4,
        [pltpu.SemaphoreType.DMA((16,))],
        name="spread_far",
        out=ANY,
    )(lax.axis_index("zl")[None], *blocks)
    near, far = lax.optimization_barrier((near, far))
    far = lax.all_to_all(far, "x", 0, 0)
    near, loss_mask, sampled_ids, doc_lengths, norm_gain, residual = lax.optimization_barrier(
        (near, loss_mask, sampled_ids, doc_lengths, norm_gain, residual)
    )
    source = jnp.asarray(source_columns())
    weight = call(
        weight_kernel, (256, D), jnp.bfloat16, [VMEM] * 3, flops=2 * 256 * D * 1280, name="weight", vmem=28
    )(source, norm_gain[None, :], head_weight)
    slabs = loss_mask.reshape(64, SLAB)
    upto = jnp.tril(jnp.ones((SLAB, SLAB), jnp.float32)).T
    rank = jnp.dot(slabs.astype(jnp.float32), upto, preferred_element_type=jnp.float32).astype(jnp.int32)
    rank = jnp.where(slabs == 1, rank - 1, -1)
    own_rank = lax.dynamic_slice_in_dim(rank, slab, 1, 0)
    bounds = jnp.cumsum(doc_lengths)
    position = jnp.arange(64 * SLAB, dtype=jnp.int32)
    begin = jnp.max(jnp.where(bounds[None, :] <= position[:, None], bounds[None, :], 0), axis=1)
    chosen = rank[:, None, :] == jnp.arange(SCORED, dtype=jnp.int32)[None, :, None]

    def pick(values_of):
        return jnp.sum(jnp.where(chosen, values_of.reshape(64, 1, SLAB), 0), axis=2)

    def columns(of_scored):
        pairs = of_scored.reshape(CHIPS, 2, SCORED)
        pairs = jnp.where(core == 0, pairs, pairs[:, ::-1])
        tiles = pairs.reshape(8, 4, 2, SCORED).transpose(0, 2, 1, 3)
        return jnp.repeat(tiles.reshape(8, 32), HEADS_DEV, axis=1)

    high = columns(pick(position))
    low = columns(pick(begin))
    ids = pick(sampled_ids).reshape(CHIPS, 2, SCORED).transpose(1, 0, 2).reshape(2, 128)
    first = jnp.min(low, axis=1) // 256
    half = lax.axis_index("zh")
    core_at = jnp.stack((core, half))

    mine = residual.reshape(2, HALF, CHIPS, 2, SCORED).transpose(3, 0, 1, 2, 4).reshape(4, HALF, 128)
    mine = lax.dynamic_index_in_dim(mine, y, 0, keepdims=False).astype(jnp.float32)
    mine = jnp.where(h == 0, mine, 0.0)

    own_begin = lax.dynamic_slice_in_dim(begin, slab * SLAB, SLAB, 0)
    own_position = slab * SLAB + jnp.arange(SLAB, dtype=jnp.int32)
    at = jnp.stack((core, own_begin[0] // 256, chip, half))
    base = ((slab * 2 + h) * 4 + y) * 256

    near, low, high, first, ids, own_begin = lax.optimization_barrier((near, low, high, first, ids, own_begin))
    near_other = lax.ppermute(near, "c", [(0, 1), (1, 0)])

    far, weight, mine = lax.optimization_barrier((far, weight, mine))
    far_other = lax.ppermute(far, "c", [(0, 1), (1, 0)])
    blocks = (near, far, near_other, far_other)
    held = [pltpu.VMEM((2, CHIPS, BLOCK, 128), jnp.bfloat16), pltpu.SemaphoreType.DMA((16,))]
    scores = pltpu.VMEM((2 * GROUP * SLAB, 256), jnp.float32)
    parts = call(
        scored_kernel,
        (4, HALF, 128),
        jnp.float32,
        [SMEM, SMEM, VMEM, VMEM] + [ANY] * 4 + [VMEM],
        [pltpu.VMEM((256, 128), jnp.float32), pltpu.VMEM((256, 1024), jnp.bfloat16)] + held + [scores, scores],
        name="scored",
        vmem=28,
    )(core_at, first, low, high, *blocks, out_weight)

    token = jax.ShapeDtypeStruct((8, 128), jnp.float32)

    def context_of(start_head, after):
        return call(
            functools.partial(context_kernel, start_head),
            (SLAB, 512),
            jnp.bfloat16,
            [SMEM, VMEM, VMEM] + [ANY] * 4 + [VMEM, ANY],
            held + [pltpu.VMEM((2 * GROUP * SLAB, 512), jnp.float32)] * 2,
            flops=4 * 1024 * 4224 * 128,
            size=6 * 2**20,
            name="context",
            vmem=28,
            more=token,
        )(at, own_begin[None, :], own_position[None, :], *blocks, queries, after)

    parts = lax.all_to_all(parts, "y", 0, 0)
    block = pltpu.VMEM((HALF, 128), jnp.bfloat16)
    sums, after = call(
        add_kernel,
        (16, HALF, 128),
        jnp.bfloat16,
        [VMEM] * 2,
        [block, pltpu.SemaphoreType.DMA((16,))],
        name="add",
        out=HBM,
        more=token,
    )(parts, mine)
    context_a, done_a = context_of(0, after)
    sums = lax.all_to_all(sums, ("h", "zh", "zl"), 0, 0)
    hidden, after = call(hidden_kernel, (16, 8 * HALF, 128), jnp.bfloat16, [VMEM, ANY], name="hidden", more=token)(
        sums, done_a
    )
    context_b, done_b = context_of(4, after)
    hidden = lax.all_to_all(hidden, ("x", "y"), 0, 0).reshape(4, 2, 640, 128)
    hidden, done_b = lax.optimization_barrier((hidden, done_b))
    hidden_other = lax.ppermute(hidden, "c", [(0, 1), (1, 0)])
    at_logits = jnp.stack((core, base))
    shares, squares = call(
        own_logits_kernel,
        (2, 256, 128),
        jnp.float32,
        [SMEM] + [VMEM] * 2,
        name="own_logits",
        more=jax.ShapeDtypeStruct((2, 8, 128), jnp.float32),
    )(at_logits, hidden, weight)
    tiles = call(logits_kernel, (32, 8, 128), jnp.float32, [SMEM] + [VMEM] * 5 + [ANY], name="logits")(
        at_logits, ids, shares, squares, hidden_other, weight, done_b
    )
    context = jnp.concatenate((context_a, context_b), axis=1)
    tiles = lax.all_to_all(tiles, ("x", "y", "c"), 0, 0)
    tiles = call(merge_kernel, (16, 8, 128), jnp.float32, [VMEM], name="merge")(tiles)
    tiles = lax.all_to_all(tiles, ("h", "zh", "zl"), 0, 0)
    logprob = call(final_kernel, (1, 128), jnp.float32, [SMEM, VMEM, VMEM], name="final")(
        jnp.stack((core, chip)), own_rank, tiles
    )
    return context, logprob.reshape(128)


def solution(mesh):
    fine = Mesh(mesh.devices.reshape(4, 2, 4, 2, 2, 4), ("x", "zh", "zl", "c", "h", "y"))
    ctx, tp = ("x", "zh", "zl", "c"), ("h", "y")
    placed = (
        P(ctx, tp),
        P(ctx, tp),
        P(ctx, tp),
        P(ctx, tp),
        P(ctx, None),
        P(),
        P(ctx + tp, None),
        P(),
        P(),
        P(),
    )
    return jax.shard_map(
        body, mesh=fine, in_specs=placed, out_specs=(P(ctx, tp), P(ctx)), check_vma=False
    )
```

```python
import functools
import math

import jax
import jax.numpy as jnp
import numpy as np
from jax import lax
from jax.experimental import pallas as pl
from jax.experimental.pallas import tpu as pltpu
from jax.sharding import Mesh
from jax.sharding import PartitionSpec as P

HEAD_DIM = 128
SCORED = 4
HEADS_DEV = 8
SLAB = 128
GROUP = 2
CHIPS = 32
BLOCK = 2 * SLAB + SCORED * HEADS_DEV
FEATS = 80
HALF = 40
D = 5120

masked_fill = -1e30
start_max = -5e29
norm_eps = 1e-06
LOG2E = 1.4426950408889634
SCALE2 = LOG2E / math.sqrt(HEAD_DIM)
NT = (((1,), (1,)), ((), ()))
TN = (((0,), (0,)), ((), ()))
SMEM = pl.BlockSpec(memory_space=pltpu.SMEM)
VMEM = pl.BlockSpec(memory_space=pltpu.VMEM)
ANY = pl.BlockSpec(memory_space=pl.ANY)
HBM = pl.BlockSpec(memory_space=pltpu.HBM)


def iota(shape, axis):
    return lax.broadcasted_iota(jnp.int32, shape, axis)


def send_copies(source, out_ref, sems):
    copies = [pltpu.make_async_copy(source, out_ref.at[i], sems.at[i]) for i in range(out_ref.shape[0])]
    for copy in copies:
        copy.start()
    for copy in copies:
        copy.wait()


def pack_kernel(at_ref, mask_ref, q_ref, k_ref, v_ref, block_ref, out_ref, block, queries, rows, sems):
    copies = [
        pltpu.make_async_copy(k_ref, block.at[pl.ds(0, SLAB)], sems.at[0]),
        pltpu.make_async_copy(v_ref, block.at[pl.ds(SLAB, SLAB)], sems.at[1]),
        pltpu.make_async_copy(q_ref, queries, sems.at[2]),
    ]
    for copy in copies:
        copy.start()
    mask = mask_ref[pl.ds(at_ref[0], 1), :]
    upto = (iota((SLAB, SLAB), 0) <= iota((SLAB, SLAB), 1)).astype(jnp.bfloat16)
    ones = jnp.broadcast_to(mask.astype(jnp.float32), (8, SLAB)).astype(jnp.bfloat16)
    rank = jnp.dot(ones, upto, preferred_element_type=jnp.float32).astype(jnp.int32) - 1
    chosen = jnp.where((iota((8, SLAB), 0) == rank) & (mask == 1), 1.0, 0.0).astype(jnp.bfloat16)
    for copy in copies:
        copy.wait()
    picked = jnp.dot(chosen, queries[...], preferred_element_type=jnp.float32)
    for h in range(HEADS_DEV):
        rows[pl.ds(h, SCORED, stride=HEADS_DEV), :] = picked[:SCORED, h * 128 : (h + 1) * 128]
    block[2 * SLAB :, :] = rows[...].astype(jnp.bfloat16)
    single = pltpu.make_async_copy(block, block_ref, sems.at[4])
    single.start()
    send_copies(block, out_ref, sems)
    single.wait()


def spread_kernel(near_ref, out_ref, sems):
    send_copies(near_ref, out_ref, sems)


def spread_far_kernel(at_ref, *refs):
    out_ref, sems = refs[-2:]
    copies = []
    for i in range(4):
        for k in range(4):
            copies.append(
                pltpu.make_async_copy(refs[k], out_ref.at[i, jnp.bitwise_xor(at_ref[0], k)], sems.at[i * 4 + k])
            )
    for copy in copies:
        copy.start()
    for copy in copies:
        copy.wait()


def collect(half, near_far, held, sems):
    copies = []
    for i, (near_ref, far_ref) in enumerate(near_far):
        for x in range(4):
            for j, ref in enumerate((near_ref, far_ref)):
                at = x * 8 + (half * 4 if j == 0 else (1 - half) * 4)
                target = held.at[i, pl.ds(pl.multiple_of(at, 4), 4)]
                copies.append(pltpu.make_async_copy(ref.at[x], target, sems.at[i * 8 + x * 2 + j]))
    for copy in copies:
        copy.start()
    for copy in copies:
        copy.wait()


def weight_kernel(source_ref, gain_ref, w_ref, early_ref, out_ref):
    width = 1280
    move = (iota((width, width), 0) == source_ref[...]).astype(jnp.bfloat16)
    for x in range(4):
        part = w_ref[:, x * width : (x + 1) * width].astype(jnp.float32)
        part = (part * gain_ref[:, x * width : (x + 1) * width]).astype(jnp.bfloat16)
        moved = jnp.dot(part, move, preferred_element_type=jnp.float32).astype(jnp.bfloat16)
        for c in range(2):
            out_ref[:, (c * 4 + x) * 640 : (c * 4 + x + 1) * 640] = moved[:, c * 640 : (c + 1) * 640]


def attend(own_ref, other_ref, core, q, low, high, first, last, bufs):
    columns = q.shape[0]
    half = GROUP * SLAB
    row = iota((2 * half, 1), 0)
    inside = jnp.where(row < half, row, row - half)
    key0 = (inside // SLAB) * (2 * SLAB) + inside % SLAB + jnp.where(row < half, core, 1 - core) * SLAB
    turned = q.T

    def rows(g, at):
        chips = pl.ds(pl.multiple_of(jnp.minimum(g * GROUP, CHIPS - GROUP), GROUP), GROUP)
        parts = [ref[chips, at : at + SLAB, :].reshape(half, HEAD_DIM) for ref in (own_ref, other_ref)]
        return jnp.concatenate(parts, axis=0)

    def scores(g):
        return jnp.dot(rows(g, 0), turned, preferred_element_type=jnp.float32)

    def soften(g, buf, carry):
        top, total, acc = carry
        offset = g * (2 * half)
        s = jnp.where((key0 >= low - offset) & (key0 <= high - offset), buf[...] * SCALE2, masked_fill)
        new_top = jnp.maximum(top, jnp.max(s, axis=0, keepdims=True))
        p = jnp.exp2(s - new_top)
        keep = jnp.exp2(top - new_top)
        total = total * keep + jnp.sum(p, axis=0, keepdims=True)
        pv = lax.dot_general(rows(g, SLAB), p.astype(jnp.bfloat16), TN, preferred_element_type=jnp.float32)
        return new_top, total, acc * keep + pv

    begin = first // GROUP
    steps = (last // GROUP + 2 - begin) // 2

    def step(i, carry):
        g = begin + 2 * i
        bufs[1][...] = scores(g + 1)
        carry = soften(g, bufs[0], carry)
        bufs[0][...] = scores(g + 2)
        return soften(g + 1, bufs[1], carry)

    bufs[0][...] = scores(begin)
    start = (
        jnp.full((1, columns), start_max, jnp.float32),
        jnp.zeros((1, columns), jnp.float32),
        jnp.zeros((HEAD_DIM, columns), jnp.float32),
    )
    _, total, acc = lax.fori_loop(0, steps, step, start)
    return acc / total


def scored_kernel(core_ref, first_ref, low_ref, high_ref, near, far, near_other, far_other, w_ref, *refs):
    out_ref, rows, scored, held, sems = refs[-7:-2]
    core = core_ref[0]
    collect(core_ref[1], ((near, far), (near_other, far_other)), held, sems)
    own_ref, other_ref = held.at[0], held.at[1]
    for t in range(8):
        q = jnp.concatenate(
            (
                own_ref[4 * t : 4 * t + 4, 2 * SLAB :, :].reshape(128, HEAD_DIM),
                other_ref[4 * t : 4 * t + 4, 2 * SLAB :, :].reshape(128, HEAD_DIM),
            ),
            axis=0,
        )
        mixed = attend(
            own_ref,
            other_ref,
            core,
            q,
            low_ref[t : t + 1, :],
            high_ref[t : t + 1, :],
            first_ref[t],
            4 * t + 3,
            refs[-2:],
        )
        rows[...] = mixed.T
        for h in range(HEADS_DEV):
            part = rows[pl.ds(h, 32, stride=HEADS_DEV), :].astype(jnp.bfloat16)
            lanes = slice(h * 128, (h + 1) * 128)
            scored[pl.ds(pl.multiple_of(core * 128 + t * 16, 16), 16), lanes] = part[:16]
            scored[pl.ds(pl.multiple_of((1 - core) * 128 + t * 16, 16), 16), lanes] = part[16:]
    partial = lax.dot_general(w_ref[...], scored[...], NT, preferred_element_type=jnp.float32)
    for half in range(2):
        for feats in range(2):
            out_ref[half * 2 + feats] = partial[
                feats * HALF : (feats + 1) * HALF, half * 128 : (half + 1) * 128
            ]


def context_kernel(start_head, at_ref, low_ref, high_ref, near, far, near_other, far_other, q_ref, *refs):
    out_ref, token_ref, held, sems = refs[-6:-2]
    token_ref[...] = jnp.zeros_like(token_ref)
    collect(at_ref[3], ((near, far), (near_other, far_other)), held, sems)
    own_ref, other_ref = held.at[0], held.at[1]
    heads = range(start_head, start_head + 4)
    q = jnp.concatenate([q_ref[:, h * 128 : (h + 1) * 128] for h in heads], axis=0)
    low, high = jnp.tile(low_ref[...], (1, 4)), jnp.tile(high_ref[...], (1, 4))
    mixed = attend(own_ref, other_ref, at_ref[0], q, low, high, at_ref[1], at_ref[2], refs[-2:])
    for i in range(4):
        out_ref[:, i * 128 : (i + 1) * 128] = mixed[:, i * 128 : (i + 1) * 128].T.astype(jnp.bfloat16)


def add_kernel(parts_ref, residual_ref, out_ref, token_ref, block, sems):
    token_ref[...] = jnp.zeros_like(token_ref)
    total = residual_ref[...]
    for i in range(parts_ref.shape[0]):
        total = total + parts_ref[i]
    block[...] = total.astype(jnp.bfloat16)
    send_copies(block, out_ref, sems)


def hidden_kernel(parts_ref, dep_ref, out_ref, token_ref):
    token_ref[...] = jnp.zeros_like(token_ref)
    total = parts_ref[:8].astype(jnp.float32) + parts_ref[8:].astype(jnp.float32)
    total = total.reshape(8 * HALF, 128).astype(jnp.bfloat16)
    for i in range(out_ref.shape[0]):
        out_ref[i] = total


def add_logits(core, hidden_ref, w_ref, half):
    total = jnp.zeros((256, 128), jnp.float32)
    square = jnp.zeros((8, 128), jnp.float32)
    for x in range(4):
        part = hidden_ref[x, half]
        lanes = pl.ds(pl.multiple_of((core * 4 + x) * 640, 128), 640)
        total = total + jnp.dot(w_ref[:, lanes], part, preferred_element_type=jnp.float32)
        wide = part.astype(jnp.float32)
        square = square + jnp.sum((wide * wide).reshape(80, 8, 128), axis=0)
    return total, square


def own_logits_kernel(at_ref, own_ref, w_ref, out_ref, square_ref):
    for half in range(2):
        out_ref[half], square_ref[half] = add_logits(at_ref[0], own_ref, w_ref, half)


def logits_kernel(at_ref, ids_ref, sum_ref, square_ref, other_ref, w_ref, dep_ref, out_ref):
    core, base = at_ref[0], at_ref[1]
    tops, targets = [], []
    for half in range(2):
        total, square = add_logits(1 - core, other_ref, w_ref, half)
        total, square = total + sum_ref[half], square + square_ref[half]
        mean = jnp.sum(square, axis=0, keepdims=True) * (1.0 / D)
        total = total * lax.rsqrt(mean + norm_eps)
        top = jnp.max(total, axis=0, keepdims=True)
        tops.append(top + jnp.log(jnp.sum(jnp.exp(total - top), axis=0, keepdims=True)))
        hit = iota((256, 128), 0) + base == ids_ref[half : half + 1, :]
        targets.append(jnp.sum(jnp.where(hit, total, 0.0), axis=0, keepdims=True))
    tile = jnp.concatenate(tops + targets + [jnp.zeros((4, 128), jnp.float32)], axis=0)
    for i in range(out_ref.shape[0]):
        out_ref[i] = tile


def merge(parts_ref):
    parts = parts_ref[...]
    top = jnp.max(parts, axis=0)
    lse = top + jnp.log(jnp.sum(jnp.exp(parts - top[None]), axis=0))
    return jnp.where(iota((8, 128), 0) < 2, lse, jnp.sum(parts, axis=0))


def merge_kernel(parts_ref, out_ref):
    tile = merge(parts_ref)
    for i in range(out_ref.shape[0]):
        out_ref[i] = tile


def final_kernel(at_ref, rank_ref, parts_ref, out_ref):
    core, chip = at_ref[0], at_ref[1]
    tile = merge(parts_ref)
    logprob = jnp.where(core == 0, tile[2:3] - tile[0:1], tile[3:4] - tile[1:2])
    lane = iota((1, 128), 1)
    result = jnp.zeros((1, 128), jnp.float32)
    for k in range(SCORED):
        value = jnp.sum(jnp.where(lane == chip * SCORED + k, logprob, 0.0), axis=1, keepdims=True)
        result = jnp.where(rank_ref[...] == k, value, result)
    out_ref[...] = result


def call(kernel, shape, dtype, specs, scratch=(), flops=0, size=0, name=None, out=VMEM, more=None, more_out=VMEM, vmem=16):
    shapes = jax.ShapeDtypeStruct(shape, dtype)
    return pl.pallas_call(
        kernel,
        out_shape=shapes if more is None else (shapes, more),
        in_specs=specs,
        out_specs=out if more is None else (out, more_out),
        scratch_shapes=list(scratch),
        compiler_params=pltpu.CompilerParams(vmem_limit_bytes=int(vmem * 2**20)),
        cost_estimate=pl.CostEstimate(flops=flops, bytes_accessed=size, transcendentals=0),
        name=name,
    )


def source_columns():
    c, yf, z, k = np.meshgrid(np.arange(2), np.arange(2), np.arange(8), np.arange(40), indexing="ij")
    return (((z * 2 + c) * 2 + yf) * 40 + k).reshape(1, 1280).astype(np.int32)


def body(
    queries,
    keys,
    values,
    out_weight,
    residual,
    norm_gain,
    head_weight,
    sampled_ids,
    loss_mask,
    doc_lengths,
):
    x, z, core = lax.axis_index("x"), lax.axis_index(("zh", "zl")), lax.axis_index("c")
    h, y = lax.axis_index("h"), lax.axis_index("y")
    chip = x * 8 + z
    slab = chip * 2 + core
    slabs = loss_mask.reshape(64, SLAB)
    block, packed = call(
        pack_kernel,
        (BLOCK, 128),
        jnp.bfloat16,
        [SMEM, VMEM, HBM, HBM, HBM],
        [
            pltpu.VMEM((BLOCK, 128), jnp.bfloat16),
            pltpu.VMEM((SLAB, 1024), jnp.bfloat16),
            pltpu.VMEM((32, 128), jnp.float32),
            pltpu.SemaphoreType.DMA((5,)),
        ],
        name="pack",
        out=ANY,
        more_out=ANY,
        vmem=63.9,
        more=jax.ShapeDtypeStruct((4, BLOCK, 128), jnp.bfloat16),
    )(slab[None], slabs, queries, keys, values)
    block = lax.ppermute(block, ("zh", "zl"), [(i, i ^ 4) for i in range(8)])
    near = lax.all_to_all(packed, "zl", 0, 0)
    near = call(
        spread_kernel, (4, 4, BLOCK, 128), jnp.bfloat16, [VMEM], [pltpu.SemaphoreType.DMA((4,))], name="spread", out=ANY
    )(near)
    near, block = lax.optimization_barrier((near, block))
    near = lax.all_to_all(near, "x", 0, 0)
    blocks = [block] + [lax.ppermute(block, "zl", [(i, i ^ k) for i in range(4)]) for k in (1, 2, 3)]
    far = call(
        spread_far_kernel,
        (4, 4, BLOCK, 128),
        jnp.bfloat16,
        [SMEM] + [VMEM] * 4,
        [pltpu.SemaphoreType.DMA((16,))],
        name="spread_far",
        out=ANY,
    )(lax.axis_index("zl")[None], *blocks)
    near, far = lax.optimization_barrier((near, far))
    far = lax.all_to_all(far, "x", 0, 0)
    near, loss_mask, sampled_ids, doc_lengths, norm_gain, residual = lax.optimization_barrier(
        (near, loss_mask, sampled_ids, doc_lengths, norm_gain, residual)
    )
    source = jnp.asarray(source_columns())
    weight = call(
        weight_kernel, (256, D), jnp.bfloat16, [VMEM] * 4, flops=2 * 256 * D * 1280, name="weight", vmem=28
    )(source, norm_gain[None, :], head_weight, out_weight)
    slabs = loss_mask.reshape(64, SLAB)
    upto = jnp.tril(jnp.ones((SLAB, SLAB), jnp.float32)).T
    rank = jnp.dot(slabs.astype(jnp.float32), upto, preferred_element_type=jnp.float32).astype(jnp.int32)
    rank = jnp.where(slabs == 1, rank - 1, -1)
    own_rank = lax.dynamic_slice_in_dim(rank, slab, 1, 0)
    bounds = jnp.cumsum(doc_lengths)
    position = jnp.arange(64 * SLAB, dtype=jnp.int32)
    begin = jnp.max(jnp.where(bounds[None, :] <= position[:, None], bounds[None, :], 0), axis=1)
    chosen = rank[:, None, :] == jnp.arange(SCORED, dtype=jnp.int32)[None, :, None]

    def pick(values_of):
        return jnp.sum(jnp.where(chosen, values_of.reshape(64, 1, SLAB), 0), axis=2)

    def columns(of_scored):
        pairs = of_scored.reshape(CHIPS, 2, SCORED)
        pairs = jnp.where(core == 0, pairs, pairs[:, ::-1])
        tiles = pairs.reshape(8, 4, 2, SCORED).transpose(0, 2, 1, 3)
        return jnp.repeat(tiles.reshape(8, 32), HEADS_DEV, axis=1)

    high = columns(pick(position))
    low = columns(pick(begin))
    ids = pick(sampled_ids).reshape(CHIPS, 2, SCORED).transpose(1, 0, 2).reshape(2, 128)
    first = jnp.min(low, axis=1) // 256
    half = lax.axis_index("zh")
    core_at = jnp.stack((core, half))

    mine = residual.reshape(2, HALF, CHIPS, 2, SCORED).transpose(3, 0, 1, 2, 4).reshape(4, HALF, 128)
    mine = lax.dynamic_index_in_dim(mine, y, 0, keepdims=False).astype(jnp.float32)
    mine = jnp.where(h == 0, mine, 0.0)

    own_begin = lax.dynamic_slice_in_dim(begin, slab * SLAB, SLAB, 0)
    own_position = slab * SLAB + jnp.arange(SLAB, dtype=jnp.int32)
    at = jnp.stack((core, own_begin[0] // 256, chip, half))
    base = ((slab * 2 + h) * 4 + y) * 256

    near, low, high, first, ids, own_begin = lax.optimization_barrier((near, low, high, first, ids, own_begin))
    near_other = lax.ppermute(near, "c", [(0, 1), (1, 0)])

    far, weight, mine = lax.optimization_barrier((far, weight, mine))
    far_other = lax.ppermute(far, "c", [(0, 1), (1, 0)])
    blocks = (near, far, near_other, far_other)
    held = [pltpu.VMEM((2, CHIPS, BLOCK, 128), jnp.bfloat16), pltpu.SemaphoreType.DMA((16,))]
    scores = pltpu.VMEM((2 * GROUP * SLAB, 256), jnp.float32)
    parts = call(
        scored_kernel,
        (4, HALF, 128),
        jnp.float32,
        [SMEM, SMEM, VMEM, VMEM] + [ANY] * 4 + [VMEM],
        [pltpu.VMEM((256, 128), jnp.float32), pltpu.VMEM((256, 1024), jnp.bfloat16)] + held + [scores, scores],
        name="scored",
        vmem=28,
    )(core_at, first, low, high, *blocks, out_weight)

    token = jax.ShapeDtypeStruct((8, 128), jnp.float32)

    def context_of(start_head, after):
        return call(
            functools.partial(context_kernel, start_head),
            (SLAB, 512),
            jnp.bfloat16,
            [SMEM, VMEM, VMEM] + [ANY] * 4 + [VMEM, ANY],
            held + [pltpu.VMEM((2 * GROUP * SLAB, 512), jnp.float32)] * 2,
            flops=4 * 1024 * 4224 * 128,
            size=6 * 2**20,
            name="context",
            vmem=28,
            more=token,
        )(at, own_begin[None, :], own_position[None, :], *blocks, queries, after)

    parts = lax.all_to_all(parts, "y", 0, 0)
    block = pltpu.VMEM((HALF, 128), jnp.bfloat16)
    sums, after = call(
        add_kernel,
        (16, HALF, 128),
        jnp.bfloat16,
        [VMEM] * 2,
        [block, pltpu.SemaphoreType.DMA((16,))],
        name="add",
        out=HBM,
        more=token,
    )(parts, mine)
    context_a, done_a = context_of(0, after)
    sums = lax.all_to_all(sums, ("h", "zh", "zl"), 0, 0)
    hidden, after = call(hidden_kernel, (16, 8 * HALF, 128), jnp.bfloat16, [VMEM, ANY], name="hidden", more=token)(
        sums, done_a
    )
    context_b, done_b = context_of(4, after)
    hidden = lax.all_to_all(hidden, ("x", "y"), 0, 0).reshape(4, 2, 640, 128)
    hidden, done_b = lax.optimization_barrier((hidden, done_b))
    hidden_other = lax.ppermute(hidden, "c", [(0, 1), (1, 0)])
    at_logits = jnp.stack((core, base))
    shares, squares = call(
        own_logits_kernel,
        (2, 256, 128),
        jnp.float32,
        [SMEM] + [VMEM] * 2,
        name="own_logits",
        more=jax.ShapeDtypeStruct((2, 8, 128), jnp.float32),
    )(at_logits, hidden, weight)
    tiles = call(logits_kernel, (32, 8, 128), jnp.float32, [SMEM] + [VMEM] * 5 + [ANY], name="logits")(
        at_logits, ids, shares, squares, hidden_other, weight, done_b
    )
    context = jnp.concatenate((context_a, context_b), axis=1)
    tiles = lax.all_to_all(tiles, ("x", "y", "c"), 0, 0)
    tiles = call(merge_kernel, (16, 8, 128), jnp.float32, [VMEM], name="merge")(tiles)
    tiles = lax.all_to_all(tiles, ("h", "zh", "zl"), 0, 0)
    logprob = call(final_kernel, (1, 128), jnp.float32, [SMEM, VMEM, VMEM], name="final")(
        jnp.stack((core, chip)), own_rank, tiles
    )
    return context, logprob.reshape(128)


def solution(mesh):
    fine = Mesh(mesh.devices.reshape(4, 2, 4, 2, 2, 4), ("x", "zh", "zl", "c", "h", "y"))
    ctx, tp = ("x", "zh", "zl", "c"), ("h", "y")
    placed = (
        P(ctx, tp),
        P(ctx, tp),
        P(ctx, tp),
        P(ctx, tp),
        P(ctx, None),
        P(),
        P(ctx + tp, None),
        P(),
        P(),
        P(),
    )
    return jax.shard_map(
        body, mesh=fine, in_specs=placed, out_specs=(P(ctx, tp), P(ctx)), check_vma=False
    )
```
